32 devices in a mesh: chan: 4 (over x, core), vox: 8 (over z, y).
Axes of the slice: x: 2, y: 2, z: 4, core: 2. Of those that a mesh axis runs over, the one named last changes fastest.
Arguments:
- features: bfloat16 [256, 5632], P('chan'), may hold values from -6 to 6
- hrf_filters: float32 [3, 5632, 16], P(None, 'chan'), may hold values from -1.5 to 1.5
- weights: bfloat16 [3, 5632, 40960], P(None, 'chan', 'vox'), may hold values from -0.046875 to 0.046875
- voxel_parcel: int32 [40960], P('vox'), may hold values from 0 to 799, as said below
- parcel_owner: int32 [800], replicated, may hold values from 0 to 7, as said below
Outputs:
- owned: bfloat16 [64, 1280, 256], P('vox', None, 'chan')
The draws below stay inside these ranges and needn't reach their ends.
Inputs may be any that keep to these rules, and one draw needn't show every extreme that they name: `voxel_parcel`: among the 5120 voxels of one index of vox, at most 1280 belong to parcels of one owner, and some owner gets exactly 1280; one owner gets exactly 1280 from every index of vox. `parcel_owner`: every owner holds exactly 100 parcels.
All inputs are finite; a program needn't handle non-finite values.
Results may differ from the reference program's by a relative error of at most 0.01.
Values may be sent and summed in bfloat16 or wider, within the bound.
No kernel may reach another device: no remote copies, remote signals or barrier semaphores. Data moves between devices by JAX's collectives and lax.ppermute only.
A program may use at most 128 MiB of HBM per device.

```python
import jax
import jax.numpy as jnp
from jax import lax

CH = 5632
BASES = 3
FILTER_TAPS = 16
TAP_SPACING = 2
TIME = 256
VOX_DEV = 5120
VOXELS = 40960
SEND = 1280
PAR_OWNER = 100
PARCELS = 800
N_CHAN = 4
N_VOX = 8


def one_permutation(derived_key, count):
    return jax.random.permutation(derived_key, count)


def parcel_tables(key):
    base = jax.random.fold_in(key, 11)
    key_perm, key_rank, key_star, key_shuffle, key_first, key_second = jax.random.split(base, 6)
    shuffled_ids = jax.random.permutation(key_perm, PARCELS).astype(jnp.int32)
    parcel_owner = (shuffled_ids % N_VOX).astype(jnp.int32)
    inverse = jnp.argsort(shuffled_ids).astype(jnp.int32)
    ranked = jax.vmap(lambda derived_key: one_permutation(derived_key, N_VOX))(jax.random.split(key_rank, N_VOX)).astype(jnp.int32)
    central_holder = jax.random.randint(key_star, (), 0, N_VOX).astype(jnp.int32)
    ranked = (ranked + central_holder - ranked[:, :1]) % N_VOX
    position = jnp.arange(VOX_DEV, dtype=jnp.int32)
    quarter = N_VOX // 4
    edge_one = quarter * SEND
    edge_two = edge_one + quarter * (SEND // 2)
    rank_of = jnp.where(position < edge_one, position // SEND, jnp.where(position < edge_two, quarter + (position - edge_one) // (SEND // 2), 2 * quarter + (position - edge_two) // (SEND // 4)))
    owner_seq = ranked[:, rank_of]
    shuffle = jax.vmap(lambda derived_key: one_permutation(derived_key, VOX_DEV))(jax.random.split(key_shuffle, N_VOX)).astype(jnp.int32)
    voxel_owner = jnp.take_along_axis(owner_seq, shuffle, axis=1)
    first_draw = jax.random.randint(key_first, (N_VOX, VOX_DEV), 0, PAR_OWNER).astype(jnp.int32)
    second_draw = jax.random.randint(key_second, (N_VOX, VOX_DEV), 0, PAR_OWNER).astype(jnp.int32)
    member = first_draw * second_draw // PAR_OWNER
    voxel_parcel = inverse[member * N_VOX + voxel_owner].reshape(-1)
    return (voxel_parcel.astype(jnp.int32), parcel_owner)


def draw_voxel_parcel(key, part):
    return parcel_tables(key)[0]


def draw_parcel_owner(key, part):
    return parcel_tables(key)[1]


def shard_levels(rng, extent, shards, low, largest):
    loudness = 1.0
    for dim, blocks in shards:
        draws = jax.random.uniform(jax.random.fold_in(jax.random.fold_in(rng, 6), dim), (blocks,), jnp.float32, low / len(shards), largest / len(shards))
        loudness = loudness * jnp.repeat(jnp.exp(draws), extent[dim] // blocks).reshape((-1,) + (1,) * (len(extent) - 1 - dim))
    return loudness


def noise(key, dims, width, bound, cuts=(), kind=jnp.bfloat16):
    factor_of = shard_levels(key, dims, cuts, -0.22, 0.18) if cuts else 1.0
    array = jax.random.normal(key, dims, jnp.float32) * width * factor_of
    return jnp.minimum(jnp.maximum(array, -bound), bound).astype(kind)


def setup_inputs(seed: int = 0) -> dict:
    key_list = jax.random.split(jax.random.key(seed), 6)
    features = noise(key_list[0], (TIME, CH), 1.0, 6.0, ((0, 4),))
    hrf_filters = noise(key_list[1], (BASES, CH, FILTER_TAPS), FILTER_TAPS ** -0.5, 1.5, ((1, 4),), jnp.float32)
    weights = noise(key_list[2], (BASES, CH, VOXELS), (BASES * CH) ** -0.5, 0.046875, ((1, 4), (2, 8)))
    voxel_parcel = draw_voxel_parcel(jax.random.fold_in(key_list[5], 71), 0)
    parcel_owner = draw_parcel_owner(jax.random.fold_in(key_list[5], 71), 0)
    return dict(features=features, hrf_filters=hrf_filters, weights=weights, voxel_parcel=voxel_parcel, parcel_owner=parcel_owner)


def reference(features, hrf_filters, weights, voxel_parcel, parcel_owner):
    series = features.astype(jnp.float32).T
    largest_delay = TAP_SPACING * (FILTER_TAPS - 1)
    padded = jnp.pad(series, ((0, 0), (largest_delay, 0)))
    filtered = jnp.zeros((BASES, CH, TIME), jnp.float32)
    for delay_index in range(FILTER_TAPS):
        window_start = largest_delay - TAP_SPACING * delay_index
        lagged = padded[:, window_start:window_start + TIME]
        filtered = filtered + hrf_filters[:, :, delay_index][:, :, None] * lagged[None]
    design = filtered.astype(jnp.bfloat16)
    chan_width = CH // N_CHAN

    def add_block(running, block_index):
        start = (block_index * chan_width).astype(jnp.int32)
        design_block = lax.dynamic_slice_in_dim(design, start, chan_width, 1).reshape(BASES * chan_width, TIME)
        weight_block = lax.dynamic_slice_in_dim(weights, start, chan_width, 1).reshape(BASES * chan_width, VOXELS)
        partial_value = lax.dot_general(weight_block, design_block, (((0,), (0,)), ((), ())), preferred_element_type=jnp.float32)
        rounded = lax.optimization_barrier(partial_value.astype(jnp.bfloat16))
        return running + rounded.astype(jnp.float32), None

    running, _ = lax.scan(add_block, jnp.zeros((VOXELS, TIME), jnp.float32), jnp.arange(N_CHAN, dtype=jnp.int32))
    predicted = running.astype(jnp.bfloat16)
    parcel_holders = parcel_owner[voxel_parcel].astype(jnp.int32)
    grouped = parcel_holders.reshape(N_VOX, VOX_DEV)
    onehot = (grouped[:, :, None] == jnp.arange(N_VOX, dtype=jnp.int32)[None, None, :]).astype(jnp.int32)
    before = jnp.cumsum(onehot, axis=1) - onehot
    slot_index = jnp.sum(before * onehot, axis=2)
    source = jnp.arange(N_VOX, dtype=jnp.int32)[:, None]
    target_row = ((grouped * N_VOX + source) * SEND + slot_index).reshape(-1).astype(jnp.int32)
    owned = jnp.zeros((N_VOX * N_VOX * SEND, TIME), jnp.bfloat16).at[target_row].set(predicted)
    return owned.reshape(N_VOX * N_VOX, SEND, TIME)
```

```python
import functools

import jax
import jax.numpy as jnp
from jax import lax
from jax.experimental import pallas as pl
from jax.experimental.pallas import tpu as pltpu
from jax.sharding import PartitionSpec as P

FILTER_TAPS = 16
TAP_SPACING = 2
LANES = 128
SLOT_TILE = 128
VOX_BLOCK = 256
GROUP = 8
CHUNKS = 5
MIB = 1 << 20

VMEM = functools.partial(pl.BlockSpec, memory_space=pltpu.VMEM)
SMEM = functools.partial(pl.BlockSpec, memory_space=pltpu.SMEM)


def places_kernel(send_cap, owners, parcel_ref, table_ref, key_ref, start_ref):
    rows = parcel_ref.shape[0]
    parcel = parcel_ref[...]
    high, low = parcel >> 7, parcel & 127
    owner = jnp.zeros_like(parcel)
    for entry in range(table_ref.shape[0]):
        line = jnp.broadcast_to(table_ref[entry : entry + 1, :], parcel.shape)
        found = jnp.take_along_axis(line, low, axis=1, mode="promise_in_bounds")
        owner = jnp.where(high == entry, found, owner)
    above = lax.broadcasted_iota(jnp.int32, (LANES, LANES), 0) < lax.broadcasted_iota(jnp.int32, (LANES, LANES), 1)
    above = above.astype(jnp.float32).astype(jnp.bfloat16)
    ones = jnp.ones((LANES, LANES), jnp.bfloat16)
    ahead = lax.broadcasted_iota(jnp.int32, (rows, rows), 1) < lax.broadcasted_iota(jnp.int32, (rows, rows), 0)
    ahead = ahead.astype(jnp.float32).astype(jnp.bfloat16)
    step = VOX_BLOCK // LANES
    marks = start_ref.shape[0]
    block_ahead = lax.broadcasted_iota(jnp.int32, (marks, rows), 1) < step * lax.broadcasted_iota(jnp.int32, (marks, rows), 0)
    block_ahead = block_ahead.astype(jnp.float32).astype(jnp.bfloat16)
    lane = lax.broadcasted_iota(jnp.int32, (marks, LANES), 1)
    dot = functools.partial(jnp.dot, preferred_element_type=jnp.float32)
    key = jnp.zeros(parcel.shape, jnp.float32)
    starts = jnp.zeros((marks, LANES), jnp.float32)
    for o in range(owners):
        mine = owner == o
        hot = mine.astype(jnp.float32).astype(jnp.bfloat16)
        totals = dot(hot, ones).astype(jnp.bfloat16)
        slot = dot(hot, above) + dot(ahead, totals)
        key = jnp.where(mine, slot + float(o * send_cap), key)
        starts = jnp.where(lane == o, dot(block_ahead, totals), starts)
    key_ref[...] = key.astype(jnp.int32)
    start_ref[...] = starts.astype(jnp.int32)


def pairs_kernel(blocks, owners, start_ref, list_ref, count_ref):
    def at(index, count):
        block, owner = index // owners, lax.rem(index, owners)
        first, last = start_ref[block, owner], start_ref[block + 1, owner]
        low, high = first >> 7, (last - 1) >> 7
        word = (block << 16) | (owner << 8) | low
        for extra in range(VOX_BLOCK // SLOT_TILE + 1):
            list_ref[count + extra] = word + extra
        return count + jnp.where(last > first, high - low + 1, 0)

    count = lax.fori_loop(0, blocks * owners, at, jnp.int32(0))
    for extra in range(GROUP):
        list_ref[count + extra] = -1
    count_ref[0] = (count + GROUP - 1) // GROUP


def design_kernel(place_ref, series_ref, filter_ref, design_ref, shifted):
    time_len, width = series_ref.shape
    bases = filter_ref.shape[0]
    parts = place_ref.shape[0]
    block = time_len // parts
    rows = 32
    lead = TAP_SPACING * FILTER_TAPS
    for s in range(shifted.shape[0]):
        shifted[s, : lead + 8, :] = jnp.zeros((lead + 8, LANES), jnp.float32)

    def columns(tile, carry):
        at = pl.ds(pl.multiple_of(tile * LANES, LANES), LANES)
        series = series_ref[:, at].astype(jnp.float32)
        for s in range(shifted.shape[0]):
            shifted[s, lead + s * TAP_SPACING : lead + s * TAP_SPACING + time_len, :] = series
        for group in range(time_len // rows):
            sums = [jnp.zeros((rows, LANES), jnp.float32) for _ in range(bases)]
            for tap in range(FILTER_TAPS):
                delay = tap * TAP_SPACING
                start = lead + group * rows - 8 * (delay // 8)
                lagged = shifted[(delay % 8) // TAP_SPACING, start : start + rows, :]
                for b in range(bases):
                    sums[b] = sums[b] + filter_ref[b, tap : tap + 1, at] * lagged
            part, inner = (group * rows) // block, (group * rows) % block
            row = pl.ds(pl.multiple_of(place_ref[part] * block + inner, rows), rows)
            for b in range(bases):
                lanes = pl.ds(pl.multiple_of(b * width + tile * LANES, LANES), LANES)
                design_ref[row, lanes] = sums[b].astype(jnp.bfloat16)
        return carry

    lax.fori_loop(0, width // LANES, columns, 0)


def product_kernel(design_ref, weight_ref, keep_ref, send_ref):
    half = keep_ref.shape[0]
    weight = weight_ref[...]
    weight = weight.reshape(-1, weight.shape[2])
    total = jnp.dot(design_ref[...], weight, preferred_element_type=jnp.float32).astype(jnp.bfloat16)
    keep_ref[...] = total[:half]
    send_ref[...] = total[half:]


def product(design, weights, first, width):
    bases, depth, _ = weights.shape
    time_len = design.shape[0]
    out = jax.ShapeDtypeStruct((time_len // 2, width), jnp.bfloat16)
    offset = first // VOX_BLOCK
    return pl.pallas_call(
        product_kernel,
        grid=(width // VOX_BLOCK,),
        in_specs=[
            pl.BlockSpec(design.shape, lambda i: (0, 0)),
            pl.BlockSpec((bases, depth, VOX_BLOCK), lambda i: (0, 0, i + offset)),
        ],
        out_specs=[pl.BlockSpec((time_len // 2, VOX_BLOCK), lambda i: (0, i))] * 2,
        out_shape=[out, out],
        compiler_params=pltpu.CompilerParams(vmem_limit_bytes=24 * MIB),
        cost_estimate=pl.CostEstimate(
            flops=2 * time_len * bases * depth * width,
            bytes_accessed=2 * bases * depth * width + 2 * time_len * width,
            transcendentals=0,
        ),
        name="product",
    )(design, weights)


def pack_kernel(send_cap, chunks, list_ref, count_ref, key_ref, *refs):
    mine, theirs, packed_ref, summed = refs[:chunks], refs[chunks : 2 * chunks], refs[-2], refs[-1]
    width = mine[0].shape[1]
    for c in range(chunks):
        total = mine[c][...] + theirs[c][...].astype(jnp.float32)
        summed[:, c * width : (c + 1) * width] = total.astype(jnp.bfloat16)
    packed_ref[...] = jnp.zeros_like(packed_ref)
    slots = lax.broadcasted_iota(jnp.int32, (SLOT_TILE, VOX_BLOCK), 0)

    def group(g, carry):
        for i in range(GROUP):
            word = list_ref[g * GROUP + i]
            real = word >= 0
            word = jnp.where(real, word, 0)
            block, owner, tile = word >> 16, (word >> 8) & 255, word & 255
            base = jnp.where(real, owner * send_cap + tile * SLOT_TILE, -(1 << 20))
            hit = (key_ref[block] - base) == slots
            hit = jnp.where(hit, 1.0, 0.0).astype(jnp.bfloat16)
            values = summed[:, pl.ds(pl.multiple_of(block * VOX_BLOCK, VOX_BLOCK), VOX_BLOCK)]
            moved = lax.dot_general(values, hit, (((1,), (1,)), ((), ())), preferred_element_type=jnp.float32)
            at = pl.ds(pl.multiple_of(tile * SLOT_TILE, SLOT_TILE), SLOT_TILE)
            packed_ref[owner, :, at] = packed_ref[owner, :, at] + moved.astype(jnp.bfloat16)
        return carry

    lax.fori_loop(0, count_ref[0], group, 0)


def shards(features, hrf_filters, weights, voxel_parcel, parcel_owner):
    owners, parts = lax.axis_size("vox"), lax.axis_size("chan")
    me = lax.axis_index("chan")
    voxels = voxel_parcel.shape[0]
    send_cap = 2 * voxels // owners
    bases, depth, _ = weights.shape
    blocks = voxels // VOX_BLOCK
    time_block = features.shape[0]
    time_len = time_block * parts

    by_channel = lax.all_to_all(features, "chan", split_axis=1, concat_axis=0, tiled=True)

    table_rows = -(-parcel_owner.shape[0] // LANES)
    table = jnp.pad(parcel_owner, (0, table_rows * LANES - parcel_owner.shape[0])).reshape(table_rows, LANES)
    marks = -(-(blocks + 1) // 8) * 8
    key, starts = pl.pallas_call(
        functools.partial(places_kernel, send_cap, owners),
        in_specs=[VMEM(), VMEM()],
        out_specs=[VMEM(), VMEM()],
        out_shape=[
            jax.ShapeDtypeStruct((voxels // LANES, LANES), jnp.int32),
            jax.ShapeDtypeStruct((marks, LANES), jnp.int32),
        ],
        name="places",
    )(voxel_parcel.reshape(-1, LANES), table)
    pairs = blocks * owners + voxels // SLOT_TILE + owners + 2 * GROUP
    pair_list, pair_groups = pl.pallas_call(
        functools.partial(pairs_kernel, blocks, owners),
        in_specs=[SMEM()],
        out_specs=[SMEM(), SMEM()],
        out_shape=[jax.ShapeDtypeStruct((pairs,), jnp.int32), jax.ShapeDtypeStruct((1,), jnp.int32)],
        name="pairs",
    )(starts)
    key = key.reshape(blocks, 1, VOX_BLOCK)

    bits = parts.bit_length() - 1
    order = jnp.arange(parts, dtype=jnp.int32) ^ me
    place = sum(((order >> bit) & 1) << (bits - 1 - bit) for bit in range(bits)).astype(jnp.int32)
    design = pl.pallas_call(
        design_kernel,
        in_specs=[SMEM(), VMEM(), VMEM()],
        out_specs=VMEM(),
        out_shape=jax.ShapeDtypeStruct((time_len, bases * depth), jnp.bfloat16),
        scratch_shapes=[pltpu.VMEM((8 // TAP_SPACING, time_len + TAP_SPACING * FILTER_TAPS + 8, LANES), jnp.float32)],
        compiler_params=pltpu.CompilerParams(vmem_limit_bytes=24 * MIB),
        name="design",
    )(place, by_channel, jnp.transpose(hrf_filters, (0, 2, 1)))

    width = voxels // CHUNKS
    mine, theirs = [], []
    for c in range(CHUNKS):
        keep, send = product(design, weights, c * width, width)
        keep = keep.astype(jnp.float32)
        for bit in range(bits):
            got = lax.ppermute(send, "chan", [(i, i ^ (1 << bit)) for i in range(parts)])
            if bit == bits - 1:
                mine.append(keep)
                theirs.append(got)
            else:
                total = keep + got.astype(jnp.float32)
                rows = total.shape[0] // 2
                keep, send = total[:rows], total[rows:].astype(jnp.bfloat16)

    packed = pl.pallas_call(
        functools.partial(pack_kernel, send_cap, CHUNKS),
        in_specs=[SMEM(), SMEM()] + [VMEM()] * (1 + 2 * CHUNKS),
        out_specs=VMEM(),
        out_shape=jax.ShapeDtypeStruct((owners, time_block, send_cap), jnp.bfloat16),
        scratch_shapes=[pltpu.VMEM((time_block, voxels), jnp.bfloat16)],
        compiler_params=pltpu.CompilerParams(vmem_limit_bytes=24 * MIB),
        name="pack",
    )(pair_list, pair_groups, key, *mine, *theirs)
    received = lax.all_to_all(packed, "vox", split_axis=0, concat_axis=0, tiled=True)
    return jnp.transpose(received, (0, 2, 1))


def solution(mesh):
    return jax.shard_map(
        shards,
        mesh=mesh,
        in_specs=(P("chan", None), P(None, "chan", None), P(None, "chan", "vox"), P("vox"), P()),
        out_specs=P("vox", None, "chan"),
        check_vma=False,
    )
```

```python
import functools

import jax
import jax.numpy as jnp
from jax import lax
from jax.experimental import pallas as pl
from jax.experimental.pallas import tpu as pltpu
from jax.sharding import PartitionSpec as P

FILTER_TAPS = 16
TAP_SPACING = 2
LANES = 128
SLOT_TILE = 128
VOX_BLOCK = 256
PRODUCT_BLOCK = 512
GROUP = 8
CHUNKS = 5
MIB = 1 << 20

VMEM = functools.partial(pl.BlockSpec, memory_space=pltpu.VMEM)
SMEM = functools.partial(pl.BlockSpec, memory_space=pltpu.SMEM)
ANY = functools.partial(pl.BlockSpec, memory_space=pl.ANY)


def places_kernel(send_cap, owners, parcel_ref, table_ref, key_ref, start_ref):
    rows = parcel_ref.shape[0]
    parcel = parcel_ref[...]
    high, low = parcel >> 7, parcel & 127
    owner = jnp.zeros_like(parcel)
    for entry in range(table_ref.shape[0]):
        line = jnp.broadcast_to(table_ref[entry : entry + 1, :], parcel.shape)
        found = jnp.take_along_axis(line, low, axis=1, mode="promise_in_bounds")
        owner = jnp.where(high == entry, found, owner)
    above = lax.broadcasted_iota(jnp.int32, (LANES, LANES), 0) < lax.broadcasted_iota(jnp.int32, (LANES, LANES), 1)
    above = above.astype(jnp.float32).astype(jnp.bfloat16)
    ones = jnp.ones((LANES, LANES), jnp.bfloat16)
    ahead = lax.broadcasted_iota(jnp.int32, (rows, rows), 1) < lax.broadcasted_iota(jnp.int32, (rows, rows), 0)
    ahead = ahead.astype(jnp.float32).astype(jnp.bfloat16)
    step = VOX_BLOCK // LANES
    marks = start_ref.shape[0]
    block_ahead = lax.broadcasted_iota(jnp.int32, (marks, rows), 1) < step * lax.broadcasted_iota(jnp.int32, (marks, rows), 0)
    block_ahead = block_ahead.astype(jnp.float32).astype(jnp.bfloat16)
    lane = lax.broadcasted_iota(jnp.int32, (marks, LANES), 1)
    dot = functools.partial(jnp.dot, preferred_element_type=jnp.float32)
    key = jnp.zeros(parcel.shape, jnp.float32)
    starts = jnp.zeros((marks, LANES), jnp.float32)
    for o in range(owners):
        mine = owner == o
        hot = mine.astype(jnp.float32).astype(jnp.bfloat16)
        totals = dot(hot, ones).astype(jnp.bfloat16)
        slot = dot(hot, above) + dot(ahead, totals)
        key = jnp.where(mine, slot + float(o * send_cap), key)
        starts = jnp.where(lane == o, dot(block_ahead, totals), starts)
    key = key.astype(jnp.int32)
    for row in range(rows):
        line = jnp.broadcast_to(key[row : row + 1, :], (LANES, LANES))
        key_ref[row * LANES : (row + 1) * LANES, :] = line.T
    start_ref[...] = starts.astype(jnp.int32)


def pairs_kernel(blocks, owners, start_ref, list_ref, count_ref):
    def at(index, count):
        block, owner = index // owners, lax.rem(index, owners)
        first, last = start_ref[block, owner], start_ref[block + 1, owner]
        low, high = first >> 7, (last - 1) >> 7
        word = (block << 16) | (owner << 8) | low
        for extra in range(VOX_BLOCK // SLOT_TILE + 1):
            list_ref[count + extra] = word + extra
        return count + jnp.where(last > first, high - low + 1, 0)

    count = lax.fori_loop(0, blocks * owners, at, jnp.int32(0))
    for extra in range(GROUP):
        list_ref[count + extra] = -1
    count_ref[0] = (count + GROUP - 1) // GROUP


def design_kernel(parts, block_ref, place_ref, *refs):
    series_refs, (filter_ref, _, design_ref, plain, shifted) = refs[:parts], refs[parts:]
    block, width = series_refs[0].shape
    bases = filter_ref.shape[0]
    time_len = parts * block
    rows = 32
    lead = TAP_SPACING * FILTER_TAPS
    for s in range(shifted.shape[0]):
        shifted[s, : lead + 8, :] = jnp.zeros((lead + 8, LANES), jnp.float32)

    def columns(tile, carry):
        at = pl.ds(pl.multiple_of(tile * LANES, LANES), LANES)
        for d in range(parts):
            row = pl.ds(pl.multiple_of(block_ref[d] * block, block), block)
            plain[row, :] = series_refs[d][:, at].astype(jnp.float32)
        series = plain[...]
        for s in range(shifted.shape[0]):
            shifted[s, lead + s * TAP_SPACING : lead + s * TAP_SPACING + time_len, :] = series
        for group in range(time_len // rows):
            sums = [jnp.zeros((rows, LANES), jnp.float32) for _ in range(bases)]
            for tap in range(FILTER_TAPS):
                delay = tap * TAP_SPACING
                start = lead + group * rows - 8 * (delay // 8)
                lagged = shifted[(delay % 8) // TAP_SPACING, start : start + rows, :]
                for b in range(bases):
                    sums[b] = sums[b] + filter_ref[b, tap : tap + 1, at] * lagged
            part, inner = (group * rows) // block, (group * rows) % block
            row = pl.ds(pl.multiple_of(place_ref[part] * block + inner, rows), rows)
            for b in range(bases):
                lanes = pl.ds(pl.multiple_of(b * width + tile * LANES, LANES), LANES)
                design_ref[row, lanes] = sums[b].astype(jnp.bfloat16)
        return carry

    lax.fori_loop(0, width // LANES, columns, 0)


def product_kernel(design_ref, weight_ref, *refs):
    keep_ref, send_ref = refs[-2:]
    half = keep_ref.shape[0]
    weight = weight_ref[...]
    weight = weight.reshape(-1, weight.shape[2])
    total = jnp.dot(design_ref[...], weight, preferred_element_type=jnp.float32).astype(jnp.bfloat16)
    keep_ref[...] = total[:half]
    send_ref[...] = total[half:]


def product(design, weights, first, width, after):
    bases, depth, _ = weights.shape
    time_len = design.shape[0]
    out = jax.ShapeDtypeStruct((time_len // 2, width), jnp.bfloat16)
    offset = first // PRODUCT_BLOCK
    return pl.pallas_call(
        product_kernel,
        grid=(width // PRODUCT_BLOCK,),
        in_specs=[
            pl.BlockSpec(design.shape, lambda i: (0, 0)),
            pl.BlockSpec((bases, depth, PRODUCT_BLOCK), lambda i: (0, 0, i + offset)),
        ]
        + [ANY()] * len(after),
        out_specs=[pl.BlockSpec((time_len // 2, PRODUCT_BLOCK), lambda i: (0, i))] * 2,
        out_shape=[out, out],
        compiler_params=pltpu.CompilerParams(vmem_limit_bytes=32 * MIB),
        cost_estimate=pl.CostEstimate(
            flops=2 * time_len * bases * depth * width,
            bytes_accessed=2 * bases * depth * width + 2 * time_len * width,
            transcendentals=0,
        ),
        name="product",
    )(design, weights, *after)


def pack_kernel(send_cap, chunks, list_ref, count_ref, key_ref, *refs):
    terms, packed_ref, summed = refs[:-2], refs[-2], refs[-1]
    each = len(terms) // chunks
    width = terms[0].shape[1]
    for c in range(chunks):
        total = sum(term[: summed.shape[0], :].astype(jnp.float32) for term in terms[c * each : (c + 1) * each])
        summed[:, c * width : (c + 1) * width] = total.astype(jnp.bfloat16)
    packed_ref[...] = jnp.zeros_like(packed_ref)
    slots = lax.broadcasted_iota(jnp.int32, (VOX_BLOCK, SLOT_TILE), 1)

    def group(g, carry):
        for i in range(GROUP):
            word = list_ref[g * GROUP + i]
            real = word >= 0
            word = jnp.where(real, word, 0)
            block, owner, tile = word >> 16, (word >> 8) & 255, word & 255
            base = jnp.where(real, owner * send_cap + tile * SLOT_TILE, -(1 << 20))
            voxel = pl.ds(pl.multiple_of(block * VOX_BLOCK, VOX_BLOCK), VOX_BLOCK)
            hit = key_ref[voxel, :] == slots + base
            hit = jnp.where(hit, 1.0, 0.0).astype(jnp.bfloat16)
            moved = jnp.dot(summed[:, voxel], hit, preferred_element_type=jnp.float32)
            at = pl.ds(pl.multiple_of(tile * SLOT_TILE, SLOT_TILE), SLOT_TILE)
            packed_ref[owner, :, at] = packed_ref[owner, :, at] + moved.astype(jnp.bfloat16)
        return carry

    lax.fori_loop(0, count_ref[0], group, 0)


def shards(features, hrf_filters, weights, voxel_parcel, parcel_owner):
    owners, parts = lax.axis_size("vox"), lax.axis_size("chan")
    me = lax.axis_index("chan")
    voxels = voxel_parcel.shape[0]
    send_cap = 2 * voxels // owners
    bases, depth, _ = weights.shape
    blocks = voxels // VOX_BLOCK
    time_block = features.shape[0]
    time_len = time_block * parts

    series = [lax.dynamic_slice_in_dim(features, (me ^ d) * depth, depth, 1) for d in range(parts)]
    for d in range(1, parts):
        series[d] = lax.ppermute(series[d], "chan", [(i, i ^ d) for i in range(parts)])

    table_rows = -(-parcel_owner.shape[0] // LANES)
    table = jnp.pad(parcel_owner, (0, table_rows * LANES - parcel_owner.shape[0])).reshape(table_rows, LANES)
    marks = -(-(blocks + 1) // 8) * 8
    key, starts = pl.pallas_call(
        functools.partial(places_kernel, send_cap, owners),
        in_specs=[VMEM(), VMEM()],
        out_specs=[VMEM(), VMEM()],
        out_shape=[
            jax.ShapeDtypeStruct((voxels, LANES), jnp.int32),
            jax.ShapeDtypeStruct((marks, LANES), jnp.int32),
        ],
        name="places",
    )(voxel_parcel.reshape(-1, LANES), table)
    pairs = blocks * owners + voxels // SLOT_TILE + owners + 2 * GROUP
    pair_list, pair_groups = pl.pallas_call(
        functools.partial(pairs_kernel, blocks, owners),
        in_specs=[SMEM()],
        out_specs=[SMEM(), SMEM()],
        out_shape=[jax.ShapeDtypeStruct((pairs,), jnp.int32), jax.ShapeDtypeStruct((1,), jnp.int32)],
        name="pairs",
    )(starts)

    bits = parts.bit_length() - 1
    order = jnp.arange(parts, dtype=jnp.int32) ^ me
    place = sum(((order >> bit) & 1) << (bits - 1 - bit) for bit in range(bits)).astype(jnp.int32)
    design = pl.pallas_call(
        functools.partial(design_kernel, parts),
        in_specs=[SMEM(), SMEM()] + [VMEM()] * (parts + 1) + [ANY()],
        out_specs=VMEM(),
        out_shape=jax.ShapeDtypeStruct((time_len, bases * depth), jnp.bfloat16),
        scratch_shapes=[
            pltpu.VMEM((time_len, LANES), jnp.float32),
            pltpu.VMEM((8 // TAP_SPACING, time_len + TAP_SPACING * FILTER_TAPS + 8, LANES), jnp.float32),
        ],
        compiler_params=pltpu.CompilerParams(vmem_limit_bytes=32 * MIB),
        name="design",
    )(order, place, *series, jnp.transpose(hrf_filters, (0, 2, 1)), pair_list)

    width = voxels // CHUNKS
    terms, sent, got = [], [], []
    for c in range(CHUNKS):
        keep, send = product(design, weights, c * width, width, sent[max(c - 2, 0) : max(c - 1, 0)] + got[max(c - 3, 0) : max(c - 2, 0)])
        own = [keep]
        for bit in range(bits):
            if bit > 0:
                rows = own[-1].shape[0] // 2
                send = sum(term[rows : 2 * rows].astype(jnp.float32) for term in own).astype(jnp.bfloat16)
                if bit == 1:
                    sent.append(send)
            own.append(lax.ppermute(send, "chan", [(i, i ^ (1 << bit)) for i in range(parts)]))
        terms.extend(own)
        got.append(own[-1])

    packed = pl.pallas_call(
        functools.partial(pack_kernel, send_cap, CHUNKS),
        in_specs=[SMEM(), SMEM()] + [VMEM()] * (1 + len(terms)),
        out_specs=VMEM(),
        out_shape=jax.ShapeDtypeStruct((owners, time_block, send_cap), jnp.bfloat16),
        scratch_shapes=[pltpu.VMEM((time_block, voxels), jnp.bfloat16)],
        compiler_params=pltpu.CompilerParams(vmem_limit_bytes=32 * MIB),
        name="pack",
    )(pair_list, pair_groups, key, *terms)
    received = lax.all_to_all(packed, "vox", split_axis=0, concat_axis=0, tiled=True)
    return jnp.transpose(received, (0, 2, 1))


def solution(mesh):
    return jax.shard_map(
        shards,
        mesh=mesh,
        in_specs=(P("chan", None), P(None, "chan", None), P(None, "chan", "vox"), P("vox"), P()),
        out_specs=P("vox", None, "chan"),
        check_vma=False,
    )
```

```python
import functools

import jax
import jax.numpy as jnp
from jax import lax
from jax.experimental import pallas as pl
from jax.experimental.pallas import tpu as pltpu
from jax.sharding import PartitionSpec as P

FILTER_TAPS = 16
TAP_SPACING = 2
LANES = 128
SLOT_TILE = 128
VOX_BLOCK = 256
CHAN_SLICE = 512
CHUNK_UNITS = (2, 2, 2, 2, 1, 1)
PACK_FIRST = 4
MIB = 1 << 20

VMEM = functools.partial(pl.BlockSpec, memory_space=pltpu.VMEM)
SMEM = functools.partial(pl.BlockSpec, memory_space=pltpu.SMEM)
ANY = functools.partial(pl.BlockSpec, memory_space=pl.ANY)


def slices_of(depth):
    out = []
    for first in range(0, depth, CHAN_SLICE):
        size = min(CHAN_SLICE, depth - first)
        out.append((first, size, -(-size // LANES) * LANES))
    return out


def places_kernel(owners, spread, parcel_ref, table_ref, onehot_ref, tile_ref, start_ref):
    rows = parcel_ref.shape[0]
    parcel = parcel_ref[...]
    high, low = parcel >> 7, parcel & 127
    owner = jnp.zeros_like(parcel)
    for entry in range(table_ref.shape[0]):
        line = jnp.broadcast_to(table_ref[entry : entry + 1, :], parcel.shape)
        found = jnp.take_along_axis(line, low, axis=1, mode="promise_in_bounds")
        owner = jnp.where(high == entry, found, owner)

    def below(shape, scale=1):
        less = lax.broadcasted_iota(jnp.int32, shape, 1) < scale * lax.broadcasted_iota(jnp.int32, shape, 0)
        return less.astype(jnp.float32).astype(jnp.bfloat16)

    lane = lax.broadcasted_iota(jnp.int32, (LANES, LANES), 1)
    above = (lax.broadcasted_iota(jnp.int32, (LANES, LANES), 0) < lane).astype(jnp.float32).astype(jnp.bfloat16)
    ones = jnp.ones((LANES, LANES), jnp.bfloat16)
    marks = start_ref.shape[0]
    ahead, block_ahead = below((rows, rows)), below((marks, rows), VOX_BLOCK // LANES)
    mark_lane = lax.broadcasted_iota(jnp.int32, (marks, LANES), 1)
    dot = functools.partial(jnp.dot, preferred_element_type=jnp.float32)
    slots = jnp.zeros(parcel.shape, jnp.float32)
    starts = jnp.zeros((marks, LANES), jnp.float32)
    for o in range(owners):
        mine = owner == o
        hot = mine.astype(jnp.float32).astype(jnp.bfloat16)
        totals = dot(hot, ones).astype(jnp.bfloat16)
        slots = jnp.where(mine, dot(hot, above) + dot(ahead, totals), slots)
        starts = jnp.where(mark_lane == o, dot(block_ahead, totals), starts)
    slots = slots.astype(jnp.int32)
    start_ref[...] = starts.astype(jnp.int32)
    tile_ref[...] = owner * spread + (slots >> 7)
    inner = slots & 127
    for row in range(rows):
        line = jnp.broadcast_to(inner[row : row + 1, :], (LANES, LANES))
        hit = jnp.where(line.T == lane, 1.0, 0.0)
        onehot_ref[row * LANES : (row + 1) * LANES, :] = hit.astype(jnp.bfloat16)


def filter_tile(block_ref, place_ref, series_refs, filter_ref, design_ref, plain, shifted, at, lanes):
    parts, block = len(series_refs), series_refs[0].shape[0]
    time_len = parts * block
    rows = 32
    lead = TAP_SPACING * FILTER_TAPS
    column = slice(at, at + LANES)
    for d in range(parts):
        row = pl.ds(pl.multiple_of(block_ref[d] * block, block), block)
        plain[row, :] = series_refs[d][:, column].astype(jnp.float32)
    series = plain[...]
    for s in range(shifted.shape[0]):
        shifted[s, lead + s * TAP_SPACING : lead + s * TAP_SPACING + time_len, :] = series
    for group in range(time_len // rows):
        sums = [jnp.zeros((rows, LANES), jnp.float32) for _ in lanes]
        for tap in range(FILTER_TAPS):
            delay = tap * TAP_SPACING
            start = lead + group * rows - 8 * (delay // 8)
            lagged = shifted[(delay % 8) // TAP_SPACING, start : start + rows, :]
            for b in range(len(lanes)):
                sums[b] = sums[b] + filter_ref[b, tap : tap + 1, column] * lagged
        part, inner = (group * rows) // block, (group * rows) % block
        row = pl.ds(pl.multiple_of(place_ref[part] * block + inner, rows), rows)
        for b, lane in enumerate(lanes):
            design_ref[row, lane : lane + LANES] = sums[b].astype(jnp.bfloat16)


def weight_copies(weight_ref, buffers, sems, first, width):
    copies, depth = [], weight_ref.shape[1]
    for i, (start, size, padded) in enumerate(slices_of(depth)):
        if size < padded:
            buffers[i][:, size:, :] = jnp.zeros_like(buffers[i][:, size:, :])
        copies.append(
            pltpu.make_async_copy(
                weight_ref.at[:, pl.ds(start, size), pl.ds(first, width)],
                buffers[i].at[:, pl.ds(0, size), :],
                sems.at[i],
            )
        )
    for copy in copies:
        copy.start()
    return copies


def add_slice(design_ref, buffer, lane, total):
    weight = buffer[...]
    weight = weight.reshape(-1, weight.shape[2])
    total[...] += jnp.dot(
        design_ref[:, lane : lane + weight.shape[0]], weight, preferred_element_type=jnp.float32
    )


def hand_out(total, keep_ref, send_ref):
    half = keep_ref.shape[0]
    keep_ref[...] = total[:half, :].astype(jnp.bfloat16)
    send_ref[...] = total[half:, :].astype(jnp.bfloat16)


def product_kernel(first, extra, design_ref, weight_ref, *refs):
    keep_ref, send_ref, total, sems, *buffers = refs[extra:]
    copies = weight_copies(weight_ref, buffers, sems, first, keep_ref.shape[1])
    total[...] = jnp.zeros_like(total)
    lane = 0
    for copy, buffer in zip(copies, buffers):
        copy.wait()
        add_slice(design_ref, buffer, lane, total)
        lane += buffer.shape[0] * buffer.shape[1]
    hand_out(total, keep_ref, send_ref)


def first_kernel(parts, extra, block_ref, place_ref, *refs):
    series_refs, (filter_ref, weight_ref), refs = refs[:parts], refs[parts : parts + 2], refs[parts + 2 + extra :]
    design_ref, keep_ref, send_ref, plain, shifted, total, sems, *buffers = refs
    copies = weight_copies(weight_ref, buffers, sems, 0, keep_ref.shape[1])
    total[...] = jnp.zeros_like(total)
    bases = weight_ref.shape[0]
    lead = TAP_SPACING * FILTER_TAPS
    for s in range(shifted.shape[0]):
        shifted[s, : lead + 8, :] = jnp.zeros((lead + 8, LANES), jnp.float32)
    slices = slices_of(weight_ref.shape[1])

    def filters(i):
        start, _, padded = slices[i]
        for at in range(0, padded, LANES):
            lanes = [bases * start + b * padded + at for b in range(bases)]
            filter_tile(
                block_ref, place_ref, series_refs, filter_ref, design_ref, plain, shifted, start + at, lanes
            )

    filters(0)
    for i, (copy, buffer) in enumerate(zip(copies, buffers)):
        copy.wait()
        add_slice(design_ref, buffer, bases * slices[i][0], total)
        if i + 1 < len(copies):
            filters(i + 1)
    hand_out(total, keep_ref, send_ref)


def product(weights, time_len, first, width, after, design=None, sources=()):
    bases, depth, _ = weights.shape
    slices = slices_of(depth)
    half = jax.ShapeDtypeStruct((time_len // 2, width), jnp.bfloat16)
    lanes = bases * sum(padded for _, _, padded in slices)
    scratch = [pltpu.VMEM((time_len, width), jnp.float32), pltpu.SemaphoreType.DMA((len(slices),))]
    scratch += [pltpu.VMEM((bases, padded, width), jnp.bfloat16) for _, _, padded in slices]
    flops = 2 * time_len * bases * depth * width
    common = dict(
        compiler_params=pltpu.CompilerParams(vmem_limit_bytes=40 * MIB),
        cost_estimate=pl.CostEstimate(
            flops=flops, bytes_accessed=2 * bases * depth * width + 2 * time_len * width, transcendentals=0
        ),
    )
    if design is not None:
        return pl.pallas_call(
            functools.partial(product_kernel, first, len(after)),
            in_specs=[VMEM(), ANY()] + [ANY()] * len(after),
            out_specs=[VMEM(), VMEM()],
            out_shape=[half, half],
            scratch_shapes=scratch,
            name="product",
            **common,
        )(design, weights, *after)
    order, place, series, filters = sources
    parts = len(series)
    return pl.pallas_call(
        functools.partial(first_kernel, parts, len(after)),
        in_specs=[SMEM(), SMEM()] + [VMEM()] * (parts + 1) + [ANY()] + [ANY()] * len(after),
        out_specs=[VMEM(), VMEM(), VMEM()],
        out_shape=[jax.ShapeDtypeStruct((time_len, lanes), jnp.bfloat16), half, half],
        scratch_shapes=[
            pltpu.VMEM((time_len, LANES), jnp.float32),
            pltpu.VMEM((8 // TAP_SPACING, time_len + TAP_SPACING * FILTER_TAPS + 8, LANES), jnp.float32),
        ]
        + scratch,
        name="first_product",
        **common,
    )(order, place, *series, filters, weights, *after)


def pack_kernel(spread, widths, first, more, start_ref, onehot_ref, tile_ref, *refs):
    *terms, packed_ref, summed = refs
    if more:
        packed_ref[...] = terms.pop(0)[...]
    else:
        packed_ref[...] = jnp.zeros_like(packed_ref)
    owners, time_block, send_cap = packed_ref.shape
    each, at = len(terms) // len(widths), 0
    for c, width in enumerate(widths):
        total = sum(term[:time_block, :].astype(jnp.float32) for term in terms[c * each : (c + 1) * each])
        summed[:, at : at + width] = total.astype(jnp.bfloat16)
        at += width
    last_tile = send_cap // SLOT_TILE - 1
    step = VOX_BLOCK // LANES

    def block_step(index, carry):
        block = first + index
        values = summed[:, pl.ds(pl.multiple_of(index * VOX_BLOCK, VOX_BLOCK), VOX_BLOCK)]
        onehot = onehot_ref[pl.ds(pl.multiple_of(block * VOX_BLOCK, VOX_BLOCK), VOX_BLOCK), :]
        tiles = jnp.concatenate([tile_ref[pl.ds(block * step + i, 1), :] for i in range(step)], axis=1)

        def move(owner, tile):
            chosen = jnp.where(tiles == owner * spread + tile, 1.0, 0.0).astype(jnp.bfloat16)
            return jnp.dot(values * chosen, onehot, preferred_element_type=jnp.float32).astype(jnp.bfloat16)

        def put(owner, tile, moved):
            tile = jnp.minimum(tile, last_tile)
            at = pl.ds(pl.multiple_of(tile * SLOT_TILE, SLOT_TILE), SLOT_TILE)
            packed_ref[owner, :, at] = packed_ref[owner, :, at] + moved

        low = [start_ref[block, o] >> 7 for o in range(owners)]
        moved = [move(o, low[o] + extra) for o in range(owners) for extra in range(2)]
        for o in range(owners):
            for extra in range(2):
                put(o, low[o] + extra, moved[2 * o + extra])
        for o in range(owners):

            @pl.when((start_ref[block + 1, o] - 1) >> 7 > low[o] + 1)
            def _():
                put(o, low[o] + 2, move(o, low[o] + 2))

        return carry

    lax.fori_loop(0, sum(widths) // VOX_BLOCK, block_step, 0)


def shards(features, hrf_filters, weights, voxel_parcel, parcel_owner):
    owners, parts = lax.axis_size("vox"), lax.axis_size("chan")
    me = lax.axis_index("chan")
    voxels = voxel_parcel.shape[0]
    send_cap = 2 * voxels // owners
    bases, depth, _ = weights.shape
    blocks = voxels // VOX_BLOCK
    time_block = features.shape[0]
    time_len = time_block * parts

    series = [lax.dynamic_slice_in_dim(features, (me ^ d) * depth, depth, 1) for d in range(parts)]
    for d in range(1, parts):
        series[d] = lax.ppermute(series[d], "chan", [(i, i ^ d) for i in range(parts)])
    filters = jnp.transpose(hrf_filters, (0, 2, 1))
    spare = -depth % LANES
    if spare:
        series = [jnp.pad(part, ((0, 0), (0, spare))) for part in series]
        filters = jnp.pad(filters, ((0, 0), (0, 0), (0, spare)))

    table_rows = -(-parcel_owner.shape[0] // LANES)
    table = jnp.pad(parcel_owner, (0, table_rows * LANES - parcel_owner.shape[0])).reshape(table_rows, LANES)
    marks = -(-(blocks + 1) // 8) * 8
    spread = send_cap // SLOT_TILE + 3
    onehot, tiles, starts = pl.pallas_call(
        functools.partial(places_kernel, owners, spread),
        in_specs=[VMEM(), VMEM()],
        out_specs=[VMEM(), VMEM(), VMEM()],
        out_shape=[
            jax.ShapeDtypeStruct((voxels, LANES), jnp.bfloat16),
            jax.ShapeDtypeStruct((voxels // LANES, LANES), jnp.int32),
            jax.ShapeDtypeStruct((marks, LANES), jnp.int32),
        ],
        name="places",
    )(voxel_parcel.reshape(-1, LANES), table)

    bits = parts.bit_length() - 1
    order = jnp.arange(parts, dtype=jnp.int32) ^ me
    place = sum(((order >> bit) & 1) << (bits - 1 - bit) for bit in range(bits)).astype(jnp.int32)

    unit = voxels // sum(CHUNK_UNITS)
    widths = [unit * units for units in CHUNK_UNITS]
    terms, sent, got = [], [], []
    design, first = None, 0
    for c, width in enumerate(widths):
        if c == 0:
            design, keep, send = product(
                weights, time_len, first, width, [starts], sources=(order, place, series, filters)
            )
        else:
            after = sent[max(c - 2, 0) : max(c - 1, 0)] + got[max(c - 3, 0) : max(c - 2, 0)]
            keep, send = product(weights, time_len, first, width, after, design)
        first += width
        own = [keep]
        for bit in range(bits):
            if bit > 0:
                rows = own[-1].shape[0] // 2
                send = sum(term[rows : 2 * rows].astype(jnp.float32) for term in own).astype(jnp.bfloat16)
                if bit == 1:
                    sent.append(send)
            own.append(lax.ppermute(send, "chan", [(i, i ^ (1 << bit)) for i in range(parts)]))
        terms.append(own)
        got.append(own[-1])

    packed = []
    for low, high in ((0, PACK_FIRST), (PACK_FIRST, len(widths))):
        args = packed + [term for own in terms[low:high] for term in own]
        here = widths[low:high]
        packed = [
            pl.pallas_call(
                functools.partial(pack_kernel, spread, here, sum(widths[:low]) // VOX_BLOCK, len(packed)),
                in_specs=[SMEM(), VMEM(), VMEM()] + [VMEM()] * len(args),
                out_specs=VMEM(),
                out_shape=jax.ShapeDtypeStruct((owners, time_block, send_cap), jnp.bfloat16),
                scratch_shapes=[pltpu.VMEM((time_block, sum(here)), jnp.bfloat16)],
                compiler_params=pltpu.CompilerParams(vmem_limit_bytes=32 * MIB),
                name="pack",
            )(starts, onehot, tiles, *args)
        ]
    received = lax.all_to_all(packed[0], "vox", split_axis=0, concat_axis=0, tiled=True)
    return jnp.transpose(received, (0, 2, 1))


def solution(mesh):
    return jax.shard_map(
        shards,
        mesh=mesh,
        in_specs=(P("chan", None), P(None, "chan", None), P(None, "chan", "vox"), P("vox"), P()),
        out_specs=P("vox", None, "chan"),
        check_vma=False,
    )
```

```python
import functools

import jax
import jax.numpy as jnp
from jax import lax
from jax.experimental import pallas as pl
from jax.experimental.pallas import tpu as pltpu
from jax.sharding import PartitionSpec as P

FILTER_TAPS = 16
TAP_SPACING = 2
LANES = 128
SLOT_TILE = 128
VOX_BLOCK = 256
CHAN_SLICE = 512
COLUMNS = 512
CHUNK_UNITS = (5, 5, 4, 4, 2)
EARLY = 2
PACK_FIRST = 3
MIB = 1 << 20

VMEM = functools.partial(pl.BlockSpec, memory_space=pltpu.VMEM)
SMEM = functools.partial(pl.BlockSpec, memory_space=pltpu.SMEM)
ANY = functools.partial(pl.BlockSpec, memory_space=pl.ANY)


def copy_weights(weight_ref, held, sems, first):
    copies, depth = [], weight_ref.shape[1]
    for i, ref in enumerate(held):
        if ref.shape[1] > depth:
            ref[:, depth:, :] = jnp.zeros_like(ref[:, depth:, :])
        copies.append(
            pltpu.make_async_copy(
                weight_ref.at[:, :, pl.ds(first, ref.shape[2])], ref.at[:, pl.ds(0, depth), :], sems.at[i]
            )
        )
        copies[-1].start()
        first += ref.shape[2]
    return copies


def places_kernel(owners, spread, parcel_ref, table_ref, weight_ref, onehot_ref, tile_ref, start_ref, *refs):
    copies = copy_weights(weight_ref, refs[:-1], refs[-1], 0)
    rows = parcel_ref.shape[0]
    parcel = parcel_ref[...]
    high, low = parcel >> 7, parcel & 127
    owner = jnp.zeros_like(parcel)
    for entry in range(table_ref.shape[0]):
        line = jnp.broadcast_to(table_ref[entry : entry + 1, :], parcel.shape)
        found = jnp.take_along_axis(line, low, axis=1, mode="promise_in_bounds")
        owner = jnp.where(high == entry, found, owner)

    def below(shape, scale=1):
        less = lax.broadcasted_iota(jnp.int32, shape, 1) < scale * lax.broadcasted_iota(jnp.int32, shape, 0)
        return less.astype(jnp.float32).astype(jnp.bfloat16)

    lane = lax.broadcasted_iota(jnp.int32, (LANES, LANES), 1)
    above = (lax.broadcasted_iota(jnp.int32, (LANES, LANES), 0) < lane).astype(jnp.float32).astype(jnp.bfloat16)
    ones = jnp.ones((LANES, LANES), jnp.bfloat16)
    marks = start_ref.shape[0]
    ahead, block_ahead = below((rows, rows)), below((marks, rows), VOX_BLOCK // LANES)
    mark_lane = lax.broadcasted_iota(jnp.int32, (marks, LANES), 1)
    dot = functools.partial(jnp.dot, preferred_element_type=jnp.float32)
    slots = jnp.zeros(parcel.shape, jnp.float32)
    starts = jnp.zeros((marks, LANES), jnp.float32)
    for o in range(owners):
        mine = owner == o
        hot = mine.astype(jnp.float32).astype(jnp.bfloat16)
        totals = dot(hot, ones).astype(jnp.bfloat16)
        slots = jnp.where(mine, dot(hot, above) + dot(ahead, totals), slots)
        starts = jnp.where(mark_lane == o, dot(block_ahead, totals), starts)
    slots = slots.astype(jnp.int32)
    start_ref[...] = starts.astype(jnp.int32)
    tile_ref[...] = owner * spread + (slots >> 7)
    inner = slots & 127
    for row in range(rows):
        line = jnp.broadcast_to(inner[row : row + 1, :], (LANES, LANES))
        hit = jnp.where(line.T == lane, 1.0, 0.0)
        onehot_ref[row * LANES : (row + 1) * LANES, :] = hit.astype(jnp.bfloat16)
    for copy in copies:
        copy.wait()


def filter_tile(block_ref, place_ref, series_refs, filter_ref, design_ref, plain, shifted, at, lanes):
    parts, block = len(series_refs), series_refs[0].shape[0]
    time_len = parts * block
    rows = 32
    lead = TAP_SPACING * FILTER_TAPS
    column = slice(at, at + LANES)
    for d in range(parts):
        row = pl.ds(pl.multiple_of(block_ref[d] * block, block), block)
        plain[row, :] = series_refs[d][:, column].astype(jnp.float32)
    series = plain[...]
    for s in range(shifted.shape[0]):
        shifted[s, lead + s * TAP_SPACING : lead + s * TAP_SPACING + time_len, :] = series
    for group in range(time_len // rows):
        sums = [jnp.zeros((rows, LANES), jnp.float32) for _ in lanes]
        for tap in range(FILTER_TAPS):
            delay = tap * TAP_SPACING
            start = lead + group * rows - 8 * (delay // 8)
            lagged = shifted[(delay % 8) // TAP_SPACING, start : start + rows, :]
            for b in range(len(lanes)):
                sums[b] = sums[b] + filter_ref[b, tap : tap + 1, column] * lagged
        part, inner = (group * rows) // block, (group * rows) % block
        row = pl.ds(pl.multiple_of(place_ref[part] * block + inner, rows), rows)
        for b, lane in enumerate(lanes):
            design_ref[row, lane : lane + LANES] = sums[b].astype(jnp.bfloat16)


def hand_out(total, keep_ref, send_ref, columns):
    half = keep_ref.shape[0]
    keep_ref[:, columns] = total[:half].astype(jnp.bfloat16)
    send_ref[:, columns] = total[half:].astype(jnp.bfloat16)


def product_kernel(extra, design_ref, weight_ref, *refs):
    keep_ref, send_ref = refs[extra:]
    width = keep_ref.shape[1]
    for at in range(0, width, COLUMNS):
        columns = slice(at, min(at + COLUMNS, width))
        weight = weight_ref[:, :, columns]
        weight = weight.reshape(-1, weight.shape[2])
        total = jnp.dot(design_ref[...], weight, preferred_element_type=jnp.float32)
        hand_out(total, keep_ref, send_ref, columns)


def first_kernel(parts, extra, ahead, block_ref, place_ref, *refs):
    series_refs, (filter_ref, weight_ref, rest_ref), refs = refs[:parts], refs[parts : parts + 3], refs[parts + 3 + extra :]
    design_ref, keep_ref, send_ref, *held, plain, shifted, total, sems = refs
    copies = copy_weights(rest_ref, held, sems, ahead)
    total[...] = jnp.zeros_like(total)
    bases, depth, width = weight_ref.shape
    lead = TAP_SPACING * FILTER_TAPS
    for s in range(shifted.shape[0]):
        shifted[s, : lead + 8, :] = jnp.zeros((lead + 8, LANES), jnp.float32)

    def filters(start):
        for at in range(start, min(start + CHAN_SLICE, depth), LANES):
            lanes = [b * depth + at for b in range(bases)]
            filter_tile(block_ref, place_ref, series_refs, filter_ref, design_ref, plain, shifted, at, lanes)

    filters(0)
    for start in range(0, depth, CHAN_SLICE):
        end = min(start + CHAN_SLICE, depth)
        for b in range(bases):
            part = design_ref[:, b * depth + start : b * depth + end]
            total[...] += jnp.dot(part, weight_ref[b, start:end, :], preferred_element_type=jnp.float32)
        if end < depth:
            filters(end)
    hand_out(total[...], keep_ref, send_ref, slice(0, width))
    for copy in copies:
        copy.wait()


def cost(flops, read):
    return pl.CostEstimate(flops=flops, bytes_accessed=read, transcendentals=0)


def halves(time_len, width):
    return [jax.ShapeDtypeStruct((time_len // 2, width), jnp.bfloat16)] * 2


def first_product(order, place, series, filters, weight, weights, widths, ahead, after):
    parts = len(series)
    bases, depth, width = weight.shape
    time_len = parts * series[0].shape[0]
    return pl.pallas_call(
        functools.partial(first_kernel, parts, len(after), ahead),
        in_specs=[SMEM(), SMEM()] + [VMEM()] * (parts + 2) + [ANY()] * (1 + len(after)),
        out_specs=[VMEM()] * (3 + len(widths)),
        out_shape=[jax.ShapeDtypeStruct((time_len, bases * depth), jnp.bfloat16)]
        + halves(time_len, width)
        + [pltpu.VMEM((bases, depth, w), jnp.bfloat16) for w in widths],
        scratch_shapes=[
            pltpu.VMEM((time_len, LANES), jnp.float32),
            pltpu.VMEM((8 // TAP_SPACING, time_len + TAP_SPACING * FILTER_TAPS + 8, LANES), jnp.float32),
            pltpu.VMEM((time_len, width), jnp.float32),
            pltpu.SemaphoreType.DMA((len(widths),)),
        ],
        compiler_params=pltpu.CompilerParams(vmem_limit_bytes=12 * MIB),
        cost_estimate=cost(4 * time_len * bases * depth * width, 2 * bases * depth * sum(widths)),
        name="first_product",
    )(order, place, *series, filters, weight, weights, *after)


def product(design, weight, after):
    time_len, lanes = design.shape
    width = weight.shape[2]
    return pl.pallas_call(
        functools.partial(product_kernel, len(after)),
        in_specs=[VMEM(), VMEM()] + [ANY()] * len(after),
        out_specs=[VMEM(), VMEM()],
        out_shape=halves(time_len, width),
        compiler_params=pltpu.CompilerParams(vmem_limit_bytes=12 * MIB),
        cost_estimate=cost(2 * time_len * lanes * width, 2 * lanes * width),
        name="product",
    )(design, weight, *after)


def pack_kernel(spread, widths, first, more, start_ref, onehot_ref, tile_ref, *refs):
    *terms, packed_ref, summed = refs
    if more:
        packed_ref[...] = terms.pop(0)[...]
    else:
        packed_ref[...] = jnp.zeros_like(packed_ref)
    owners, time_block, send_cap = packed_ref.shape
    each, at = len(terms) // len(widths), 0
    for c, width in enumerate(widths):
        total = sum(term[:time_block, :].astype(jnp.float32) for term in terms[c * each : (c + 1) * each])
        summed[:, at : at + width] = total.astype(jnp.bfloat16)
        at += width
    last_tile = send_cap // SLOT_TILE - 1
    step = VOX_BLOCK // LANES

    def block_step(index, carry):
        block = first + index
        values = summed[:, pl.ds(pl.multiple_of(index * VOX_BLOCK, VOX_BLOCK), VOX_BLOCK)]
        onehot = onehot_ref[pl.ds(pl.multiple_of(block * VOX_BLOCK, VOX_BLOCK), VOX_BLOCK), :]
        tiles = jnp.concatenate([tile_ref[pl.ds(block * step + i, 1), :] for i in range(step)], axis=1)

        def move(owner, tile):
            chosen = jnp.where(tiles == owner * spread + tile, 1.0, 0.0).astype(jnp.bfloat16)
            return jnp.dot(values * chosen, onehot, preferred_element_type=jnp.float32).astype(jnp.bfloat16)

        def put(owner, tile, moved):
            tile = jnp.minimum(tile, last_tile)
            at = pl.ds(pl.multiple_of(tile * SLOT_TILE, SLOT_TILE), SLOT_TILE)
            packed_ref[owner, :, at] = packed_ref[owner, :, at] + moved

        low = [start_ref[block, o] >> 7 for o in range(owners)]
        moved = [move(o, low[o] + extra) for o in range(owners) for extra in range(2)]
        for o in range(owners):
            for extra in range(2):
                put(o, low[o] + extra, moved[2 * o + extra])
        for o in range(owners):

            @pl.when((start_ref[block + 1, o] - 1) >> 7 > low[o] + 1)
            def _():
                put(o, low[o] + 2, move(o, low[o] + 2))

        return carry

    lax.fori_loop(0, sum(widths) // VOX_BLOCK, block_step, 0)


def shards(features, hrf_filters, weights, voxel_parcel, parcel_owner):
    owners, parts = lax.axis_size("vox"), lax.axis_size("chan")
    me = lax.axis_index("chan")
    voxels = voxel_parcel.shape[0]
    send_cap = 2 * voxels // owners
    bases, depth, _ = weights.shape
    blocks = voxels // VOX_BLOCK
    time_block = features.shape[0]
    time_len = time_block * parts

    series = [lax.dynamic_slice_in_dim(features, (me ^ d) * depth, depth, 1) for d in range(parts)]
    for d in range(1, parts):
        series[d] = lax.ppermute(series[d], "chan", [(i, i ^ d) for i in range(parts)])
    filters = jnp.transpose(hrf_filters, (0, 2, 1))
    spare = -depth % LANES
    if spare:
        series = [jnp.pad(part, ((0, 0), (0, spare))) for part in series]
        filters = jnp.pad(filters, ((0, 0), (0, 0), (0, spare)))

    table_rows = -(-parcel_owner.shape[0] // LANES)
    table = jnp.pad(parcel_owner, (0, table_rows * LANES - parcel_owner.shape[0])).reshape(table_rows, LANES)
    marks = -(-(blocks + 1) // 8) * 8
    spread = send_cap // SLOT_TILE + 3
    unit = voxels // sum(CHUNK_UNITS)
    widths = [unit * units for units in CHUNK_UNITS]
    onehot, tiles, starts, *held = pl.pallas_call(
        functools.partial(places_kernel, owners, spread),
        in_specs=[VMEM(), VMEM(), ANY()],
        out_specs=[VMEM()] * (3 + EARLY),
        out_shape=[
            jax.ShapeDtypeStruct((voxels, LANES), jnp.bfloat16),
            jax.ShapeDtypeStruct((voxels // LANES, LANES), jnp.int32),
            jax.ShapeDtypeStruct((marks, LANES), jnp.int32),
        ]
        + [pltpu.VMEM((bases, depth + spare, width), jnp.bfloat16) for width in widths[:EARLY]],
        scratch_shapes=[pltpu.SemaphoreType.DMA((EARLY,))],
        compiler_params=pltpu.CompilerParams(vmem_limit_bytes=8 * MIB),
        cost_estimate=cost(0, 2 * bases * depth * sum(widths[:EARLY])),
        name="places",
    )(voxel_parcel.reshape(-1, LANES), table, weights)

    bits = parts.bit_length() - 1
    order = jnp.arange(parts, dtype=jnp.int32) ^ me
    place = sum(((order >> bit) & 1) << (bits - 1 - bit) for bit in range(bits)).astype(jnp.int32)

    terms, sent, got = [], [], []
    for c in range(len(widths)):
        if c == 0:
            design, keep, send, *rest = first_product(
                order, place, series, filters, held[0], weights, widths[EARLY:], sum(widths[:EARLY]), [starts]
            )
            held = held + rest
        else:
            after = sent[max(c - 2, 0) : max(c - 1, 0)] + got[max(c - 3, 0) : max(c - 2, 0)]
            keep, send = product(design, held[c], after)
        own = [keep]
        for bit in range(bits):
            if bit > 0:
                rows = own[-1].shape[0] // 2
                send = sum(term[rows : 2 * rows].astype(jnp.float32) for term in own).astype(jnp.bfloat16)
                if bit == 1:
                    sent.append(send)
            own.append(lax.ppermute(send, "chan", [(i, i ^ (1 << bit)) for i in range(parts)]))
        terms.append(own)
        got.append(own[-1])

    packed = []
    for low, high in ((0, PACK_FIRST), (PACK_FIRST, len(widths))):
        args = packed + [term for own in terms[low:high] for term in own]
        here = widths[low:high]
        packed = [
            pl.pallas_call(
                functools.partial(pack_kernel, spread, here, sum(widths[:low]) // VOX_BLOCK, len(packed)),
                in_specs=[SMEM(), VMEM(), VMEM()] + [VMEM()] * len(args),
                out_specs=VMEM(),
                out_shape=jax.ShapeDtypeStruct((owners, time_block, send_cap), jnp.bfloat16),
                scratch_shapes=[pltpu.VMEM((time_block, sum(here)), jnp.bfloat16)],
                compiler_params=pltpu.CompilerParams(vmem_limit_bytes=12 * MIB),
                name="pack",
            )(starts, onehot, tiles, *args)
        ]
    received = lax.all_to_all(packed[0], "vox", split_axis=0, concat_axis=0, tiled=True)
    return jnp.transpose(received, (0, 2, 1))


def solution(mesh):
    return jax.shard_map(
        shards,
        mesh=mesh,
        in_specs=(P("chan", None), P(None, "chan", None), P(None, "chan", "vox"), P("vox"), P()),
        out_specs=P("vox", None, "chan"),
        check_vma=False,
    )
```

```python
import functools

import jax
import jax.numpy as jnp
from jax import lax
from jax.experimental import pallas as pl
from jax.experimental.pallas import tpu as pltpu
from jax.sharding import PartitionSpec as P

FILTER_TAPS = 16
TAP_SPACING = 2
LANES = 128
SLOT_TILE = 128
VOX_BLOCK = 256
COLUMNS = 512
ROWS = 32
PIECE_UNITS = (9, 4, 1, 3, 3)
CHUNK_PARTS = (
    ((0, 0, 2),),
    ((0, 2, 6),),
    ((0, 6, 9), (1, 0, 2)),
    ((1, 2, 4), (2, 0, 1), (3, 0, 2)),
    ((3, 2, 3), (4, 0, 3)),
)
PACK_FIRST = 3
MIB = 1 << 20

VMEM = functools.partial(pl.BlockSpec, memory_space=pltpu.VMEM)
SMEM = functools.partial(pl.BlockSpec, memory_space=pltpu.SMEM)
ANY = functools.partial(pl.BlockSpec, memory_space=pl.ANY)


def copy_piece(weight_ref, piece_ref, sem, first):
    depth = weight_ref.shape[1]
    if piece_ref.shape[1] > depth:
        piece_ref[:, depth:, :] = jnp.zeros_like(piece_ref[:, depth:, :])
    copy = pltpu.make_async_copy(
        weight_ref.at[:, :, pl.ds(first, piece_ref.shape[2])], piece_ref.at[:, pl.ds(0, depth), :], sem
    )
    copy.start()
    return copy


def cost(flops, read):
    return pl.CostEstimate(flops=flops, bytes_accessed=read, transcendentals=0)


def places(owners, spread, parcel_ref, table_ref, onehot_ref, tile_ref, start_ref):
    rows = parcel_ref.shape[0]
    parcel = parcel_ref[...]
    high, low = parcel >> 7, parcel & 127
    owner = jnp.zeros_like(parcel)
    for entry in range(table_ref.shape[0]):
        line = jnp.broadcast_to(table_ref[entry : entry + 1, :], parcel.shape)
        found = jnp.take_along_axis(line, low, axis=1, mode="promise_in_bounds")
        owner = jnp.where(high == entry, found, owner)

    def below(shape, scale=1):
        less = lax.broadcasted_iota(jnp.int32, shape, 1) < scale * lax.broadcasted_iota(jnp.int32, shape, 0)
        return less.astype(jnp.float32).astype(jnp.bfloat16)

    lane = lax.broadcasted_iota(jnp.int32, (LANES, LANES), 1)
    above = (lax.broadcasted_iota(jnp.int32, (LANES, LANES), 0) < lane).astype(jnp.float32).astype(jnp.bfloat16)
    ones = jnp.ones((LANES, LANES), jnp.bfloat16)
    marks = start_ref.shape[0]
    ahead, block_ahead = below((rows, rows)), below((marks, rows), VOX_BLOCK // LANES)
    mark_lane = lax.broadcasted_iota(jnp.int32, (marks, LANES), 1)
    dot = functools.partial(jnp.dot, preferred_element_type=jnp.float32)
    slots = jnp.zeros(parcel.shape, jnp.float32)
    starts = jnp.zeros((marks, LANES), jnp.float32)
    for o in range(owners):
        mine = owner == o
        hot = mine.astype(jnp.float32).astype(jnp.bfloat16)
        totals = dot(hot, ones).astype(jnp.bfloat16)
        slots = jnp.where(mine, dot(hot, above) + dot(ahead, totals), slots)
        starts = jnp.where(mark_lane == o, dot(block_ahead, totals), starts)
    slots = slots.astype(jnp.int32)
    start_ref[...] = starts.astype(jnp.int32)
    tile_ref[...] = owner * spread + (slots >> 7)
    inner = slots & 127
    for row in range(rows):
        line = jnp.broadcast_to(inner[row : row + 1, :], (LANES, LANES))
        hit = jnp.where(line.T == lane, 1.0, 0.0)
        onehot_ref[row * LANES : (row + 1) * LANES, :] = hit.astype(jnp.bfloat16)


def clear_lead(shifted):
    lead = TAP_SPACING * FILTER_TAPS
    for s in range(shifted.shape[0]):
        shifted[s, : lead + 8, :] = jnp.zeros((lead + 8, LANES), jnp.float32)


def shift(plain, shifted):
    lead, time_len = TAP_SPACING * FILTER_TAPS, plain.shape[0]
    series = plain[...]
    for s in range(shifted.shape[0]):
        shifted[s, lead + s * TAP_SPACING : lead + s * TAP_SPACING + time_len, :] = series


def filter_rows(shifted, filter_ref, column, first):
    lead = TAP_SPACING * FILTER_TAPS
    sums = [jnp.zeros((ROWS, LANES), jnp.float32) for _ in range(filter_ref.shape[0])]
    for tap in range(FILTER_TAPS):
        delay = tap * TAP_SPACING
        start = lead + first - 8 * (delay // 8)
        if not isinstance(start, int):
            start = pl.multiple_of(start, 8)
        lagged = shifted[(delay % 8) // TAP_SPACING, pl.ds(start, ROWS), :]
        for b in range(len(sums)):
            sums[b] = sums[b] + filter_ref[b, tap : tap + 1, column] * lagged
    return sums


def lane_tile(tile):
    return pl.ds(pl.multiple_of(tile * LANES, LANES), LANES)


def early_kernel(owners, spread, order_ref, own_ref, pair_ref, parcel_ref, table_ref, filter_ref, weight_ref, *refs):
    onehot_ref, tile_ref, start_ref, design_ref, piece_ref, plain, shifted, sems = refs
    copy = copy_piece(weight_ref, piece_ref, sems.at[0], 0)
    block, width = own_ref.shape
    core = lax.rem(order_ref[0], 2)
    own = pl.ds(pl.multiple_of(core * block, block), block)
    pair = pl.ds(pl.multiple_of((1 - core) * block, block), block)
    clear_lead(shifted)

    def columns(tile, carry):
        column = lane_tile(tile)
        plain[own, :] = own_ref[:, column].astype(jnp.float32)
        plain[pair, :] = pair_ref[:, column].astype(jnp.float32)
        shift(plain, shifted)
        for first in range(ROWS, 2 * block, ROWS):
            for b, rows in enumerate(filter_rows(shifted, filter_ref, column, first)):
                lanes = pl.ds(pl.multiple_of(b * width + tile * LANES, LANES), LANES)
                design_ref[first - ROWS : first, lanes] = rows.astype(jnp.bfloat16)
        return carry

    lax.fori_loop(0, width // LANES, columns, 0)
    places(owners, spread, parcel_ref, table_ref, onehot_ref, tile_ref, start_ref)
    copy.wait()


def design_kernel(parts, first, order_ref, place_ref, early_ref, filter_ref, weight_ref, *refs):
    series_refs, (design_ref, piece_ref, plain, shifted, sems) = refs[:parts], refs[parts:]
    copy = copy_piece(weight_ref, piece_ref, sems.at[0], first)
    block, width = series_refs[0].shape
    chip = order_ref[0] >> 1
    clear_lead(shifted)

    def place(part, inner):
        return pl.ds(pl.multiple_of(place_ref[part] * block + inner, ROWS), ROWS)

    for first in range(ROWS, 2 * block, ROWS):
        row = place(2 * chip + first // block, first % block)
        design_ref[row, :] = early_ref[first - ROWS : first, :]

    def columns(tile, carry):
        column = lane_tile(tile)
        for d in range(parts):
            row = pl.ds(pl.multiple_of(order_ref[d] * block, block), block)
            plain[row, :] = series_refs[d][:, column].astype(jnp.float32)
        shift(plain, shifted)
        for other in range(parts // 2):
            for inner in range(0, 2 * block if other else ROWS, ROWS):
                part = 2 * (chip ^ other) + inner // block
                start = part * block + inner % block
                row = place(part, inner % block)
                for b, rows in enumerate(filter_rows(shifted, filter_ref, column, start)):
                    lanes = pl.ds(pl.multiple_of(b * width + tile * LANES, LANES), LANES)
                    design_ref[row, lanes] = rows.astype(jnp.bfloat16)
        return carry

    lax.fori_loop(0, width // LANES, columns, 0)
    copy.wait()


def filter_scratch(time_len):
    return [
        pltpu.VMEM((time_len, LANES), jnp.float32),
        pltpu.VMEM((8 // TAP_SPACING, time_len + TAP_SPACING * FILTER_TAPS + 8, LANES), jnp.float32),
    ]


def product_kernel(extra, bounds, first, design_ref, *refs):
    weight_refs, refs = refs[: len(bounds)], refs[len(bounds) + extra :]
    copy = None
    if first is not None:
        weight_ref, keep_ref, send_ref, piece_ref, sems = refs
        copy = copy_piece(weight_ref, piece_ref, sems.at[0], first)
    else:
        keep_ref, send_ref = refs
    half, at = keep_ref.shape[0], 0
    for ref, (low, high) in zip(weight_refs, bounds):
        for start in range(low, high, COLUMNS):
            weight = ref[:, :, start : min(start + COLUMNS, high)]
            weight = weight.reshape(-1, weight.shape[2])
            total = jnp.dot(design_ref[...], weight, preferred_element_type=jnp.float32)
            columns = slice(at, at + weight.shape[1])
            keep_ref[:, columns] = total[:half].astype(jnp.bfloat16)
            send_ref[:, columns] = total[half:].astype(jnp.bfloat16)
            at += weight.shape[1]
    if copy is not None:
        copy.wait()


def product(design, parts, after, weights, ahead):
    time_len, lanes = design.shape
    bounds = tuple((low, high) for _, low, high in parts)
    width = sum(high - low for low, high in bounds)
    half = jax.ShapeDtypeStruct((time_len // 2, width), jnp.bfloat16)
    held = parts[0][0].shape
    more = [ahead] if ahead else []
    return pl.pallas_call(
        functools.partial(product_kernel, len(after), bounds, ahead[0] if ahead else None),
        in_specs=[VMEM()] * (1 + len(parts)) + [ANY()] * (len(after) + len(more)),
        out_specs=[VMEM()] * (2 + len(more)),
        out_shape=[half, half] + [pltpu.VMEM((*held[:2], size), jnp.bfloat16) for _, size in more],
        scratch_shapes=[pltpu.SemaphoreType.DMA((1,)) for _ in more],
        compiler_params=pltpu.CompilerParams(vmem_limit_bytes=10 * MIB),
        cost_estimate=cost(2 * time_len * lanes * width, 2 * lanes * width),
        name="product",
    )(design, *(piece for piece, _, _ in parts), *after, *([weights] if ahead else []))


def pack_kernel(spread, widths, first, more, start_ref, onehot_ref, tile_ref, *refs):
    *terms, packed_ref, summed = refs
    if more:
        packed_ref[...] = terms.pop(0)[...]
    else:
        packed_ref[...] = jnp.zeros_like(packed_ref)
    owners, time_block, send_cap = packed_ref.shape
    each, at = len(terms) // len(widths), 0
    for c, width in enumerate(widths):
        total = sum(term[:time_block, :].astype(jnp.float32) for term in terms[c * each : (c + 1) * each])
        summed[:, at : at + width] = total.astype(jnp.bfloat16)
        at += width
    last_tile = send_cap // SLOT_TILE - 1
    step = VOX_BLOCK // LANES

    def block_step(index, carry):
        block = first + index
        values = summed[:, pl.ds(pl.multiple_of(index * VOX_BLOCK, VOX_BLOCK), VOX_BLOCK)]
        onehot = onehot_ref[pl.ds(pl.multiple_of(block * VOX_BLOCK, VOX_BLOCK), VOX_BLOCK), :]
        tiles = jnp.concatenate([tile_ref[pl.ds(block * step + i, 1), :] for i in range(step)], axis=1)

        def chosen(owner, tile):
            hit = jnp.where(tiles == owner * spread + tile, 1.0, 0.0)
            return values * hit.astype(jnp.bfloat16)

        def put(owner, tile, moved):
            tile = jnp.minimum(tile, last_tile)
            at = pl.ds(pl.multiple_of(tile * SLOT_TILE, SLOT_TILE), SLOT_TILE)
            packed_ref[owner, :, at] = packed_ref[owner, :, at] + moved

        def move(targets):
            rows = jnp.concatenate([chosen(owner, tile) for owner, tile in targets], axis=0)
            moved = jnp.dot(rows, onehot, preferred_element_type=jnp.float32).astype(jnp.bfloat16)
            for i, (owner, tile) in enumerate(targets):
                put(owner, tile, moved[i * time_block : (i + 1) * time_block])

        low = [start_ref[block, o] >> 7 for o in range(owners)]
        high = [(start_ref[block + 1, o] - 1) >> 7 for o in range(owners)]
        move([(o, low[o] + extra) for extra in range(2) for o in range(owners)])
        longest = functools.reduce(jnp.maximum, [high[o] - low[o] for o in range(owners)])

        @pl.when(longest > 1)
        def _():
            move([(o, low[o] + 2) for o in range(owners)])

        return carry

    lax.fori_loop(0, sum(widths) // VOX_BLOCK, block_step, 0)


def shards(features, hrf_filters, weights, voxel_parcel, parcel_owner):
    owners, parts = lax.axis_size("vox"), lax.axis_size("chan")
    me = lax.axis_index("chan")
    voxels = voxel_parcel.shape[0]
    send_cap = 2 * voxels // owners
    bases, depth, _ = weights.shape
    blocks = voxels // VOX_BLOCK
    time_block = features.shape[0]
    time_len = time_block * parts

    series = [lax.dynamic_slice_in_dim(features, (me ^ d) * depth, depth, 1) for d in range(parts)]
    for d in range(1, parts):
        series[d] = lax.ppermute(series[d], "chan", [(i, i ^ d) for i in range(parts)])
    filters = jnp.transpose(hrf_filters, (0, 2, 1))
    unit = voxels // sum(PIECE_UNITS)
    pieces = [unit * units for units in PIECE_UNITS]
    firsts = [sum(pieces[:i]) for i in range(len(pieces))]
    spare = -depth % LANES
    held = lambda i: pltpu.VMEM((bases, depth + spare, pieces[i]), jnp.bfloat16)
    lanes = bases * (depth + spare)
    if spare:
        series = [jnp.pad(part, ((0, 0), (0, spare))) for part in series]
        filters = jnp.pad(filters, ((0, 0), (0, 0), (0, spare)))

    table_rows = -(-parcel_owner.shape[0] // LANES)
    table = jnp.pad(parcel_owner, (0, table_rows * LANES - parcel_owner.shape[0])).reshape(table_rows, LANES)
    marks = -(-(blocks + 1) // 8) * 8
    spread = send_cap // SLOT_TILE + 3
    bits = parts.bit_length() - 1
    order = jnp.arange(parts, dtype=jnp.int32) ^ me
    place = sum(((order >> bit) & 1) << (bits - 1 - bit) for bit in range(bits)).astype(jnp.int32)

    early_rows = 2 * time_block - ROWS
    onehot, tiles, starts, early, piece = pl.pallas_call(
        functools.partial(early_kernel, owners, spread),
        in_specs=[SMEM()] + [VMEM()] * 5 + [ANY()],
        out_specs=[VMEM()] * 5,
        out_shape=[
            jax.ShapeDtypeStruct((voxels, LANES), jnp.bfloat16),
            jax.ShapeDtypeStruct((voxels // LANES, LANES), jnp.int32),
            jax.ShapeDtypeStruct((marks, LANES), jnp.int32),
            jax.ShapeDtypeStruct((early_rows, lanes), jnp.bfloat16),
            held(0),
        ],
        scratch_shapes=filter_scratch(2 * time_block) + [pltpu.SemaphoreType.DMA((1,))],
        compiler_params=pltpu.CompilerParams(vmem_limit_bytes=10 * MIB),
        cost_estimate=cost(0, 2 * bases * depth * pieces[0]),
        name="early",
    )(order, series[0], series[1], voxel_parcel.reshape(-1, LANES), table, filters, weights)
    copied = [piece]
    design, piece = pl.pallas_call(
        functools.partial(design_kernel, parts, firsts[1]),
        in_specs=[SMEM(), SMEM(), VMEM(), VMEM(), ANY()] + [VMEM()] * parts,
        out_specs=[VMEM(), VMEM()],
        out_shape=[jax.ShapeDtypeStruct((time_len, lanes), jnp.bfloat16), held(1)],
        scratch_shapes=filter_scratch(time_len) + [pltpu.SemaphoreType.DMA((1,))],
        compiler_params=pltpu.CompilerParams(vmem_limit_bytes=10 * MIB),
        cost_estimate=cost(0, 2 * bases * depth * pieces[1]),
        name="design",
    )(order, place, early, filters, weights, *series)
    copied.append(piece)

    widths, terms, sent, got = [], [], [], []
    for c, chunk in enumerate(CHUNK_PARTS):
        takes = [(copied[i], unit * low, unit * high) for i, low, high in chunk]
        widths.append(sum(high - low for _, low, high in takes))
        after = sent[max(c - 2, 0) : max(c - 1, 0)] + got[max(c - 3, 0) : max(c - 2, 0)]
        more = len(copied) < len(pieces)
        ahead = (firsts[len(copied)], pieces[len(copied)]) if more else None
        keep, send, *piece = product(design, takes, after, weights, ahead)
        copied.extend(piece)
        own = [keep]
        for bit in range(bits):
            if bit > 0:
                rows = own[-1].shape[0] // 2
                send = sum(term[rows : 2 * rows].astype(jnp.float32) for term in own).astype(jnp.bfloat16)
                if bit == 1:
                    sent.append(send)
            own.append(lax.ppermute(send, "chan", [(i, i ^ (1 << bit)) for i in range(parts)]))
        terms.append(own)
        got.append(own[-1])

    packed = []
    for low, high in ((0, PACK_FIRST), (PACK_FIRST, len(widths))):
        args = packed + [term for own in terms[low:high] for term in own]
        here = widths[low:high]
        packed = [
            pl.pallas_call(
                functools.partial(pack_kernel, spread, here, sum(widths[:low]) // VOX_BLOCK, len(packed)),
                in_specs=[SMEM(), VMEM(), VMEM()] + [VMEM()] * len(args),
                out_specs=VMEM(),
                out_shape=jax.ShapeDtypeStruct((owners, time_block, send_cap), jnp.bfloat16),
                scratch_shapes=[pltpu.VMEM((time_block, sum(here)), jnp.bfloat16)],
                compiler_params=pltpu.CompilerParams(vmem_limit_bytes=12 * MIB),
                name="pack",
            )(starts, onehot, tiles, *args)
        ]
    received = lax.all_to_all(packed[0], "vox", split_axis=0, concat_axis=0, tiled=True)
    return jnp.transpose(received, (0, 2, 1))


def solution(mesh):
    return jax.shard_map(
        shards,
        mesh=mesh,
        in_specs=(P("chan", None), P(None, "chan", None), P(None, "chan", "vox"), P("vox"), P()),
        out_specs=P("vox", None, "chan"),
        check_vma=False,
    )
```

```python
import functools

import jax
import jax.numpy as jnp
from jax import lax
from jax.experimental import pallas as pl
from jax.experimental.pallas import tpu as pltpu
from jax.sharding import PartitionSpec as P

FILTER_TAPS = 16
TAP_SPACING = 2
LANES = 128
SLOT_TILE = 128
VOX_BLOCK = 256
COLUMNS = 512
ROWS = 32
CHUNKS = 5
COPIES = (((0, 2), (1, 4), (2, 3)), ((2, 2), (3, 2)), ((3, 1),), ((3, 2), (4, 1)), ((4, 3),))
PACK_FIRST = 4
MIB = 1 << 20

VMEM = functools.partial(pl.BlockSpec, memory_space=pltpu.VMEM)
SMEM = functools.partial(pl.BlockSpec, memory_space=pltpu.SMEM)
ANY = functools.partial(pl.BlockSpec, memory_space=pl.ANY)
HBM = functools.partial(pl.BlockSpec, memory_space=pltpu.HBM)


def copy_pieces(weight_ref, piece_refs, sems, first):
    depth, copies = weight_ref.shape[1], []
    for i, ref in enumerate(piece_refs):
        if ref.shape[1] > depth:
            ref[:, depth:, :] = jnp.zeros_like(ref[:, depth:, :])
        copy = pltpu.make_async_copy(
            weight_ref.at[:, :, pl.ds(first, ref.shape[2])], ref.at[:, pl.ds(0, depth), :], sems.at[i]
        )
        copy.start()
        copies.append(copy)
        first += ref.shape[2]
    return copies


def wait_all(copies):
    for copy in copies:
        copy.wait()


def cost(flops, read):
    return pl.CostEstimate(flops=flops, bytes_accessed=read, transcendentals=0)


def places(owners, spread, parcel_ref, table_ref, onehot_ref, tile_ref, start_ref):
    rows = parcel_ref.shape[0]
    parcel = parcel_ref[...]
    high, low = parcel >> 7, parcel & 127
    owner = jnp.zeros_like(parcel)
    for entry in range(table_ref.shape[0]):
        line = jnp.broadcast_to(table_ref[entry : entry + 1, :], parcel.shape)
        found = jnp.take_along_axis(line, low, axis=1, mode="promise_in_bounds")
        owner = jnp.where(high == entry, found, owner)

    def below(shape, scale=1):
        less = lax.broadcasted_iota(jnp.int32, shape, 1) < scale * lax.broadcasted_iota(jnp.int32, shape, 0)
        return less.astype(jnp.float32).astype(jnp.bfloat16)

    lane = lax.broadcasted_iota(jnp.int32, (LANES, LANES), 1)
    above = (lax.broadcasted_iota(jnp.int32, (LANES, LANES), 0) < lane).astype(jnp.float32).astype(jnp.bfloat16)
    ones = jnp.ones((LANES, LANES), jnp.bfloat16)
    marks = start_ref.shape[0]
    ahead, block_ahead = below((rows, rows)), below((marks, rows), VOX_BLOCK // LANES)
    mark_lane = lax.broadcasted_iota(jnp.int32, (marks, LANES), 1)
    dot = functools.partial(jnp.dot, preferred_element_type=jnp.float32)
    slots = jnp.zeros(parcel.shape, jnp.float32)
    starts = jnp.zeros((marks, LANES), jnp.float32)
    for o in range(owners):
        mine = owner == o
        hot = mine.astype(jnp.float32).astype(jnp.bfloat16)
        totals = dot(hot, ones).astype(jnp.bfloat16)
        slots = jnp.where(mine, dot(hot, above) + dot(ahead, totals), slots)
        starts = jnp.where(mark_lane == o, dot(block_ahead, totals), starts)
    slots = slots.astype(jnp.int32)
    start_ref[...] = starts.astype(jnp.int32)
    tile_ref[...] = owner * spread + (slots >> 7)
    inner = slots & 127
    for row in range(rows):
        line = jnp.broadcast_to(inner[row : row + 1, :], (LANES, LANES))
        hit = jnp.where(line.T == lane, 1.0, 0.0)
        onehot_ref[row * LANES : (row + 1) * LANES, :] = hit.astype(jnp.bfloat16)


def clear_lead(shifted):
    lead = TAP_SPACING * FILTER_TAPS
    for s in range(shifted.shape[0]):
        shifted[s, : lead + 8, :] = jnp.zeros((lead + 8, LANES), jnp.float32)


def shift(plain, shifted):
    lead, time_len = TAP_SPACING * FILTER_TAPS, plain.shape[0]
    series = plain[...]
    for s in range(shifted.shape[0]):
        shifted[s, lead + s * TAP_SPACING : lead + s * TAP_SPACING + time_len, :] = series


def filter_rows(shifted, filter_ref, column, first):
    lead = TAP_SPACING * FILTER_TAPS
    sums = [jnp.zeros((ROWS, LANES), jnp.float32) for _ in range(filter_ref.shape[0])]
    for tap in range(FILTER_TAPS):
        delay = tap * TAP_SPACING
        start = lead + first - 8 * (delay // 8)
        if not isinstance(start, int):
            start = pl.multiple_of(start, 8)
        lagged = shifted[(delay % 8) // TAP_SPACING, pl.ds(start, ROWS), :]
        for b in range(len(sums)):
            sums[b] = sums[b] + filter_ref[b, tap : tap + 1, column] * lagged
    return sums


def lane_tile(tile):
    return pl.ds(pl.multiple_of(tile * LANES, LANES), LANES)


def early_kernel(owners, spread, order_ref, own_ref, pair_ref, parcel_hbm, table_ref, filter_hbm, weight_ref, *refs):
    onehot_ref, tile_ref, start_ref, design_ref, *piece_refs, plain, shifted, filter_ref, parcel_ref, sems = refs
    count = len(piece_refs)
    load_filter = pltpu.make_async_copy(filter_hbm, filter_ref, sems.at[count])
    load_parcel = pltpu.make_async_copy(parcel_hbm, parcel_ref, sems.at[count + 1])
    load_filter.start()
    load_parcel.start()
    copies = copy_pieces(weight_ref, piece_refs, sems, 0)
    block, width = own_ref.shape
    core = lax.rem(order_ref[0], 2)
    own = pl.ds(pl.multiple_of(core * block, block), block)
    pair = pl.ds(pl.multiple_of((1 - core) * block, block), block)
    clear_lead(shifted)
    load_filter.wait()

    def columns(tile, carry):
        column = lane_tile(tile)
        plain[own, :] = own_ref[:, column].astype(jnp.float32)
        plain[pair, :] = pair_ref[:, column].astype(jnp.float32)
        shift(plain, shifted)
        for first in range(ROWS, 2 * block, ROWS):
            for b, rows in enumerate(filter_rows(shifted, filter_ref, column, first)):
                lanes = pl.ds(pl.multiple_of(b * width + tile * LANES, LANES), LANES)
                design_ref[first - ROWS : first, lanes] = rows.astype(jnp.bfloat16)
        return carry

    lax.fori_loop(0, width // LANES, columns, 0)
    load_parcel.wait()
    places(owners, spread, parcel_ref, table_ref, onehot_ref, tile_ref, start_ref)
    wait_all(copies)


def design_kernel(parts, first, order_ref, place_ref, early_ref, filter_ref, weight_ref, *refs):
    series_refs, (design_ref, *piece_refs, plain, shifted, sems) = refs[:parts], refs[parts:]
    copies = copy_pieces(weight_ref, piece_refs, sems, first)
    block, width = series_refs[0].shape
    chip = order_ref[0] >> 1
    clear_lead(shifted)

    def place(part, inner):
        return pl.ds(pl.multiple_of(place_ref[part] * block + inner, ROWS), ROWS)

    for first in range(ROWS, 2 * block, ROWS):
        row = place(2 * chip + first // block, first % block)
        design_ref[row, :] = early_ref[first - ROWS : first, :]

    def columns(tile, carry):
        column = lane_tile(tile)
        for d in range(parts):
            row = pl.ds(pl.multiple_of(order_ref[d] * block, block), block)
            plain[row, :] = series_refs[d][:, column].astype(jnp.float32)
        shift(plain, shifted)
        for other in range(parts // 2):
            for inner in range(0, 2 * block if other else ROWS, ROWS):
                part = 2 * (chip ^ other) + inner // block
                start = part * block + inner % block
                row = place(part, inner % block)
                for b, rows in enumerate(filter_rows(shifted, filter_ref, column, start)):
                    lanes = pl.ds(pl.multiple_of(b * width + tile * LANES, LANES), LANES)
                    design_ref[row, lanes] = rows.astype(jnp.bfloat16)
        return carry

    lax.fori_loop(0, width // LANES, columns, 0)
    wait_all(copies)


def filter_scratch(time_len):
    return [
        pltpu.VMEM((time_len, LANES), jnp.float32),
        pltpu.VMEM((8 // TAP_SPACING, time_len + TAP_SPACING * FILTER_TAPS + 8, LANES), jnp.float32),
    ]


def product_kernel(taken, extra, first, design_ref, *refs):
    weight_refs, refs = refs[:taken], refs[taken + extra :]
    copies = []
    if first is not None:
        weight_ref, keep_ref, send_ref, *piece_refs, sems = refs
        copies = copy_pieces(weight_ref, piece_refs, sems, first)
    else:
        keep_ref, send_ref = refs
    half, at = keep_ref.shape[0], 0
    for ref in weight_refs:
        for start in range(0, ref.shape[2], COLUMNS):
            weight = ref[:, :, start : min(start + COLUMNS, ref.shape[2])]
            weight = weight.reshape(-1, weight.shape[2])
            total = jnp.dot(design_ref[...], weight, preferred_element_type=jnp.float32)
            columns = slice(at, at + weight.shape[1])
            keep_ref[:, columns] = total[:half].astype(jnp.bfloat16)
            send_ref[:, columns] = total[half:].astype(jnp.bfloat16)
            at += weight.shape[1]
    wait_all(copies)


def product(design, taken, after, weights, first, ahead):
    time_len, lanes = design.shape
    width = sum(piece.shape[2] for piece in taken)
    half = jax.ShapeDtypeStruct((time_len // 2, width), jnp.bfloat16)
    return pl.pallas_call(
        functools.partial(product_kernel, len(taken), len(after), first if ahead else None),
        in_specs=[VMEM()] * (1 + len(taken)) + [ANY()] * (len(after) + bool(ahead)),
        out_specs=[VMEM()] * (2 + len(ahead)),
        out_shape=[half, half] + ahead,
        scratch_shapes=[pltpu.SemaphoreType.DMA((len(ahead),))] if ahead else [],
        compiler_params=pltpu.CompilerParams(vmem_limit_bytes=10 * MIB),
        cost_estimate=cost(2 * time_len * lanes * width, 2 * lanes * width),
        name="product",
    )(design, *taken, *after, *([weights] if ahead else []))


def pack_kernel(spread, widths, first, start_ref, onehot_ref, tile_ref, *refs):
    *terms, out_ref, summed, packed = refs
    owners, time_block = packed.shape[:2]
    if first:
        packed[...] = terms.pop(0)[...]
    else:
        packed[...] = jnp.zeros_like(packed)
    each, at = len(terms) // len(widths), 0
    for c, width in enumerate(widths):
        total = sum(term[:time_block, :].astype(jnp.float32) for term in terms[c * each : (c + 1) * each])
        summed[:, at : at + width] = total.astype(jnp.bfloat16)
        at += width
    step = VOX_BLOCK // LANES

    def moves(index, extras):
        block = first + index
        values = summed[:, pl.ds(pl.multiple_of(index * VOX_BLOCK, VOX_BLOCK), VOX_BLOCK)]
        onehot = onehot_ref[pl.ds(pl.multiple_of(block * VOX_BLOCK, VOX_BLOCK), VOX_BLOCK), :]
        tiles = jnp.concatenate([tile_ref[pl.ds(block * step + i, 1), :] for i in range(step)], axis=1)
        low = [start_ref[block, o] >> 7 for o in range(owners)]
        targets = [(o, low[o] + extra) for extra in extras for o in range(owners)]
        rows = []
        for owner, tile in targets:
            hit = jnp.where(tiles == owner * spread + tile, 1.0, 0.0)
            rows.append(values * hit.astype(jnp.bfloat16))
        moved = jnp.dot(jnp.concatenate(rows, axis=0), onehot, preferred_element_type=jnp.float32)
        moved = moved.astype(jnp.bfloat16)
        out = []
        for i, (owner, tile) in enumerate(targets):
            lanes = pl.ds(pl.multiple_of(tile * SLOT_TILE, SLOT_TILE), SLOT_TILE)
            out.append((owner, lanes, moved[i * time_block : (i + 1) * time_block]))
        high = [(start_ref[block + 1, o] - 1) >> 7 for o in range(owners)]
        return out, functools.reduce(jnp.maximum, [high[o] - low[o] for o in range(owners)])

    def add(targets):
        sums = [packed[owner, :, lanes] + moved for owner, lanes, moved in targets]
        for (owner, lanes, _), total in zip(targets, sums):
            packed[owner, :, lanes] = total

    def blocks(indices):
        found = [moves(index, range(2)) for index in indices]
        for targets, _ in found:
            add(targets)
        for index, (_, longest) in zip(indices, found):

            @pl.when(longest > 1)
            def _():
                add(moves(index, (2,))[0])

    count = sum(widths) // VOX_BLOCK

    def two(i, carry):
        blocks([2 * i, 2 * i + 1])
        return carry

    lax.fori_loop(0, count // 2, two, 0)
    if count % 2:
        blocks([count - 1])
    out_ref[...] = packed[:, :, : out_ref.shape[2]]


def shards(features, hrf_filters, weights, voxel_parcel, parcel_owner):
    owners, parts = lax.axis_size("vox"), lax.axis_size("chan")
    me = lax.axis_index("chan")
    voxels = voxel_parcel.shape[0]
    send_cap = 2 * voxels // owners
    bases, depth, _ = weights.shape
    blocks = voxels // VOX_BLOCK
    time_block = features.shape[0]
    time_len = time_block * parts

    series = [lax.dynamic_slice_in_dim(features, (me ^ d) * depth, depth, 1) for d in range(parts)]
    for d in range(1, parts):
        series[d] = lax.ppermute(series[d], "chan", [(i, i ^ d) for i in range(parts)])
    filters = jnp.transpose(hrf_filters, (0, 2, 1))
    spare = -depth % LANES
    lanes = bases * (depth + spare)
    unit = voxels // sum(units for pieces in COPIES for _, units in pieces)
    copied = [unit * sum(units for _, units in pieces) for pieces in COPIES]
    firsts = [sum(copied[:i]) for i in range(len(copied))]
    held = [[] for _ in range(CHUNKS)]

    def room(i):
        if i >= len(COPIES):
            return []
        return [pltpu.VMEM((bases, depth + spare, unit * units), jnp.bfloat16) for _, units in COPIES[i]]

    def keep_pieces(i, pieces):
        for (chunk, _), piece in zip(COPIES[i] if i < len(COPIES) else (), pieces):
            held[chunk].append(piece)

    if spare:
        series = [jnp.pad(part, ((0, 0), (0, spare))) for part in series]
        filters = jnp.pad(filters, ((0, 0), (0, 0), (0, spare)))

    table_rows = -(-parcel_owner.shape[0] // LANES)
    table = jnp.pad(parcel_owner, (0, table_rows * LANES - parcel_owner.shape[0])).reshape(table_rows, LANES)
    marks = -(-(blocks + 1) // 8) * 8
    spread = send_cap // SLOT_TILE + 3
    bits = parts.bit_length() - 1
    order = jnp.arange(parts, dtype=jnp.int32) ^ me
    place = sum(((order >> bit) & 1) << (bits - 1 - bit) for bit in range(bits)).astype(jnp.int32)

    early_rows = 2 * time_block - ROWS
    onehot, tiles, starts, early, *pieces = pl.pallas_call(
        functools.partial(early_kernel, owners, spread),
        in_specs=[SMEM(), VMEM(), VMEM(), HBM(), VMEM(), HBM(), ANY()],
        out_specs=[VMEM()] * (4 + len(COPIES[0])),
        out_shape=[
            jax.ShapeDtypeStruct((voxels, LANES), jnp.bfloat16),
            jax.ShapeDtypeStruct((voxels // LANES, LANES), jnp.int32),
            jax.ShapeDtypeStruct((marks, LANES), jnp.int32),
            jax.ShapeDtypeStruct((early_rows, lanes), jnp.bfloat16),
        ]
        + room(0),
        scratch_shapes=filter_scratch(2 * time_block)
        + [
            pltpu.VMEM(filters.shape, jnp.float32),
            pltpu.VMEM((voxels // LANES, LANES), jnp.int32),
            pltpu.SemaphoreType.DMA((len(COPIES[0]) + 2,)),
        ],
        compiler_params=pltpu.CompilerParams(vmem_limit_bytes=10 * MIB),
        cost_estimate=cost(0, 2 * bases * depth * copied[0]),
        name="early",
    )(
        order,
        series[0],
        series[1],
        pltpu.with_memory_space_constraint(voxel_parcel.reshape(-1, LANES), pltpu.HBM),
        table,
        pltpu.with_memory_space_constraint(filters, pltpu.HBM),
        weights,
    )
    keep_pieces(0, pieces)
    design, *pieces = pl.pallas_call(
        functools.partial(design_kernel, parts, firsts[1]),
        in_specs=[SMEM(), SMEM(), VMEM(), VMEM(), ANY()] + [VMEM()] * parts,
        out_specs=[VMEM()] * (1 + len(COPIES[1])),
        out_shape=[jax.ShapeDtypeStruct((time_len, lanes), jnp.bfloat16)] + room(1),
        scratch_shapes=filter_scratch(time_len) + [pltpu.SemaphoreType.DMA((len(COPIES[1]),))],
        compiler_params=pltpu.CompilerParams(vmem_limit_bytes=10 * MIB),
        cost_estimate=cost(0, 2 * bases * depth * copied[1]),
        name="design",
    )(order, place, early, filters, weights, *series)
    keep_pieces(1, pieces)

    widths, terms, sent, got = [], [], [], []
    for c in range(CHUNKS):
        after = sent[max(c - 2, 0) : max(c - 1, 0)] + got[max(c - 3, 0) : max(c - 2, 0)]
        ahead = room(c + 2)
        keep, send, *pieces = product(design, held[c], after, weights, firsts[c + 2] if ahead else 0, ahead)
        keep_pieces(c + 2, pieces)
        widths.append(keep.shape[1])
        own = [keep]
        for bit in range(bits):
            if bit > 0:
                rows = own[-1].shape[0] // 2
                send = sum(term[rows : 2 * rows].astype(jnp.float32) for term in own).astype(jnp.bfloat16)
                if bit == 1:
                    sent.append(send)
            own.append(lax.ppermute(send, "chan", [(i, i ^ (1 << bit)) for i in range(parts)]))
        terms.append(own)
        got.append(own[-1])

    packed = []
    for low, high in ((0, PACK_FIRST), (PACK_FIRST, CHUNKS)):
        args = packed + [term for own in terms[low:high] for term in own]
        here = widths[low:high]
        room_here = send_cap if high == CHUNKS else spread * SLOT_TILE
        packed = [
            pl.pallas_call(
                functools.partial(pack_kernel, spread, here, sum(widths[:low]) // VOX_BLOCK),
                in_specs=[SMEM(), VMEM(), VMEM()] + [VMEM()] * len(args),
                out_specs=VMEM(),
                out_shape=jax.ShapeDtypeStruct((owners, time_block, room_here), jnp.bfloat16),
                scratch_shapes=[
                    pltpu.VMEM((time_block, sum(here)), jnp.bfloat16),
                    pltpu.VMEM((owners, time_block, spread * SLOT_TILE), jnp.bfloat16),
                ],
                compiler_params=pltpu.CompilerParams(vmem_limit_bytes=14 * MIB),
                name="pack",
            )(starts, onehot, tiles, *args)
        ]
    received = lax.all_to_all(packed[0], "vox", split_axis=0, concat_axis=0, tiled=True)
    return jnp.transpose(received, (0, 2, 1))


def solution(mesh):
    return jax.shard_map(
        shards,
        mesh=mesh,
        in_specs=(P("chan", None), P(None, "chan", None), P(None, "chan", "vox"), P("vox"), P()),
        out_specs=P("vox", None, "chan"),
        check_vma=False,
    )
```

```python
import functools

import jax
import jax.numpy as jnp
from jax import lax
from jax.experimental import pallas as pl
from jax.experimental.pallas import tpu as pltpu
from jax.sharding import PartitionSpec as P

FILTER_TAPS = 16
TAP_SPACING = 2
LANES = 128
SLOT_TILE = 128
VOX_BLOCK = 256
COLUMNS = 512
ROWS = 32
CHUNKS = 4
COPIES = (((0, 5), (1, 4)), ((1, 2), (2, 2)), ((2, 2),), ((2, 2),), ((3, 3),))
PACK_FIRST = 3
MIB = 1 << 20

VMEM = functools.partial(pl.BlockSpec, memory_space=pltpu.VMEM)
SMEM = functools.partial(pl.BlockSpec, memory_space=pltpu.SMEM)
ANY = functools.partial(pl.BlockSpec, memory_space=pl.ANY)
HBM = functools.partial(pl.BlockSpec, memory_space=pltpu.HBM)


def copy_pieces(weight_ref, piece_refs, sems, first):
    depth, copies = weight_ref.shape[1], []
    for i, ref in enumerate(piece_refs):
        if ref.shape[1] > depth:
            ref[:, depth:, :] = jnp.zeros_like(ref[:, depth:, :])
        for b in range(ref.shape[0]):
            copy = pltpu.make_async_copy(
                weight_ref.at[b, :, pl.ds(first, ref.shape[2])], ref.at[b, pl.ds(0, depth), :], sems.at[i, b]
            )
            copy.start()
            copies.append(copy)
        first += ref.shape[2]
    return copies


def wait_all(copies):
    for copy in copies:
        copy.wait()


def cost(flops, read):
    return pl.CostEstimate(flops=flops, bytes_accessed=read, transcendentals=0)


def places(owners, spread, parcel_ref, table_ref, onehot_ref, tile_ref, start_ref):
    rows = parcel_ref.shape[0]
    parcel = parcel_ref[...]
    high, low = parcel >> 7, parcel & 127
    owner = jnp.zeros_like(parcel)
    for entry in range(table_ref.shape[0]):
        line = jnp.broadcast_to(table_ref[entry : entry + 1, :], parcel.shape)
        found = jnp.take_along_axis(line, low, axis=1, mode="promise_in_bounds")
        owner = jnp.where(high == entry, found, owner)

    def below(shape, scale=1):
        less = lax.broadcasted_iota(jnp.int32, shape, 1) < scale * lax.broadcasted_iota(jnp.int32, shape, 0)
        return less.astype(jnp.float32).astype(jnp.bfloat16)

    lane = lax.broadcasted_iota(jnp.int32, (LANES, LANES), 1)
    above = (lax.broadcasted_iota(jnp.int32, (LANES, LANES), 0) < lane).astype(jnp.float32).astype(jnp.bfloat16)
    ones = jnp.ones((LANES, LANES), jnp.bfloat16)
    marks = start_ref.shape[0]
    ahead, block_ahead = below((rows, rows)), below((marks, rows), VOX_BLOCK // LANES)
    mark_lane = lax.broadcasted_iota(jnp.int32, (marks, LANES), 1)
    dot = functools.partial(jnp.dot, preferred_element_type=jnp.float32)
    row_block = lax.broadcasted_iota(jnp.int32, (rows, rows), 0) & -(VOX_BLOCK // LANES)
    before = lax.broadcasted_iota(jnp.int32, (rows, rows), 1) < row_block
    before = before.astype(jnp.float32).astype(jnp.bfloat16)
    slots = jnp.zeros(parcel.shape, jnp.float32)
    bases = jnp.zeros(parcel.shape, jnp.float32)
    starts = jnp.zeros((marks, LANES), jnp.float32)
    for o in range(owners):
        mine = owner == o
        hot = mine.astype(jnp.float32).astype(jnp.bfloat16)
        totals = dot(hot, ones).astype(jnp.bfloat16)
        slots = jnp.where(mine, dot(hot, above) + dot(ahead, totals), slots)
        bases = jnp.where(mine, dot(before, totals), bases)
        starts = jnp.where(mark_lane == o, dot(block_ahead, totals), starts)
    slots = slots.astype(jnp.int32)
    start_ref[...] = starts.astype(jnp.int32)
    tile_ref[...] = owner * spread + (slots >> 7)
    inner = (slots - (bases.astype(jnp.int32) & -SLOT_TILE)) & (2 * SLOT_TILE - 1)
    for row in range(rows):
        line = jnp.broadcast_to(inner[row : row + 1, :], (LANES, LANES)).T
        for side in range(2):
            hit = jnp.where(line == lane + side * LANES, 1.0, 0.0)
            at = slice(side * LANES, (side + 1) * LANES)
            onehot_ref[row * LANES : (row + 1) * LANES, at] = hit.astype(jnp.bfloat16)


def clear_lead(shifted):
    lead = TAP_SPACING * FILTER_TAPS
    for s in range(shifted.shape[0]):
        shifted[s, : lead + 8, :] = jnp.zeros((lead + 8, LANES), jnp.float32)


def shift(plain, shifted):
    lead, time_len = TAP_SPACING * FILTER_TAPS, plain.shape[0]
    series = plain[...]
    for s in range(shifted.shape[0]):
        shifted[s, lead + s * TAP_SPACING : lead + s * TAP_SPACING + time_len, :] = series


def filter_rows(shifted, filter_ref, column, first):
    lead = TAP_SPACING * FILTER_TAPS
    sums = [jnp.zeros((ROWS, LANES), jnp.float32) for _ in range(filter_ref.shape[0])]
    for tap in range(FILTER_TAPS):
        delay = tap * TAP_SPACING
        start = lead + first - 8 * (delay // 8)
        if not isinstance(start, int):
            start = pl.multiple_of(start, 8)
        lagged = shifted[(delay % 8) // TAP_SPACING, pl.ds(start, ROWS), :]
        for b in range(len(sums)):
            sums[b] = sums[b] + filter_ref[b, tap : tap + 1, column] * lagged
    return sums


def lane_tile(tile):
    return pl.ds(pl.multiple_of(tile * LANES, LANES), LANES)


def early_kernel(owners, spread, order_ref, own_ref, pair_ref, parcel_hbm, table_ref, filter_hbm, weight_ref, *refs):
    onehot_ref, tile_ref, start_ref, design_ref, *piece_refs, plain, shifted, filter_ref, parcel_ref, sems, small_sems = refs
    load_filter = pltpu.make_async_copy(filter_hbm, filter_ref, small_sems.at[0])
    load_parcel = pltpu.make_async_copy(parcel_hbm, parcel_ref, small_sems.at[1])
    load_filter.start()
    load_parcel.start()
    copies = copy_pieces(weight_ref, piece_refs, sems, 0)
    block, width = own_ref.shape
    core = lax.rem(order_ref[0], 2)
    own = pl.ds(pl.multiple_of(core * block, block), block)
    pair = pl.ds(pl.multiple_of((1 - core) * block, block), block)
    clear_lead(shifted)
    load_filter.wait()

    def columns(tile, carry):
        column = lane_tile(tile)
        plain[own, :] = own_ref[:, column].astype(jnp.float32)
        plain[pair, :] = pair_ref[:, column].astype(jnp.float32)
        shift(plain, shifted)
        for first in range(ROWS, 2 * block, ROWS):
            for b, rows in enumerate(filter_rows(shifted, filter_ref, column, first)):
                lanes = pl.ds(pl.multiple_of(b * width + tile * LANES, LANES), LANES)
                design_ref[first - ROWS : first, lanes] = rows.astype(jnp.bfloat16)
        return carry

    lax.fori_loop(0, width // LANES, columns, 0)
    load_parcel.wait()
    places(owners, spread, parcel_ref, table_ref, onehot_ref, tile_ref, start_ref)
    wait_all(copies)


def design_kernel(parts, first, order_ref, place_ref, early_ref, filter_ref, weight_ref, *refs):
    series_refs, (design_ref, *piece_refs, plain, shifted, sems) = refs[:parts], refs[parts:]
    copies = copy_pieces(weight_ref, piece_refs, sems, first)
    block, width = series_refs[0].shape
    chip = order_ref[0] >> 1
    clear_lead(shifted)

    def place(part, inner):
        return pl.ds(pl.multiple_of(place_ref[part] * block + inner, ROWS), ROWS)

    for first in range(ROWS, 2 * block, ROWS):
        row = place(2 * chip + first // block, first % block)
        design_ref[row, :] = early_ref[first - ROWS : first, :]

    def columns(tile, carry):
        column = lane_tile(tile)
        for d in range(parts):
            row = pl.ds(pl.multiple_of(order_ref[d] * block, block), block)
            plain[row, :] = series_refs[d][:, column].astype(jnp.float32)
        shift(plain, shifted)
        for other in range(parts // 2):
            for inner in range(0, 2 * block if other else ROWS, ROWS):
                part = 2 * (chip ^ other) + inner // block
                start = part * block + inner % block
                row = place(part, inner % block)
                for b, rows in enumerate(filter_rows(shifted, filter_ref, column, start)):
                    lanes = pl.ds(pl.multiple_of(b * width + tile * LANES, LANES), LANES)
                    design_ref[row, lanes] = rows.astype(jnp.bfloat16)
        return carry

    lax.fori_loop(0, width // LANES, columns, 0)
    wait_all(copies)


def filter_scratch(time_len):
    return [
        pltpu.VMEM((time_len, LANES), jnp.float32),
        pltpu.VMEM((8 // TAP_SPACING, time_len + TAP_SPACING * FILTER_TAPS + 8, LANES), jnp.float32),
    ]


def product_kernel(taken, extra, first, design_ref, *refs):
    weight_refs, refs = refs[:taken], refs[taken + extra :]
    copies = []
    if first is not None:
        weight_ref, keep_ref, send_ref, *piece_refs, sems = refs
        copies = copy_pieces(weight_ref, piece_refs, sems, first)
    else:
        keep_ref, send_ref = refs
    half, at = keep_ref.shape[0], 0
    for ref in weight_refs:
        for start in range(0, ref.shape[2], COLUMNS):
            weight = ref[:, :, start : min(start + COLUMNS, ref.shape[2])]
            weight = weight.reshape(-1, weight.shape[2])
            total = jnp.dot(design_ref[...], weight, preferred_element_type=jnp.float32)
            columns = slice(at, at + weight.shape[1])
            keep_ref[:, columns] = total[:half].astype(jnp.bfloat16)
            send_ref[:, columns] = total[half:].astype(jnp.bfloat16)
            at += weight.shape[1]
    wait_all(copies)


def product(design, taken, after, weights, first, ahead):
    time_len, lanes = design.shape
    width = sum(piece.shape[2] for piece in taken)
    half = jax.ShapeDtypeStruct((time_len // 2, width), jnp.bfloat16)
    return pl.pallas_call(
        functools.partial(product_kernel, len(taken), len(after), first if ahead else None),
        in_specs=[VMEM()] * (1 + len(taken)) + [ANY()] * (len(after) + bool(ahead)),
        out_specs=[VMEM()] * (2 + len(ahead)),
        out_shape=[half, half] + ahead,
        scratch_shapes=[pltpu.SemaphoreType.DMA((len(ahead), weights.shape[0]))] if ahead else [],
        compiler_params=pltpu.CompilerParams(vmem_limit_bytes=8 * MIB),
        cost_estimate=cost(2 * time_len * lanes * width, 2 * lanes * width),
        name="product",
    )(design, *taken, *after, *([weights] if ahead else []))


def late_kernel(each, first, *refs):
    out_ref, at = refs[-1], 0
    for c in range(0, len(refs) - 3, each):
        terms, width = refs[c : c + each], refs[c].shape[1]
        total = sum(term[first : first + out_ref.shape[0], :].astype(jnp.float32) for term in terms)
        out_ref[:, at : at + width] = total.astype(jnp.bfloat16)
        at += width


def pack_kernel(spread, widths, places, first, extra, start_ref, onehot_ref, tile_ref, *refs):
    *terms, out_ref, summed, packed = refs
    terms = terms[: len(terms) - extra]
    owners, rows = packed.shape[:2]
    if first:
        packed[...] = terms.pop(0)[...]
    else:
        packed[...] = jnp.zeros_like(packed)
    at = 0
    for width, spots in zip(widths, places):
        total = 0.0
        for row, column in spots:
            total = total + terms.pop(0)[row : row + rows, column : column + width].astype(jnp.float32)
        summed[:, at : at + width] = total.astype(jnp.bfloat16)
        at += width
    step = VOX_BLOCK // LANES

    def moves(index, far):
        block = first + index
        values = summed[:, pl.ds(pl.multiple_of(index * VOX_BLOCK, VOX_BLOCK), VOX_BLOCK)]
        onehot = onehot_ref[pl.ds(pl.multiple_of(block * VOX_BLOCK, VOX_BLOCK), VOX_BLOCK), :]
        tiles = jnp.concatenate([tile_ref[pl.ds(block * step + i, 1), :] for i in range(step)], axis=1)
        low = [start_ref[block, o] >> 7 for o in range(owners)]
        chosen = []
        for o in range(owners):
            tile = tiles - (o * spread + low[o])
            hit = jnp.where((tile == 2) if far else ((tile == 0) | (tile == 1)), 1.0, 0.0)
            chosen.append(values * hit.astype(jnp.bfloat16))
        moved = jnp.dot(jnp.concatenate(chosen, axis=0), onehot, preferred_element_type=jnp.float32)
        moved = moved.astype(jnp.bfloat16)
        out = []
        for o in range(owners):
            here = moved[o * rows : (o + 1) * rows]
            tile, here = (low[o] + 2, here[:, :SLOT_TILE]) if far else (low[o], here)
            lanes = pl.ds(pl.multiple_of(tile * SLOT_TILE, SLOT_TILE), here.shape[1])
            out.append((o, lanes, here))
        high = [(start_ref[block + 1, o] - 1) >> 7 for o in range(owners)]
        return out, functools.reduce(jnp.maximum, [high[o] - low[o] for o in range(owners)])

    def add(targets):
        sums = [packed[owner, :, lanes] + moved for owner, lanes, moved in targets]
        for (owner, lanes, _), total in zip(targets, sums):
            packed[owner, :, lanes] = total

    def blocks(indices):
        found = [moves(index, False) for index in indices]
        for targets, _ in found:
            add(targets)
        for index, (_, longest) in zip(indices, found):

            @pl.when(longest > 1)
            def _():
                add(moves(index, True)[0])

    count = sum(widths) // VOX_BLOCK

    def two(i, carry):
        blocks([2 * i, 2 * i + 1])
        return carry

    lax.fori_loop(0, count // 2, two, 0)
    if count % 2:
        blocks([count - 1])
    out_ref[...] = packed[:, :, : out_ref.shape[2]]


def shards(features, hrf_filters, weights, voxel_parcel, parcel_owner):
    owners, parts = lax.axis_size("vox"), lax.axis_size("chan")
    me = lax.axis_index("chan")
    voxels = voxel_parcel.shape[0]
    send_cap = 2 * voxels // owners
    bases, depth, _ = weights.shape
    blocks = voxels // VOX_BLOCK
    time_block = features.shape[0]
    time_len = time_block * parts

    series = [lax.dynamic_slice_in_dim(features, (me ^ d) * depth, depth, 1) for d in range(parts)]
    for d in range(1, parts):
        series[d] = lax.ppermute(series[d], "chan", [(i, i ^ d) for i in range(parts)])
    filters = jnp.transpose(hrf_filters, (0, 2, 1))
    spare = -depth % LANES
    lanes = bases * (depth + spare)
    unit = voxels // sum(units for pieces in COPIES for _, units in pieces)
    copied = [unit * sum(units for _, units in pieces) for pieces in COPIES]
    firsts = [sum(copied[:i]) for i in range(len(copied))]
    held = [[] for _ in range(CHUNKS)]

    def room(i):
        if i >= len(COPIES):
            return []
        return [pltpu.VMEM((bases, depth + spare, unit * units), jnp.bfloat16) for _, units in COPIES[i]]

    def keep_pieces(i, pieces):
        for (chunk, _), piece in zip(COPIES[i] if i < len(COPIES) else (), pieces):
            held[chunk].append(piece)

    if spare:
        series = [jnp.pad(part, ((0, 0), (0, spare))) for part in series]
        filters = jnp.pad(filters, ((0, 0), (0, 0), (0, spare)))

    table_rows = -(-parcel_owner.shape[0] // LANES)
    table = jnp.pad(parcel_owner, (0, table_rows * LANES - parcel_owner.shape[0])).reshape(table_rows, LANES)
    marks = -(-(blocks + 1) // 8) * 8
    spread = send_cap // SLOT_TILE + 3
    bits = parts.bit_length() - 1
    order = jnp.arange(parts, dtype=jnp.int32) ^ me
    place = sum(((order >> bit) & 1) << (bits - 1 - bit) for bit in range(bits)).astype(jnp.int32)

    early_rows = 2 * time_block - ROWS
    onehot, tiles, starts, early, *pieces = pl.pallas_call(
        functools.partial(early_kernel, owners, spread),
        in_specs=[SMEM(), VMEM(), VMEM(), HBM(), VMEM(), HBM(), ANY()],
        out_specs=[VMEM()] * (4 + len(COPIES[0])),
        out_shape=[
            jax.ShapeDtypeStruct((voxels, 2 * SLOT_TILE), jnp.bfloat16),
            jax.ShapeDtypeStruct((voxels // LANES, LANES), jnp.int32),
            jax.ShapeDtypeStruct((marks, LANES), jnp.int32),
            jax.ShapeDtypeStruct((early_rows, lanes), jnp.bfloat16),
        ]
        + room(0),
        scratch_shapes=filter_scratch(2 * time_block)
        + [
            pltpu.VMEM(filters.shape, jnp.float32),
            pltpu.VMEM((voxels // LANES, LANES), jnp.int32),
            pltpu.SemaphoreType.DMA((len(COPIES[0]), bases)),
            pltpu.SemaphoreType.DMA((2,)),
        ],
        compiler_params=pltpu.CompilerParams(vmem_limit_bytes=8 * MIB),
        cost_estimate=cost(0, 2 * bases * depth * copied[0]),
        name="early",
    )(
        order,
        series[0],
        series[1],
        pltpu.with_memory_space_constraint(voxel_parcel.reshape(-1, LANES), pltpu.HBM),
        table,
        pltpu.with_memory_space_constraint(filters, pltpu.HBM),
        weights,
    )
    keep_pieces(0, pieces)
    design, *pieces = pl.pallas_call(
        functools.partial(design_kernel, parts, firsts[1]),
        in_specs=[SMEM(), SMEM(), VMEM(), VMEM(), ANY()] + [VMEM()] * parts,
        out_specs=[VMEM()] * (1 + len(COPIES[1])),
        out_shape=[jax.ShapeDtypeStruct((time_len, lanes), jnp.bfloat16)] + room(1),
        scratch_shapes=filter_scratch(time_len) + [pltpu.SemaphoreType.DMA((len(COPIES[1]), bases))],
        compiler_params=pltpu.CompilerParams(vmem_limit_bytes=8 * MIB),
        cost_estimate=cost(0, 2 * bases * depth * copied[1]),
        name="design",
    )(order, place, early, filters, weights, *series)
    keep_pieces(1, pieces)

    half = time_block // 2
    widths, sums, sent, got = [], [], [], []
    for c in range(CHUNKS):
        after = sent[max(c - 2, 0) : max(c - 1, 0)] + got[max(c - 3, 0) : max(c - 2, 0)]
        ahead = room(c + 2)
        keep, send, *pieces = product(design, held[c], after, weights, firsts[c + 2] if ahead else 0, ahead)
        keep_pieces(c + 2, pieces)
        widths.append(keep.shape[1])
        own = [keep]
        for bit in range(bits):
            if bit > 0:
                rows = own[-1].shape[0] // 2
                send = added(own, rows, half if bit == bits - 1 else rows)
                if bit == bits - 1:
                    sent.append(send)
            own.append(lax.ppermute(send, "chan", [(i, i ^ (1 << bit)) for i in range(parts)]))
        sums.append(own)
        got.append(own[-1])
    def pack(low, high, second, packed, after=()):
        terms, spots = [], []
        for c in range(low, high):
            own = sums[c][:-1]
            terms += own + [late if second else got[c]]
            spots.append([(half if second else 0, 0)] * len(own) + [(0, sum(widths[:c]) if second else 0)])
        here = widths[low:high]
        lanes_out = send_cap if high == CHUNKS else spread * SLOT_TILE
        return pl.pallas_call(
            functools.partial(pack_kernel, spread, here, spots, sum(widths[:low]) // VOX_BLOCK, len(after)),
            in_specs=[SMEM(), VMEM(), VMEM()] + [VMEM()] * (len(packed) + len(terms)) + [ANY()] * len(after),
            out_specs=VMEM(),
            out_shape=jax.ShapeDtypeStruct((owners, half, lanes_out), jnp.bfloat16),
            scratch_shapes=[
                pltpu.VMEM((half, sum(here)), jnp.bfloat16),
                pltpu.VMEM((owners, half, spread * SLOT_TILE), jnp.bfloat16),
            ],
            compiler_params=pltpu.CompilerParams(vmem_limit_bytes=8 * MIB),
            cost_estimate=cost(2 * half * owners * VOX_BLOCK * sum(here), 4 * half * sum(here)),
            name="pack",
        )(starts, onehot, tiles, *packed, *terms, *after)

    def deliver(packed):
        return lax.all_to_all(packed, "vox", split_axis=0, concat_axis=0, tiled=True)

    packed = pack(0, PACK_FIRST, False, [])
    late_terms = [term for own in sums for term in own[:-1]]
    late_send = pl.pallas_call(
        functools.partial(late_kernel, bits, time_block + half),
        in_specs=[VMEM()] * len(late_terms) + [ANY()] * 2,
        out_specs=VMEM(),
        out_shape=jax.ShapeDtypeStruct((half, voxels), jnp.bfloat16),
        compiler_params=pltpu.CompilerParams(vmem_limit_bytes=6 * MIB),
        name="late",
    )(*late_terms, got[-1], packed)
    late = lax.ppermute(late_send, "chan", [(i, i ^ (1 << (bits - 1))) for i in range(parts)])
    one = deliver(pack(PACK_FIRST, CHUNKS, False, [packed], [late_send]))
    two = deliver(pack(0, CHUNKS, True, []))
    return jnp.transpose(jnp.concatenate([one, two], axis=1), (0, 2, 1))


def added(terms, first, rows):
    return sum(term[first : first + rows].astype(jnp.float32) for term in terms).astype(jnp.bfloat16)


def solution(mesh):
    return jax.shard_map(
        shards,
        mesh=mesh,
        in_specs=(P("chan", None), P(None, "chan", None), P(None, "chan", "vox"), P("vox"), P()),
        out_specs=P("vox", None, "chan"),
        check_vma=False,
    )
```

```python
import functools

import jax
import jax.numpy as jnp
from jax import lax
from jax.experimental import pallas as pl
from jax.experimental.pallas import tpu as pltpu
from jax.sharding import PartitionSpec as P

FILTER_TAPS = 16
TAP_SPACING = 2
LANES = 128
SLOT_TILE = 128
VOX_BLOCK = 256
COLUMNS = 512
ROWS = 32
CHUNKS = 4
COPIES = (((0, 5), (1, 4)), ((1, 2), (2, 2)), ((2, 2),), ((2, 2),), ((3, 3),))
PACK_FIRST = 2
MIB = 1 << 20

VMEM = functools.partial(pl.BlockSpec, memory_space=pltpu.VMEM)
SMEM = functools.partial(pl.BlockSpec, memory_space=pltpu.SMEM)
ANY = functools.partial(pl.BlockSpec, memory_space=pl.ANY)
HBM = functools.partial(pl.BlockSpec, memory_space=pltpu.HBM)


def copy_pieces(weight_ref, piece_refs, sems, first):
    depth, copies = weight_ref.shape[1], []
    for i, ref in enumerate(piece_refs):
        if ref.shape[1] > depth:
            ref[:, depth:, :] = jnp.zeros_like(ref[:, depth:, :])
        for j, at in enumerate(range(0, ref.shape[2], COLUMNS)):
            size = min(COLUMNS, ref.shape[2] - at)
            copy = pltpu.make_async_copy(
                weight_ref.at[:, :, pl.ds(first + at, size)],
                ref.at[:, pl.ds(0, depth), pl.ds(at, size)],
                sems.at[i, j],
            )
            copy.start()
            copies.append(copy)
        first += ref.shape[2]
    return copies


def wait_all(copies):
    for copy in copies:
        copy.wait()


def cost(flops, read):
    return pl.CostEstimate(flops=flops, bytes_accessed=read, transcendentals=0)


def places(owners, spread, parcel_ref, table_ref, onehot_ref, tile_ref, start_ref):
    rows = parcel_ref.shape[0]
    parcel = parcel_ref[...]
    high, low = parcel >> 7, parcel & 127
    owner = jnp.zeros_like(parcel)
    for entry in range(table_ref.shape[0]):
        line = jnp.broadcast_to(table_ref[entry : entry + 1, :], parcel.shape)
        found = jnp.take_along_axis(line, low, axis=1, mode="promise_in_bounds")
        owner = jnp.where(high == entry, found, owner)

    def below(shape, scale=1):
        less = lax.broadcasted_iota(jnp.int32, shape, 1) < scale * lax.broadcasted_iota(jnp.int32, shape, 0)
        return less.astype(jnp.float32).astype(jnp.bfloat16)

    lane = lax.broadcasted_iota(jnp.int32, (LANES, LANES), 1)
    above = (lax.broadcasted_iota(jnp.int32, (LANES, LANES), 0) < lane).astype(jnp.float32).astype(jnp.bfloat16)
    ones = jnp.ones((LANES, LANES), jnp.bfloat16)
    marks = start_ref.shape[0]
    ahead, block_ahead = below((rows, rows)), below((marks, rows), VOX_BLOCK // LANES)
    mark_lane = lax.broadcasted_iota(jnp.int32, (marks, LANES), 1)
    dot = functools.partial(jnp.dot, preferred_element_type=jnp.float32)
    row_block = lax.broadcasted_iota(jnp.int32, (rows, rows), 0) & -(VOX_BLOCK // LANES)
    before = lax.broadcasted_iota(jnp.int32, (rows, rows), 1) < row_block
    before = before.astype(jnp.float32).astype(jnp.bfloat16)
    slots = jnp.zeros(parcel.shape, jnp.float32)
    bases = jnp.zeros(parcel.shape, jnp.float32)
    starts = jnp.zeros((marks, LANES), jnp.float32)
    for o in range(owners):
        mine = owner == o
        hot = mine.astype(jnp.float32).astype(jnp.bfloat16)
        totals = dot(hot, ones).astype(jnp.bfloat16)
        slots = jnp.where(mine, dot(hot, above) + dot(ahead, totals), slots)
        bases = jnp.where(mine, dot(before, totals), bases)
        starts = jnp.where(mark_lane == o, dot(block_ahead, totals), starts)
    slots = slots.astype(jnp.int32)
    start_ref[...] = starts.astype(jnp.int32)
    tile_ref[...] = owner * spread + (slots >> 7)
    inner = (slots - (bases.astype(jnp.int32) & -SLOT_TILE)) & (2 * SLOT_TILE - 1)
    for row in range(rows):
        line = jnp.broadcast_to(inner[row : row + 1, :], (LANES, LANES)).T
        for side in range(2):
            hit = jnp.where(line == lane + side * LANES, 1.0, 0.0)
            at = slice(side * LANES, (side + 1) * LANES)
            onehot_ref[row * LANES : (row + 1) * LANES, at] = hit.astype(jnp.bfloat16)


def clear_lead(shifted):
    lead = TAP_SPACING * FILTER_TAPS
    for s in range(shifted.shape[0]):
        shifted[s, : lead + 8, :] = jnp.zeros((lead + 8, LANES), jnp.float32)


def shift(plain, shifted):
    lead, time_len = TAP_SPACING * FILTER_TAPS, plain.shape[0]
    series = plain[...]
    for s in range(shifted.shape[0]):
        shifted[s, lead + s * TAP_SPACING : lead + s * TAP_SPACING + time_len, :] = series


def filter_rows(shifted, filter_ref, column, first):
    lead = TAP_SPACING * FILTER_TAPS
    sums = [jnp.zeros((ROWS, LANES), jnp.float32) for _ in range(filter_ref.shape[0])]
    for tap in range(FILTER_TAPS):
        delay = tap * TAP_SPACING
        start = lead + first - 8 * (delay // 8)
        if not isinstance(start, int):
            start = pl.multiple_of(start, 8)
        lagged = shifted[(delay % 8) // TAP_SPACING, pl.ds(start, ROWS), :]
        for b in range(len(sums)):
            sums[b] = sums[b] + filter_ref[b, tap : tap + 1, column] * lagged
    return sums


def lane_tile(tile):
    return pl.ds(pl.multiple_of(tile * LANES, LANES), LANES)


def early_kernel(owners, spread, order_ref, own_ref, pair_ref, parcel_hbm, table_ref, filter_hbm, weight_ref, *refs):
    onehot_ref, tile_ref, start_ref, design_ref, *piece_refs, plain, shifted, filter_ref, parcel_ref, sems, small_sems = refs
    load_filter = pltpu.make_async_copy(filter_hbm, filter_ref, small_sems.at[0])
    load_parcel = pltpu.make_async_copy(parcel_hbm, parcel_ref, small_sems.at[1])
    load_filter.start()
    load_parcel.start()
    copies = copy_pieces(weight_ref, piece_refs, sems, 0)
    block, width = own_ref.shape
    core = lax.rem(order_ref[0], 2)
    own = pl.ds(pl.multiple_of(core * block, block), block)
    pair = pl.ds(pl.multiple_of((1 - core) * block, block), block)
    clear_lead(shifted)
    load_filter.wait()

    def columns(tile, carry):
        column = lane_tile(tile)
        plain[own, :] = own_ref[:, column].astype(jnp.float32)
        plain[pair, :] = pair_ref[:, column].astype(jnp.float32)
        shift(plain, shifted)
        for first in range(ROWS, 2 * block, ROWS):
            for b, rows in enumerate(filter_rows(shifted, filter_ref, column, first)):
                lanes = pl.ds(pl.multiple_of(b * width + tile * LANES, LANES), LANES)
                design_ref[first - ROWS : first, lanes] = rows.astype(jnp.bfloat16)
        return carry

    lax.fori_loop(0, width // LANES, columns, 0)
    load_parcel.wait()
    places(owners, spread, parcel_ref, table_ref, onehot_ref, tile_ref, start_ref)
    wait_all(copies)


def design_kernel(parts, first, order_ref, place_ref, early_ref, filter_ref, weight_ref, *refs):
    series_refs, (design_ref, *piece_refs, plain, shifted, sems) = refs[:parts], refs[parts:]
    copies = copy_pieces(weight_ref, piece_refs, sems, first)
    block, width = series_refs[0].shape
    chip = order_ref[0] >> 1
    clear_lead(shifted)

    def place(part, inner):
        return pl.ds(pl.multiple_of(place_ref[part] * block + inner, ROWS), ROWS)

    for first in range(ROWS, 2 * block, ROWS):
        row = place(2 * chip + first // block, first % block)
        design_ref[row, :] = early_ref[first - ROWS : first, :]

    def columns(tile, carry):
        column = lane_tile(tile)
        for d in range(parts):
            row = pl.ds(pl.multiple_of(order_ref[d] * block, block), block)
            plain[row, :] = series_refs[d][:, column].astype(jnp.float32)
        shift(plain, shifted)
        for other in range(parts // 2):
            for inner in range(0, 2 * block if other else ROWS, ROWS):
                part = 2 * (chip ^ other) + inner // block
                start = part * block + inner % block
                row = place(part, inner % block)
                for b, rows in enumerate(filter_rows(shifted, filter_ref, column, start)):
                    lanes = pl.ds(pl.multiple_of(b * width + tile * LANES, LANES), LANES)
                    design_ref[row, lanes] = rows.astype(jnp.bfloat16)
        return carry

    lax.fori_loop(0, width // LANES, columns, 0)
    wait_all(copies)


def filter_scratch(time_len):
    return [
        pltpu.VMEM((time_len, LANES), jnp.float32),
        pltpu.VMEM((8 // TAP_SPACING, time_len + TAP_SPACING * FILTER_TAPS + 8, LANES), jnp.float32),
    ]


def product_kernel(taken, extra, first, design_ref, *refs):
    weight_refs, refs = refs[:taken], refs[taken + extra :]
    copies = []
    if first is not None:
        weight_ref, keep_ref, send_ref, *piece_refs, sems = refs
        copies = copy_pieces(weight_ref, piece_refs, sems, first)
    else:
        keep_ref, send_ref = refs
    half, at = keep_ref.shape[0], 0
    for ref in weight_refs:
        for start in range(0, ref.shape[2], COLUMNS):
            weight = ref[:, :, start : min(start + COLUMNS, ref.shape[2])]
            weight = weight.reshape(-1, weight.shape[2])
            total = jnp.dot(design_ref[...], weight, preferred_element_type=jnp.float32)
            columns = slice(at, at + weight.shape[1])
            keep_ref[:, columns] = total[:half].astype(jnp.bfloat16)
            send_ref[:, columns] = total[half:].astype(jnp.bfloat16)
            at += weight.shape[1]
    wait_all(copies)


def product(design, taken, after, weights, first, ahead):
    time_len, lanes = design.shape
    width = sum(piece.shape[2] for piece in taken)
    half = jax.ShapeDtypeStruct((time_len // 2, width), jnp.bfloat16)
    return pl.pallas_call(
        functools.partial(product_kernel, len(taken), len(after), first if ahead else None),
        in_specs=[VMEM()] * (1 + len(taken)) + [ANY()] * (len(after) + bool(ahead)),
        out_specs=[VMEM()] * (2 + len(ahead)),
        out_shape=[half, half] + ahead,
        scratch_shapes=[pltpu.SemaphoreType.DMA((len(ahead), 4))] if ahead else [],
        compiler_params=pltpu.CompilerParams(vmem_limit_bytes=8 * MIB),
        cost_estimate=cost(2 * time_len * lanes * width, 2 * lanes * width),
        name="product",
    )(design, *taken, *after, *([weights] if ahead else []))


def add_rows(terms, each, first, out_ref):
    at, rows = 0, out_ref.shape[0]
    for c in range(0, len(terms), each):
        chunk, width = terms[c : c + each], terms[c].shape[1]
        total = sum(term[first : first + rows, :].astype(jnp.float32) for term in chunk)
        out_ref[:, at : at + width] = total.astype(jnp.bfloat16)
        at += width


def pack_kernel(spread, widths, places, first, later, start_ref, onehot_ref, tile_ref, *refs):
    if later:
        count, each = later
        *terms, out_ref, send_ref, keep_ref, summed, packed = refs
        rows = packed.shape[1]
        add_rows(terms[-count:], each, 3 * rows, send_ref)
        add_rows(terms[-count:], each, rows, keep_ref)
        terms = terms[:-count]
    else:
        *terms, out_ref, summed, packed = refs
    owners, rows = packed.shape[:2]
    if first:
        packed[...] = terms.pop(0)[...]
    else:
        packed[...] = jnp.zeros_like(packed)
    at = 0
    for width, spots in zip(widths, places):
        total = 0.0
        for row, column in spots:
            total = total + terms.pop(0)[row : row + rows, column : column + width].astype(jnp.float32)
        summed[:, at : at + width] = total.astype(jnp.bfloat16)
        at += width
    step = VOX_BLOCK // LANES

    def moves(index, far):
        block = first + index
        values = summed[:, pl.ds(pl.multiple_of(index * VOX_BLOCK, VOX_BLOCK), VOX_BLOCK)]
        onehot = onehot_ref[pl.ds(pl.multiple_of(block * VOX_BLOCK, VOX_BLOCK), VOX_BLOCK), :]
        tiles = jnp.concatenate([tile_ref[pl.ds(block * step + i, 1), :] for i in range(step)], axis=1)
        low = [start_ref[block, o] >> 7 for o in range(owners)]
        chosen = []
        for o in range(owners):
            tile = tiles - (o * spread + low[o])
            hit = jnp.where((tile == 2) if far else ((tile == 0) | (tile == 1)), 1.0, 0.0)
            chosen.append(values * hit.astype(jnp.bfloat16))
        moved = jnp.dot(jnp.concatenate(chosen, axis=0), onehot, preferred_element_type=jnp.float32)
        moved = moved.astype(jnp.bfloat16)
        out = []
        for o in range(owners):
            here = moved[o * rows : (o + 1) * rows]
            tile, here = (low[o] + 2, here[:, :SLOT_TILE]) if far else (low[o], here)
            lanes = pl.ds(pl.multiple_of(tile * SLOT_TILE, SLOT_TILE), here.shape[1])
            out.append((o, lanes, here))
        high = [(start_ref[block + 1, o] - 1) >> 7 for o in range(owners)]
        return out, functools.reduce(jnp.maximum, [high[o] - low[o] for o in range(owners)])

    def add(targets):
        sums = [packed[owner, :, lanes] + moved for owner, lanes, moved in targets]
        for (owner, lanes, _), total in zip(targets, sums):
            packed[owner, :, lanes] = total

    def blocks(indices):
        found = [moves(index, False) for index in indices]
        for targets, _ in found:
            add(targets)
        for index, (_, longest) in zip(indices, found):

            @pl.when(longest > 1)
            def _():
                add(moves(index, True)[0])

    count = sum(widths) // VOX_BLOCK

    def two(i, carry):
        blocks([2 * i, 2 * i + 1])
        return carry

    lax.fori_loop(0, count // 2, two, 0)
    if count % 2:
        blocks([count - 1])
    out_ref[...] = packed[:, :, : out_ref.shape[2]]


def shards(features, hrf_filters, weights, voxel_parcel, parcel_owner):
    owners, parts = lax.axis_size("vox"), lax.axis_size("chan")
    me = lax.axis_index("chan")
    voxels = voxel_parcel.shape[0]
    send_cap = 2 * voxels // owners
    bases, depth, _ = weights.shape
    blocks = voxels // VOX_BLOCK
    time_block = features.shape[0]
    time_len = time_block * parts

    series = [lax.dynamic_slice_in_dim(features, (me ^ d) * depth, depth, 1) for d in range(parts)]
    for d in range(1, parts):
        series[d] = lax.ppermute(series[d], "chan", [(i, i ^ d) for i in range(parts)])
    filters = jnp.transpose(hrf_filters, (0, 2, 1))
    spare = -depth % LANES
    lanes = bases * (depth + spare)
    unit = voxels // sum(units for pieces in COPIES for _, units in pieces)
    copied = [unit * sum(units for _, units in pieces) for pieces in COPIES]
    firsts = [sum(copied[:i]) for i in range(len(copied))]
    held = [[] for _ in range(CHUNKS)]

    def room(i):
        if i >= len(COPIES):
            return []
        return [pltpu.VMEM((bases, depth + spare, unit * units), jnp.bfloat16) for _, units in COPIES[i]]

    def keep_pieces(i, pieces):
        for (chunk, _), piece in zip(COPIES[i] if i < len(COPIES) else (), pieces):
            held[chunk].append(piece)

    if spare:
        series = [jnp.pad(part, ((0, 0), (0, spare))) for part in series]
        filters = jnp.pad(filters, ((0, 0), (0, 0), (0, spare)))

    table_rows = -(-parcel_owner.shape[0] // LANES)
    table = jnp.pad(parcel_owner, (0, table_rows * LANES - parcel_owner.shape[0])).reshape(table_rows, LANES)
    marks = -(-(blocks + 1) // 8) * 8
    spread = send_cap // SLOT_TILE + 3
    bits = parts.bit_length() - 1
    order = jnp.arange(parts, dtype=jnp.int32) ^ me
    place = sum(((order >> bit) & 1) << (bits - 1 - bit) for bit in range(bits)).astype(jnp.int32)

    early_rows = 2 * time_block - ROWS
    onehot, tiles, starts, early, *pieces = pl.pallas_call(
        functools.partial(early_kernel, owners, spread),
        in_specs=[SMEM(), VMEM(), VMEM(), HBM(), VMEM(), HBM(), ANY()],
        out_specs=[VMEM()] * (4 + len(COPIES[0])),
        out_shape=[
            jax.ShapeDtypeStruct((voxels, 2 * SLOT_TILE), jnp.bfloat16),
            jax.ShapeDtypeStruct((voxels // LANES, LANES), jnp.int32),
            jax.ShapeDtypeStruct((marks, LANES), jnp.int32),
            jax.ShapeDtypeStruct((early_rows, lanes), jnp.bfloat16),
        ]
        + room(0),
        scratch_shapes=filter_scratch(2 * time_block)
        + [
            pltpu.VMEM(filters.shape, jnp.float32),
            pltpu.VMEM((voxels // LANES, LANES), jnp.int32),
            pltpu.SemaphoreType.DMA((len(COPIES[0]), 4)),
            pltpu.SemaphoreType.DMA((2,)),
        ],
        compiler_params=pltpu.CompilerParams(vmem_limit_bytes=8 * MIB),
        cost_estimate=cost(0, 2 * bases * depth * copied[0]),
        name="early",
    )(
        order,
        series[0],
        series[1],
        pltpu.with_memory_space_constraint(voxel_parcel.reshape(-1, LANES), pltpu.HBM),
        table,
        pltpu.with_memory_space_constraint(filters, pltpu.HBM),
        weights,
    )
    keep_pieces(0, pieces)
    design, *pieces = pl.pallas_call(
        functools.partial(design_kernel, parts, firsts[1]),
        in_specs=[SMEM(), SMEM(), VMEM(), VMEM(), ANY()] + [VMEM()] * parts,
        out_specs=[VMEM()] * (1 + len(COPIES[1])),
        out_shape=[jax.ShapeDtypeStruct((time_len, lanes), jnp.bfloat16)] + room(1),
        scratch_shapes=filter_scratch(time_len) + [pltpu.SemaphoreType.DMA((len(COPIES[1]), 4))],
        compiler_params=pltpu.CompilerParams(vmem_limit_bytes=8 * MIB),
        cost_estimate=cost(0, 2 * bases * depth * copied[1]),
        name="design",
    )(order, place, early, filters, weights, *series)
    keep_pieces(1, pieces)

    half = time_block // 2
    widths, sums, sent, got = [], [], [], []
    for c in range(CHUNKS):
        after = sent[max(c - 2, 0) : max(c - 1, 0)] + got[max(c - 3, 0) : max(c - 2, 0)]
        ahead = room(c + 2)
        keep, send, *pieces = product(design, held[c], after, weights, firsts[c + 2] if ahead else 0, ahead)
        keep_pieces(c + 2, pieces)
        widths.append(keep.shape[1])
        own = [keep]
        for bit in range(bits):
            if bit > 0:
                rows = own[-1].shape[0] // 2
                send = added(own, rows, half if bit == bits - 1 else rows)
                if bit == bits - 1:
                    sent.append(send)
            own.append(lax.ppermute(send, "chan", [(i, i ^ (1 << bit)) for i in range(parts)]))
        sums.append(own)
        got.append(own[-1])
    def pack(chunks, terms, spots, packed=(), later=()):
        here = [widths[c] for c in chunks]
        lanes_out = send_cap if chunks[-1] == CHUNKS - 1 else spread * SLOT_TILE
        spec = (len(later), bits) if later else None
        return pl.pallas_call(
            functools.partial(pack_kernel, spread, here, spots, sum(widths[: chunks[0]]) // VOX_BLOCK, spec),
            in_specs=[SMEM(), VMEM(), VMEM()] + [VMEM()] * (len(packed) + len(terms) + len(later)),
            out_specs=[VMEM()] * (3 if later else 1),
            out_shape=[jax.ShapeDtypeStruct((owners, half, lanes_out), jnp.bfloat16)]
            + ([jax.ShapeDtypeStruct((half, voxels), jnp.bfloat16)] if later else [])
            + ([pltpu.VMEM((half, voxels), jnp.bfloat16)] if later else []),
            scratch_shapes=[
                pltpu.VMEM((half, sum(here)), jnp.bfloat16),
                pltpu.VMEM((owners, half, spread * SLOT_TILE), jnp.bfloat16),
            ],
            compiler_params=pltpu.CompilerParams(vmem_limit_bytes=8 * MIB),
            cost_estimate=cost(2 * half * owners * VOX_BLOCK * sum(here), 4 * half * sum(here)),
            name="pack",
        )(starts, onehot, tiles, *packed, *terms, *later)

    def deliver(packed):
        return lax.all_to_all(packed, "vox", split_axis=0, concat_axis=0, tiled=True)

    def early_terms(chunks):
        return [term for c in chunks for term in sums[c]], [[(0, 0)] * len(sums[c]) for c in chunks]

    low, high = range(PACK_FIRST), range(PACK_FIRST, CHUNKS)
    packed, late_send, late_own = pack(low, *early_terms(low), later=[term for own in sums for term in own[:-1]])
    late = lax.ppermute(late_send, "chan", [(i, i ^ (1 << (bits - 1))) for i in range(parts)])
    one = deliver(*pack(high, *early_terms(high), packed=[packed]))
    starting = [sum(widths[:c]) for c in range(CHUNKS)]
    two = deliver(
        *pack(range(CHUNKS), [late_own, late] * CHUNKS, [[(0, first)] * 2 for first in starting])
    )
    return jnp.transpose(jnp.concatenate([one, two], axis=1), (0, 2, 1))


def added(terms, first, rows):
    return sum(term[first : first + rows].astype(jnp.float32) for term in terms).astype(jnp.bfloat16)


def solution(mesh):
    return jax.shard_map(
        shards,
        mesh=mesh,
        in_specs=(P("chan", None), P(None, "chan", None), P(None, "chan", "vox"), P("vox"), P()),
        out_specs=P("vox", None, "chan"),
        check_vma=False,
    )
```

```python
import functools

import jax
import jax.numpy as jnp
from jax import lax
from jax.experimental import pallas as pl
from jax.experimental.pallas import tpu as pltpu
from jax.sharding import PartitionSpec as P

FILTER_TAPS = 16
TAP_SPACING = 2
LANES = 128
SLOT_TILE = 128
VOX_BLOCK = 256
COLUMNS = 512
ROWS = 32
CHUNKS = 4
COPIES = (((0, 4), (1, 5)), ((1, 1), (2, 4)), (), ((2, 2), (3, 1)), ((3, 2), (3, 1)))
PACK_FIRST = 2
MIB = 1 << 20

VMEM = functools.partial(pl.BlockSpec, memory_space=pltpu.VMEM)
SMEM = functools.partial(pl.BlockSpec, memory_space=pltpu.SMEM)
ANY = functools.partial(pl.BlockSpec, memory_space=pl.ANY)
HBM = functools.partial(pl.BlockSpec, memory_space=pltpu.HBM)


def copy_pieces(weight_ref, piece_refs, sems, first):
    depth, copies = weight_ref.shape[1], []
    for i, ref in enumerate(piece_refs):
        if ref.shape[1] > depth:
            ref[:, depth:, :] = jnp.zeros_like(ref[:, depth:, :])
        copy = pltpu.make_async_copy(
            weight_ref.at[:, :, pl.ds(first, ref.shape[2])], ref.at[:, pl.ds(0, depth), :], sems.at[i]
        )
        copy.start()
        copies.append(copy)
        first += ref.shape[2]
    return copies


def wait_all(copies):
    for copy in copies:
        copy.wait()


def cost(flops, read):
    return pl.CostEstimate(flops=flops, bytes_accessed=read, transcendentals=0)


def places(owners, spread, parcel_ref, table_ref, inner_ref, tile_ref, start_ref):
    rows = parcel_ref.shape[0]
    parcel = parcel_ref[...]
    high, low = parcel >> 7, parcel & 127
    owner = jnp.zeros_like(parcel)
    for entry in range(table_ref.shape[0]):
        line = jnp.broadcast_to(table_ref[entry : entry + 1, :], parcel.shape)
        found = jnp.take_along_axis(line, low, axis=1, mode="promise_in_bounds")
        owner = jnp.where(high == entry, found, owner)

    def below(shape, scale=1):
        less = lax.broadcasted_iota(jnp.int32, shape, 1) < scale * lax.broadcasted_iota(jnp.int32, shape, 0)
        return less.astype(jnp.float32).astype(jnp.bfloat16)

    lane = lax.broadcasted_iota(jnp.int32, (LANES, LANES), 1)
    above = (lax.broadcasted_iota(jnp.int32, (LANES, LANES), 0) < lane).astype(jnp.float32).astype(jnp.bfloat16)
    ones = jnp.ones((LANES, LANES), jnp.bfloat16)
    marks = start_ref.shape[0]
    ahead, block_ahead = below((rows, rows)), below((marks, rows), VOX_BLOCK // LANES)
    mark_lane = lax.broadcasted_iota(jnp.int32, (marks, LANES), 1)
    dot = functools.partial(jnp.dot, preferred_element_type=jnp.float32)
    row_block = lax.broadcasted_iota(jnp.int32, (rows, rows), 0) & -(VOX_BLOCK // LANES)
    before = lax.broadcasted_iota(jnp.int32, (rows, rows), 1) < row_block
    before = before.astype(jnp.float32).astype(jnp.bfloat16)
    slots = jnp.zeros(parcel.shape, jnp.float32)
    bases = jnp.zeros(parcel.shape, jnp.float32)
    starts = jnp.zeros((marks, LANES), jnp.float32)
    for o in range(owners):
        mine = owner == o
        hot = mine.astype(jnp.float32).astype(jnp.bfloat16)
        totals = dot(hot, ones).astype(jnp.bfloat16)
        slots = jnp.where(mine, dot(hot, above) + dot(ahead, totals), slots)
        bases = jnp.where(mine, dot(before, totals), bases)
        starts = jnp.where(mark_lane == o, dot(block_ahead, totals), starts)
    slots = slots.astype(jnp.int32)
    start_ref[...] = starts.astype(jnp.int32)
    tile_ref[...] = owner * spread + (slots >> 7)
    inner_ref[...] = (slots - (bases.astype(jnp.int32) & -SLOT_TILE)) & (2 * SLOT_TILE - 1)


def clear_lead(shifted):
    lead = TAP_SPACING * FILTER_TAPS
    for s in range(shifted.shape[0]):
        shifted[s, : lead + 8, :] = jnp.zeros((lead + 8, LANES), jnp.float32)


def shift(plain, shifted):
    lead, time_len = TAP_SPACING * FILTER_TAPS, plain.shape[0]
    series = plain[...]
    for s in range(shifted.shape[0]):
        shifted[s, lead + s * TAP_SPACING : lead + s * TAP_SPACING + time_len, :] = series


def filter_rows(shifted, filter_ref, column, first):
    lead = TAP_SPACING * FILTER_TAPS
    sums = [jnp.zeros((ROWS, LANES), jnp.float32) for _ in range(filter_ref.shape[0])]
    for tap in range(FILTER_TAPS):
        delay = tap * TAP_SPACING
        start = lead + first - 8 * (delay // 8)
        if not isinstance(start, int):
            start = pl.multiple_of(start, 8)
        lagged = shifted[(delay % 8) // TAP_SPACING, pl.ds(start, ROWS), :]
        for b in range(len(sums)):
            sums[b] = sums[b] + filter_ref[b, tap : tap + 1, column] * lagged
    return sums


def lane_tile(tile):
    return pl.ds(pl.multiple_of(tile * LANES, LANES), LANES)


def early_kernel(owners, spread, order_ref, own_ref, pair_ref, parcel_hbm, table_ref, filter_hbm, weight_ref, *refs):
    inner_ref, tile_ref, start_ref, design_ref, *piece_refs, plain, shifted, filter_ref, parcel_ref, sems, small_sems = refs
    load_filter = pltpu.make_async_copy(filter_hbm, filter_ref, small_sems.at[0])
    load_parcel = pltpu.make_async_copy(parcel_hbm, parcel_ref, small_sems.at[1])
    load_filter.start()
    load_parcel.start()
    copies = copy_pieces(weight_ref, piece_refs, sems, 0)
    block, width = own_ref.shape
    core = lax.rem(order_ref[0], 2)
    own = pl.ds(pl.multiple_of(core * block, block), block)
    pair = pl.ds(pl.multiple_of((1 - core) * block, block), block)
    clear_lead(shifted)
    load_filter.wait()

    def columns(tile, carry):
        column = lane_tile(tile)
        plain[own, :] = own_ref[:, column].astype(jnp.float32)
        plain[pair, :] = pair_ref[:, column].astype(jnp.float32)
        shift(plain, shifted)
        for first in range(ROWS, 2 * block, ROWS):
            for b, rows in enumerate(filter_rows(shifted, filter_ref, column, first)):
                lanes = pl.ds(pl.multiple_of(b * width + tile * LANES, LANES), LANES)
                design_ref[first - ROWS : first, lanes] = rows.astype(jnp.bfloat16)
        return carry

    lax.fori_loop(0, width // LANES, columns, 0)
    load_parcel.wait()
    places(owners, spread, parcel_ref, table_ref, inner_ref, tile_ref, start_ref)
    wait_all(copies)


def design_kernel(parts, first, order_ref, place_ref, early_ref, filter_ref, weight_ref, *refs):
    series_refs, (design_ref, *piece_refs, plain, shifted, sems) = refs[:parts], refs[parts:]
    copies = copy_pieces(weight_ref, piece_refs, sems, first)
    block, width = series_refs[0].shape
    chip = order_ref[0] >> 1
    clear_lead(shifted)

    def place(part, inner):
        return pl.ds(pl.multiple_of(place_ref[part] * block + inner, ROWS), ROWS)

    for first in range(ROWS, 2 * block, ROWS):
        row = place(2 * chip + first // block, first % block)
        design_ref[row, :] = early_ref[first - ROWS : first, :]

    def columns(tile, carry):
        column = lane_tile(tile)
        for d in range(parts):
            row = pl.ds(pl.multiple_of(order_ref[d] * block, block), block)
            plain[row, :] = series_refs[d][:, column].astype(jnp.float32)
        shift(plain, shifted)
        for other in range(parts // 2):
            for inner in range(0, 2 * block if other else ROWS, ROWS):
                part = 2 * (chip ^ other) + inner // block
                start = part * block + inner % block
                row = place(part, inner % block)
                for b, rows in enumerate(filter_rows(shifted, filter_ref, column, start)):
                    lanes = pl.ds(pl.multiple_of(b * width + tile * LANES, LANES), LANES)
                    design_ref[row, lanes] = rows.astype(jnp.bfloat16)
        return carry

    lax.fori_loop(0, width // LANES, columns, 0)
    wait_all(copies)


def filter_scratch(time_len):
    return [
        pltpu.VMEM((time_len, LANES), jnp.float32),
        pltpu.VMEM((8 // TAP_SPACING, time_len + TAP_SPACING * FILTER_TAPS + 8, LANES), jnp.float32),
    ]


def product_kernel(taken, extra, first, design_ref, *refs):
    weight_refs, refs = refs[:taken], refs[taken + extra :]
    copies = []
    if first is not None:
        weight_ref, keep_ref, send_ref, *piece_refs, sems = refs
        copies = copy_pieces(weight_ref, piece_refs, sems, first)
    else:
        keep_ref, send_ref = refs
    half, at = keep_ref.shape[0], 0
    for ref in weight_refs:
        for start in range(0, ref.shape[2], COLUMNS):
            weight = ref[:, :, start : min(start + COLUMNS, ref.shape[2])]
            weight = weight.reshape(-1, weight.shape[2])
            total = jnp.dot(design_ref[...], weight, preferred_element_type=jnp.float32)
            columns = slice(at, at + weight.shape[1])
            keep_ref[:, columns] = total[:half].astype(jnp.bfloat16)
            send_ref[:, columns] = total[half:].astype(jnp.bfloat16)
            at += weight.shape[1]
    wait_all(copies)


def product(design, taken, after, weights, first, ahead):
    time_len, lanes = design.shape
    width = sum(piece.shape[2] for piece in taken)
    half = jax.ShapeDtypeStruct((time_len // 2, width), jnp.bfloat16)
    return pl.pallas_call(
        functools.partial(product_kernel, len(taken), len(after), first if ahead else None),
        in_specs=[VMEM()] * (1 + len(taken)) + [ANY()] * (len(after) + bool(ahead)),
        out_specs=[VMEM()] * (2 + len(ahead)),
        out_shape=[half, half] + ahead,
        scratch_shapes=[pltpu.SemaphoreType.DMA((len(ahead),))] if ahead else [],
        compiler_params=pltpu.CompilerParams(vmem_limit_bytes=8 * MIB),
        cost_estimate=cost(2 * time_len * lanes * width, 2 * lanes * width),
        name="product",
    )(design, *taken, *after, *([weights] if ahead else []))


def add_rows(terms, each, first, out_ref):
    at, rows = 0, out_ref.shape[0]
    for c in range(0, len(terms), each):
        chunk, width = terms[c : c + each], terms[c].shape[1]
        total = sum(term[first : first + rows, :].astype(jnp.float32) for term in chunk)
        out_ref[:, at : at + width] = total.astype(jnp.bfloat16)
        at += width


def pack_kernel(spread, widths, places, first, later, outs, order_ref, start_ref, inner_ref, tile_ref, *refs):
    *refs, summed, packed = refs
    if later:
        count, each = later
        *refs, send_ref, keep_ref = refs
    terms, out_refs = refs[: len(refs) - outs], refs[len(refs) - outs :]
    if later:
        rows = packed.shape[1]
        add_rows(terms[-count:], each, 3 * rows, send_ref)
        add_rows(terms[-count:], each, rows, keep_ref)
        terms = terms[:-count]
    owners, rows = packed.shape[:2]
    if first:
        packed[...] = terms.pop(0)[...]
    else:
        packed[...] = jnp.zeros_like(packed)
    at = 0
    for width, spots in zip(widths, places):
        total = 0.0
        for row, column in spots:
            total = total + terms.pop(0)[row : row + rows, column : column + width].astype(jnp.float32)
        summed[:, at : at + width] = total.astype(jnp.bfloat16)
        at += width
    step = VOX_BLOCK // LANES
    slot_rows = lax.broadcasted_iota(jnp.int32, (2 * SLOT_TILE, VOX_BLOCK), 0)

    def moves(index, far):
        block = first + index
        values = summed[:, pl.ds(pl.multiple_of(index * VOX_BLOCK, VOX_BLOCK), VOX_BLOCK)]
        tiles, inner = (
            jnp.concatenate([ref[pl.ds(block * step + i, 1), :] for i in range(step)], axis=1)
            for ref in (tile_ref, inner_ref)
        )
        onehot = jnp.where(inner == slot_rows, 1.0, 0.0).astype(jnp.bfloat16)
        low = [start_ref[block, o] >> 7 for o in range(owners)]
        chosen = []
        for o in range(owners):
            tile = tiles - (o * spread + low[o])
            hit = jnp.where((tile == 2) if far else ((tile == 0) | (tile == 1)), 1.0, 0.0)
            chosen.append(values * hit.astype(jnp.bfloat16))
        moved = lax.dot_general(
            jnp.concatenate(chosen, axis=0), onehot, (((1,), (1,)), ((), ())), preferred_element_type=jnp.float32
        )
        moved = moved.astype(jnp.bfloat16)
        out = []
        for o in range(owners):
            here = moved[o * rows : (o + 1) * rows]
            tile, here = (low[o] + 2, here[:, :SLOT_TILE]) if far else (low[o], here)
            lanes = pl.ds(pl.multiple_of(tile * SLOT_TILE, SLOT_TILE), here.shape[1])
            out.append((o, lanes, here))
        high = [(start_ref[block + 1, o] - 1) >> 7 for o in range(owners)]
        return out, functools.reduce(jnp.maximum, [high[o] - low[o] for o in range(owners)])

    def add(targets):
        sums = [packed[owner, :, lanes] + moved for owner, lanes, moved in targets]
        for (owner, lanes, _), total in zip(targets, sums):
            packed[owner, :, lanes] = total

    def blocks(indices):
        found = [moves(index, False) for index in indices]
        for targets, _ in found:
            add(targets)
        for index, (_, longest) in zip(indices, found):

            @pl.when(longest > 1)
            def _():
                add(moves(index, True)[0])

    count = sum(widths) // VOX_BLOCK

    def two(i, carry):
        blocks([2 * i, 2 * i + 1])
        return carry

    lax.fori_loop(0, count // 2, two, 0)
    if count % 2:
        blocks([count - 1])
    if outs == 1:
        out_refs[0][...] = packed[...]
    else:
        for d, ref in enumerate(out_refs):
            ref[...] = packed[order_ref[d], :, : ref.shape[1]]


def shards(features, hrf_filters, weights, voxel_parcel, parcel_owner):
    owners, parts = lax.axis_size("vox"), lax.axis_size("chan")
    me = lax.axis_index("chan")
    voxels = voxel_parcel.shape[0]
    send_cap = 2 * voxels // owners
    bases, depth, _ = weights.shape
    blocks = voxels // VOX_BLOCK
    time_block = features.shape[0]
    time_len = time_block * parts

    series = [lax.dynamic_slice_in_dim(features, (me ^ d) * depth, depth, 1) for d in range(parts)]
    for d in range(1, parts):
        series[d] = lax.ppermute(series[d], "chan", [(i, i ^ d) for i in range(parts)])
    filters = jnp.transpose(hrf_filters, (0, 2, 1))
    spare = -depth % LANES
    lanes = bases * (depth + spare)
    unit = voxels // sum(units for pieces in COPIES for _, units in pieces)
    copied = [unit * sum(units for _, units in pieces) for pieces in COPIES]
    firsts = [sum(copied[:i]) for i in range(len(copied))]
    held = [[] for _ in range(CHUNKS)]

    def room(i):
        if i >= len(COPIES):
            return []
        return [pltpu.VMEM((bases, depth + spare, unit * units), jnp.bfloat16) for _, units in COPIES[i]]

    def keep_pieces(i, pieces):
        for (chunk, _), piece in zip(COPIES[i] if i < len(COPIES) else (), pieces):
            held[chunk].append(piece)

    if spare:
        series = [jnp.pad(part, ((0, 0), (0, spare))) for part in series]
        filters = jnp.pad(filters, ((0, 0), (0, 0), (0, spare)))

    table_rows = -(-parcel_owner.shape[0] // LANES)
    table = jnp.pad(parcel_owner, (0, table_rows * LANES - parcel_owner.shape[0])).reshape(table_rows, LANES)
    marks = -(-(blocks + 1) // 8) * 8
    spread = send_cap // SLOT_TILE + 3
    bits = parts.bit_length() - 1
    order = jnp.arange(parts, dtype=jnp.int32) ^ me
    place = sum(((order >> bit) & 1) << (bits - 1 - bit) for bit in range(bits)).astype(jnp.int32)

    early_rows = 2 * time_block - ROWS
    inner, tiles, starts, early, *pieces = pl.pallas_call(
        functools.partial(early_kernel, owners, spread),
        in_specs=[SMEM(), VMEM(), VMEM(), HBM(), VMEM(), HBM(), ANY()],
        out_specs=[VMEM()] * (4 + len(COPIES[0])),
        out_shape=[
            jax.ShapeDtypeStruct((voxels // LANES, LANES), jnp.int32),
            jax.ShapeDtypeStruct((voxels // LANES, LANES), jnp.int32),
            jax.ShapeDtypeStruct((marks, LANES), jnp.int32),
            jax.ShapeDtypeStruct((early_rows, lanes), jnp.bfloat16),
        ]
        + room(0),
        scratch_shapes=filter_scratch(2 * time_block)
        + [
            pltpu.VMEM(filters.shape, jnp.float32),
            pltpu.VMEM((voxels // LANES, LANES), jnp.int32),
            pltpu.SemaphoreType.DMA((len(COPIES[0]),)),
            pltpu.SemaphoreType.DMA((2,)),
        ],
        compiler_params=pltpu.CompilerParams(vmem_limit_bytes=8 * MIB),
        cost_estimate=cost(0, 2 * bases * depth * copied[0]),
        name="early",
    )(
        order,
        series[0],
        series[1],
        pltpu.with_memory_space_constraint(voxel_parcel.reshape(-1, LANES), pltpu.HBM),
        table,
        pltpu.with_memory_space_constraint(filters, pltpu.HBM),
        weights,
    )
    keep_pieces(0, pieces)
    design, *pieces = pl.pallas_call(
        functools.partial(design_kernel, parts, firsts[1]),
        in_specs=[SMEM(), SMEM(), VMEM(), VMEM(), ANY()] + [VMEM()] * parts,
        out_specs=[VMEM()] * (1 + len(COPIES[1])),
        out_shape=[jax.ShapeDtypeStruct((time_len, lanes), jnp.bfloat16)] + room(1),
        scratch_shapes=filter_scratch(time_len) + [pltpu.SemaphoreType.DMA((len(COPIES[1]),))],
        compiler_params=pltpu.CompilerParams(vmem_limit_bytes=8 * MIB),
        cost_estimate=cost(0, 2 * bases * depth * copied[1]),
        name="design",
    )(order, place, early, filters, weights, *series)
    keep_pieces(1, pieces)

    half = time_block // 2
    widths, sums, sent, got = [], [], [], []
    for c in range(CHUNKS):
        after = sent[max(c - 2, 0) : max(c - 1, 0)] + got[max(c - 3, 0) : max(c - 2, 0)]
        ahead = room(c + 2)
        keep, send, *pieces = product(design, held[c], after, weights, firsts[c + 2] if ahead else 0, ahead)
        keep_pieces(c + 2, pieces)
        widths.append(keep.shape[1])
        own = [keep]
        for bit in range(bits):
            if bit > 0:
                rows = own[-1].shape[0] // 2
                send = added(own, rows, half if bit == bits - 1 else rows)
                if bit == bits - 1:
                    sent.append(send)
            own.append(lax.ppermute(send, "chan", [(i, i ^ (1 << bit)) for i in range(parts)]))
        sums.append(own)
        got.append(own[-1])
    here = lax.axis_index("vox")
    targets = jnp.arange(owners, dtype=jnp.int32) ^ here

    def pack(chunks, terms, spots, packed=(), later=()):
        sizes = [widths[c] for c in chunks]
        spec = (len(later), bits) if later else None
        if chunks[-1] == CHUNKS - 1:
            outs = [jax.ShapeDtypeStruct((half, send_cap), jnp.bfloat16)] * owners
        else:
            outs = [jax.ShapeDtypeStruct((owners, half, spread * SLOT_TILE), jnp.bfloat16)]
        more = []
        if later:
            more = [jax.ShapeDtypeStruct((half, voxels), jnp.bfloat16), pltpu.VMEM((half, voxels), jnp.bfloat16)]
        return pl.pallas_call(
            functools.partial(
                pack_kernel, spread, sizes, spots, sum(widths[: chunks[0]]) // VOX_BLOCK, spec, len(outs)
            ),
            in_specs=[SMEM(), SMEM(), VMEM(), VMEM()] + [VMEM()] * (len(packed) + len(terms) + len(later)),
            out_specs=[VMEM()] * (len(outs) + len(more)),
            out_shape=outs + more,
            scratch_shapes=[
                pltpu.VMEM((half, sum(sizes)), jnp.bfloat16),
                pltpu.VMEM((owners, half, spread * SLOT_TILE), jnp.bfloat16),
            ],
            compiler_params=pltpu.CompilerParams(vmem_limit_bytes=8 * MIB),
            cost_estimate=cost(2 * half * owners * VOX_BLOCK * sum(sizes), 4 * half * sum(sizes)),
            name="pack",
        )(targets, starts, inner, tiles, *packed, *terms, *later)

    def deliver(packed):
        got = list(packed)
        far, near = range(owners - 1, owners // 2 - 1, -1), range(owners // 2 - 1, -1, -1)
        for d in [d for pair in zip(far, near) for d in pair if d]:
            got[d] = lax.ppermute(packed[d], "vox", [(i, i ^ d) for i in range(owners)])
        return got

    def early_terms(chunks):
        return [term for c in chunks for term in sums[c]], [[(0, 0)] * len(sums[c]) for c in chunks]

    low, high = range(PACK_FIRST), range(PACK_FIRST, CHUNKS)
    packed = pack(low, *early_terms(low))
    *one, late_send, late_own = pack(
        high, *early_terms(high), packed=packed, later=[term for own in sums for term in own[:-1]]
    )
    late = lax.ppermute(late_send, "chan", [(i, i ^ (1 << (bits - 1))) for i in range(parts)])
    one = deliver(one)
    starting = [sum(widths[:c]) for c in range(CHUNKS)]
    two = pack(range(CHUNKS), [late_own, late] * CHUNKS, [[(0, first)] * 2 for first in starting])
    two = pl.pallas_call(
        gate_kernel,
        in_specs=[ANY()] * (2 * owners),
        out_specs=[ANY()] * owners,
        out_shape=[jax.ShapeDtypeStruct((half, send_cap), jnp.bfloat16)] * owners,
        input_output_aliases={i: i for i in range(owners)},
        name="gate",
    )(*two, *one)
    two = deliver(two)
    owned = pl.pallas_call(
        functools.partial(assemble_kernel, owners),
        in_specs=[SMEM()] + [ANY()] * (2 * owners),
        out_specs=HBM(),
        out_shape=jax.ShapeDtypeStruct((owners, time_block, send_cap), jnp.bfloat16),
        scratch_shapes=[pltpu.SemaphoreType.DMA((2 * owners,))],
        name="assemble",
    )(targets, *one, *two)
    return jnp.transpose(owned, (0, 2, 1))


def gate_kernel(*refs):
    pass


def assemble_kernel(owners, order_ref, *refs):
    *parts, out_ref, sems = refs
    half = out_ref.shape[1] // 2
    copies = []
    for i, ref in enumerate(parts):
        rows = pl.ds(i // owners * half, half)
        copies.append(pltpu.make_async_copy(ref, out_ref.at[order_ref[i % owners], rows, :], sems.at[i]))
        copies[-1].start()
    wait_all(copies)


def added(terms, first, rows):
    return sum(term[first : first + rows].astype(jnp.float32) for term in terms).astype(jnp.bfloat16)


def solution(mesh):
    return jax.shard_map(
        shards,
        mesh=mesh,
        in_specs=(P("chan", None), P(None, "chan", None), P(None, "chan", "vox"), P("vox"), P()),
        out_specs=P("vox", None, "chan"),
        check_vma=False,
    )
```

```python
import functools

import jax
import jax.numpy as jnp
from jax import lax
from jax.experimental import pallas as pl
from jax.experimental.pallas import tpu as pltpu
from jax.sharding import PartitionSpec as P

FILTER_TAPS = 16
TAP_SPACING = 2
LANES = 128
SLOT_TILE = 128
VOX_BLOCK = 256
COLUMNS = 512
ROWS = 32
CHUNKS = 4
COPIES = (((0, 4), (1, 5)), ((1, 1), (2, 4)), (), ((2, 2), (3, 1)), ((3, 2), (3, 1)))
PACK_FIRST = 2
MIB = 1 << 20

VMEM = functools.partial(pl.BlockSpec, memory_space=pltpu.VMEM)
SMEM = functools.partial(pl.BlockSpec, memory_space=pltpu.SMEM)
ANY = functools.partial(pl.BlockSpec, memory_space=pl.ANY)
HBM = functools.partial(pl.BlockSpec, memory_space=pltpu.HBM)


def copy_pieces(weight_ref, piece_refs, sems, first):
    depth, copies = weight_ref.shape[1], []
    for i, ref in enumerate(piece_refs):
        if ref.shape[1] > depth:
            ref[:, depth:, :] = jnp.zeros_like(ref[:, depth:, :])
        copy = pltpu.make_async_copy(
            weight_ref.at[:, :, pl.ds(first, ref.shape[2])], ref.at[:, pl.ds(0, depth), :], sems.at[i]
        )
        copy.start()
        copies.append(copy)
        first += ref.shape[2]
    return copies


def wait_all(copies):
    for copy in copies:
        copy.wait()


def cost(flops, read):
    return pl.CostEstimate(flops=flops, bytes_accessed=read, transcendentals=0)


def places(owners, spread, parcel_ref, table_ref, inner_ref, tile_ref, start_ref):
    rows = parcel_ref.shape[0]
    parcel = parcel_ref[...]
    high, low = parcel >> 7, parcel & 127
    owner = jnp.zeros_like(parcel)
    for entry in range(table_ref.shape[0]):
        line = jnp.broadcast_to(table_ref[entry : entry + 1, :], parcel.shape)
        found = jnp.take_along_axis(line, low, axis=1, mode="promise_in_bounds")
        owner = jnp.where(high == entry, found, owner)

    def below(shape, scale=1):
        less = lax.broadcasted_iota(jnp.int32, shape, 1) < scale * lax.broadcasted_iota(jnp.int32, shape, 0)
        return less.astype(jnp.float32).astype(jnp.bfloat16)

    lane = lax.broadcasted_iota(jnp.int32, (LANES, LANES), 1)
    above = (lax.broadcasted_iota(jnp.int32, (LANES, LANES), 0) < lane).astype(jnp.float32).astype(jnp.bfloat16)
    ones = jnp.ones((LANES, LANES), jnp.bfloat16)
    marks = start_ref.shape[0]
    ahead, block_ahead = below((rows, rows)), below((marks, rows), VOX_BLOCK // LANES)
    mark_lane = lax.broadcasted_iota(jnp.int32, (marks, LANES), 1)
    dot = functools.partial(jnp.dot, preferred_element_type=jnp.float32)
    row_block = lax.broadcasted_iota(jnp.int32, (rows, rows), 0) & -(VOX_BLOCK // LANES)
    before = lax.broadcasted_iota(jnp.int32, (rows, rows), 1) < row_block
    before = before.astype(jnp.float32).astype(jnp.bfloat16)
    slots = jnp.zeros(parcel.shape, jnp.float32)
    bases = jnp.zeros(parcel.shape, jnp.float32)
    starts = jnp.zeros((marks, LANES), jnp.float32)
    for o in range(owners):
        mine = owner == o
        hot = mine.astype(jnp.float32).astype(jnp.bfloat16)
        totals = dot(hot, ones).astype(jnp.bfloat16)
        slots = jnp.where(mine, dot(hot, above) + dot(ahead, totals), slots)
        bases = jnp.where(mine, dot(before, totals), bases)
        starts = jnp.where(mark_lane == o, dot(block_ahead, totals), starts)
    slots = slots.astype(jnp.int32)
    start_ref[...] = starts.astype(jnp.int32)
    tile_ref[...] = owner * spread + (slots >> 7)
    inner_ref[...] = (slots - (bases.astype(jnp.int32) & -SLOT_TILE)) & (2 * SLOT_TILE - 1)


def clear_lead(shifted):
    lead = TAP_SPACING * FILTER_TAPS
    for s in range(shifted.shape[0]):
        shifted[s, : lead + 8, :] = jnp.zeros((lead + 8, LANES), jnp.float32)


def shift(plain, shifted):
    lead, time_len = TAP_SPACING * FILTER_TAPS, plain.shape[0]
    series = plain[...]
    for s in range(shifted.shape[0]):
        shifted[s, lead + s * TAP_SPACING : lead + s * TAP_SPACING + time_len, :] = series


def filter_rows(shifted, filter_ref, column, first):
    lead = TAP_SPACING * FILTER_TAPS
    sums = [jnp.zeros((ROWS, LANES), jnp.float32) for _ in range(filter_ref.shape[0])]
    for tap in range(FILTER_TAPS):
        delay = tap * TAP_SPACING
        start = lead + first - 8 * (delay // 8)
        if not isinstance(start, int):
            start = pl.multiple_of(start, 8)
        lagged = shifted[(delay % 8) // TAP_SPACING, pl.ds(start, ROWS), :]
        for b in range(len(sums)):
            sums[b] = sums[b] + filter_ref[b, tap : tap + 1, column] * lagged
    return sums


def lane_tile(tile):
    return pl.ds(pl.multiple_of(tile * LANES, LANES), LANES)


def early_kernel(owners, spread, order_ref, own_ref, pair_ref, parcel_hbm, table_ref, filter_hbm, weight_ref, *refs):
    inner_ref, tile_ref, start_ref, design_ref, *piece_refs, plain, shifted, filter_ref, parcel_ref, sems, small_sems = refs
    load_filter = pltpu.make_async_copy(filter_hbm, filter_ref, small_sems.at[0])
    load_parcel = pltpu.make_async_copy(parcel_hbm, parcel_ref, small_sems.at[1])
    load_filter.start()
    load_parcel.start()
    copies = copy_pieces(weight_ref, piece_refs, sems, 0)
    block, width = own_ref.shape
    core = lax.rem(order_ref[0], 2)
    own = pl.ds(pl.multiple_of(core * block, block), block)
    pair = pl.ds(pl.multiple_of((1 - core) * block, block), block)
    clear_lead(shifted)
    load_filter.wait()

    def columns(tile, carry):
        column = lane_tile(tile)
        plain[own, :] = own_ref[:, column].astype(jnp.float32)
        plain[pair, :] = pair_ref[:, column].astype(jnp.float32)
        shift(plain, shifted)
        for first in range(ROWS, 2 * block, ROWS):
            for b, rows in enumerate(filter_rows(shifted, filter_ref, column, first)):
                lanes = pl.ds(pl.multiple_of(b * width + tile * LANES, LANES), LANES)
                design_ref[first - ROWS : first, lanes] = rows.astype(jnp.bfloat16)
        return carry

    lax.fori_loop(0, width // LANES, columns, 0)
    load_parcel.wait()
    places(owners, spread, parcel_ref, table_ref, inner_ref, tile_ref, start_ref)
    wait_all(copies)


def design_kernel(parts, first, order_ref, place_ref, early_ref, filter_ref, weight_ref, *refs):
    series_refs, (design_ref, *piece_refs, plain, shifted, sems) = refs[:parts], refs[parts:]
    copies = copy_pieces(weight_ref, piece_refs, sems, first)
    block, width = series_refs[0].shape
    chip = order_ref[0] >> 1
    clear_lead(shifted)

    def place(part, inner):
        return pl.ds(pl.multiple_of(place_ref[part] * block + inner, ROWS), ROWS)

    for first in range(ROWS, 2 * block, ROWS):
        row = place(2 * chip + first // block, first % block)
        design_ref[row, :] = early_ref[first - ROWS : first, :]

    def columns(tile, carry):
        column = lane_tile(tile)
        for d in range(parts):
            row = pl.ds(pl.multiple_of(order_ref[d] * block, block), block)
            plain[row, :] = series_refs[d][:, column].astype(jnp.float32)
        shift(plain, shifted)
        for other in range(parts // 2):
            for inner in range(0, 2 * block if other else ROWS, ROWS):
                part = 2 * (chip ^ other) + inner // block
                start = part * block + inner % block
                row = place(part, inner % block)
                for b, rows in enumerate(filter_rows(shifted, filter_ref, column, start)):
                    lanes = pl.ds(pl.multiple_of(b * width + tile * LANES, LANES), LANES)
                    design_ref[row, lanes] = rows.astype(jnp.bfloat16)
        return carry

    lax.fori_loop(0, width // LANES, columns, 0)
    wait_all(copies)


def filter_scratch(time_len):
    return [
        pltpu.VMEM((time_len, LANES), jnp.float32),
        pltpu.VMEM((8 // TAP_SPACING, time_len + TAP_SPACING * FILTER_TAPS + 8, LANES), jnp.float32),
    ]


def product_kernel(taken, extra, first, design_ref, *refs):
    weight_refs, refs = refs[:taken], refs[taken + extra :]
    copies = []
    if first is not None:
        weight_ref, keep_ref, send_ref, *piece_refs, sems = refs
        copies = copy_pieces(weight_ref, piece_refs, sems, first)
    else:
        keep_ref, send_ref = refs
    half, at = keep_ref.shape[0], 0
    for ref in weight_refs:
        for start in range(0, ref.shape[2], COLUMNS):
            weight = ref[:, :, start : min(start + COLUMNS, ref.shape[2])]
            weight = weight.reshape(-1, weight.shape[2])
            total = jnp.dot(design_ref[...], weight, preferred_element_type=jnp.float32)
            columns = slice(at, at + weight.shape[1])
            keep_ref[:, columns] = total[:half].astype(jnp.bfloat16)
            send_ref[:, columns] = total[half:].astype(jnp.bfloat16)
            at += weight.shape[1]
    wait_all(copies)


def product(design, taken, after, weights, first, ahead):
    time_len, lanes = design.shape
    width = sum(piece.shape[2] for piece in taken)
    half = jax.ShapeDtypeStruct((time_len // 2, width), jnp.bfloat16)
    return pl.pallas_call(
        functools.partial(product_kernel, len(taken), len(after), first if ahead else None),
        in_specs=[VMEM()] * (1 + len(taken)) + [ANY()] * (len(after) + bool(ahead)),
        out_specs=[VMEM()] * (2 + len(ahead)),
        out_shape=[half, half] + ahead,
        scratch_shapes=[pltpu.SemaphoreType.DMA((len(ahead),))] if ahead else [],
        compiler_params=pltpu.CompilerParams(vmem_limit_bytes=8 * MIB),
        cost_estimate=cost(2 * time_len * lanes * width, 2 * lanes * width),
        name="product",
    )(design, *taken, *after, *([weights] if ahead else []))


def add_rows(terms, each, first, out_ref):
    at, rows = 0, out_ref.shape[0]
    for c in range(0, len(terms), each):
        chunk, width = terms[c : c + each], terms[c].shape[1]
        total = sum(term[first : first + rows, :].astype(jnp.float32) for term in chunk)
        out_ref[:, at : at + width] = total.astype(jnp.bfloat16)
        at += width


def pack_kernel(spread, widths, places, first, later, outs, order_ref, start_ref, inner_ref, tile_ref, *refs):
    *refs, summed, packed = refs
    if later:
        count, each = later
        *refs, send_ref, keep_ref = refs
    terms, out_refs = refs[: len(refs) - outs], refs[len(refs) - outs :]
    if later:
        rows = packed.shape[1]
        add_rows(terms[-count:], each, 3 * rows, send_ref)
        add_rows(terms[-count:], each, rows, keep_ref)
        terms = terms[:-count]
    owners, rows = packed.shape[:2]
    if first:
        packed[...] = terms.pop(0)[...]
    else:
        packed[...] = jnp.zeros_like(packed)
    at = 0
    for width, spots in zip(widths, places):
        total = 0.0
        for row, column in spots:
            total = total + terms.pop(0)[row : row + rows, column : column + width].astype(jnp.float32)
        summed[:, at : at + width] = total.astype(jnp.bfloat16)
        at += width
    step = VOX_BLOCK // LANES
    slot_rows = lax.broadcasted_iota(jnp.int32, (2 * SLOT_TILE, VOX_BLOCK), 0)

    def moves(index, far):
        block = first + index
        values = summed[:, pl.ds(pl.multiple_of(index * VOX_BLOCK, VOX_BLOCK), VOX_BLOCK)]
        tiles, inner = (
            jnp.concatenate([ref[pl.ds(block * step + i, 1), :] for i in range(step)], axis=1)
            for ref in (tile_ref, inner_ref)
        )
        onehot = jnp.where(inner == slot_rows, 1.0, 0.0).astype(jnp.bfloat16)
        low = [start_ref[block, o] >> 7 for o in range(owners)]
        chosen = []
        for o in range(owners):
            tile = tiles - (o * spread + low[o])
            hit = jnp.where((tile == 2) if far else ((tile == 0) | (tile == 1)), 1.0, 0.0)
            chosen.append(values * hit.astype(jnp.bfloat16))
        moved = lax.dot_general(
            jnp.concatenate(chosen, axis=0), onehot, (((1,), (1,)), ((), ())), preferred_element_type=jnp.float32
        )
        moved = moved.astype(jnp.bfloat16)
        out = []
        for o in range(owners):
            here = moved[o * rows : (o + 1) * rows]
            tile, here = (low[o] + 2, here[:, :SLOT_TILE]) if far else (low[o], here)
            lanes = pl.ds(pl.multiple_of(tile * SLOT_TILE, SLOT_TILE), here.shape[1])
            out.append((o, lanes, here))
        high = [(start_ref[block + 1, o] - 1) >> 7 for o in range(owners)]
        return out, functools.reduce(jnp.maximum, [high[o] - low[o] for o in range(owners)])

    def add(targets):
        sums = [packed[owner, :, lanes] + moved for owner, lanes, moved in targets]
        for (owner, lanes, _), total in zip(targets, sums):
            packed[owner, :, lanes] = total

    def blocks(indices):
        found = [moves(index, False) for index in indices]
        for targets, _ in found:
            add(targets)
        for index, (_, longest) in zip(indices, found):

            @pl.when(longest > 1)
            def _():
                add(moves(index, True)[0])

    count = sum(widths) // VOX_BLOCK

    def two(i, carry):
        blocks([2 * i, 2 * i + 1])
        return carry

    lax.fori_loop(0, count // 2, two, 0)
    if count % 2:
        blocks([count - 1])
    if outs == 1:
        out_refs[0][...] = packed[...]
    else:
        for d, ref in enumerate(out_refs):
            ref[...] = packed[order_ref[d], :, : ref.shape[1]]


def shards(features, hrf_filters, weights, voxel_parcel, parcel_owner):
    owners, parts = lax.axis_size("vox"), lax.axis_size("chan")
    me = lax.axis_index("chan")
    voxels = voxel_parcel.shape[0]
    send_cap = 2 * voxels // owners
    bases, depth, _ = weights.shape
    blocks = voxels // VOX_BLOCK
    time_block = features.shape[0]
    time_len = time_block * parts

    series = [lax.dynamic_slice_in_dim(features, (me ^ d) * depth, depth, 1) for d in range(parts)]
    for d in range(1, parts):
        series[d] = lax.ppermute(series[d], "chan", [(i, i ^ d) for i in range(parts)])
    filters = jnp.transpose(hrf_filters, (0, 2, 1))
    spare = -depth % LANES
    lanes = bases * (depth + spare)
    unit = voxels // sum(units for pieces in COPIES for _, units in pieces)
    copied = [unit * sum(units for _, units in pieces) for pieces in COPIES]
    firsts = [sum(copied[:i]) for i in range(len(copied))]
    held = [[] for _ in range(CHUNKS)]

    def room(i):
        if i >= len(COPIES):
            return []
        return [pltpu.VMEM((bases, depth + spare, unit * units), jnp.bfloat16) for _, units in COPIES[i]]

    def keep_pieces(i, pieces):
        for (chunk, _), piece in zip(COPIES[i] if i < len(COPIES) else (), pieces):
            held[chunk].append(piece)

    if spare:
        series = [jnp.pad(part, ((0, 0), (0, spare))) for part in series]
        filters = jnp.pad(filters, ((0, 0), (0, 0), (0, spare)))

    table_rows = -(-parcel_owner.shape[0] // LANES)
    table = jnp.pad(parcel_owner, (0, table_rows * LANES - parcel_owner.shape[0])).reshape(table_rows, LANES)
    marks = -(-(blocks + 1) // 8) * 8
    spread = send_cap // SLOT_TILE + 3
    bits = parts.bit_length() - 1
    order = jnp.arange(parts, dtype=jnp.int32) ^ me
    place = sum(((order >> bit) & 1) << (bits - 1 - bit) for bit in range(bits)).astype(jnp.int32)

    early_rows = 2 * time_block - ROWS
    inner, tiles, starts, early, *pieces = pl.pallas_call(
        functools.partial(early_kernel, owners, spread),
        in_specs=[SMEM(), VMEM(), VMEM(), HBM(), VMEM(), HBM(), ANY()],
        out_specs=[VMEM()] * (4 + len(COPIES[0])),
        out_shape=[
            jax.ShapeDtypeStruct((voxels // LANES, LANES), jnp.int32),
            jax.ShapeDtypeStruct((voxels // LANES, LANES), jnp.int32),
            jax.ShapeDtypeStruct((marks, LANES), jnp.int32),
            jax.ShapeDtypeStruct((early_rows, lanes), jnp.bfloat16),
        ]
        + room(0),
        scratch_shapes=filter_scratch(2 * time_block)
        + [
            pltpu.VMEM(filters.shape, jnp.float32),
            pltpu.VMEM((voxels // LANES, LANES), jnp.int32),
            pltpu.SemaphoreType.DMA((len(COPIES[0]),)),
            pltpu.SemaphoreType.DMA((2,)),
        ],
        compiler_params=pltpu.CompilerParams(vmem_limit_bytes=8 * MIB),
        cost_estimate=cost(0, 2 * bases * depth * copied[0]),
        name="early",
    )(
        order,
        series[0],
        series[1],
        pltpu.with_memory_space_constraint(voxel_parcel.reshape(-1, LANES), pltpu.HBM),
        table,
        pltpu.with_memory_space_constraint(filters, pltpu.HBM),
        weights,
    )
    keep_pieces(0, pieces)
    design, *pieces = pl.pallas_call(
        functools.partial(design_kernel, parts, firsts[1]),
        in_specs=[SMEM(), SMEM(), VMEM(), VMEM(), ANY()] + [VMEM()] * parts,
        out_specs=[VMEM()] * (1 + len(COPIES[1])),
        out_shape=[jax.ShapeDtypeStruct((time_len, lanes), jnp.bfloat16)] + room(1),
        scratch_shapes=filter_scratch(time_len) + [pltpu.SemaphoreType.DMA((len(COPIES[1]),))],
        compiler_params=pltpu.CompilerParams(vmem_limit_bytes=8 * MIB),
        cost_estimate=cost(0, 2 * bases * depth * copied[1]),
        name="design",
    )(order, place, early, filters, weights, *series)
    keep_pieces(1, pieces)

    half = time_block // 2
    widths, sums, sent, got = [], [], [], []
    for c in range(CHUNKS):
        after = sent[max(c - 2, 0) : max(c - 1, 0)] + got[max(c - 3, 0) : max(c - 2, 0)]
        ahead = room(c + 2)
        keep, send, *pieces = product(design, held[c], after, weights, firsts[c + 2] if ahead else 0, ahead)
        keep_pieces(c + 2, pieces)
        widths.append(keep.shape[1])
        own = [keep]
        for bit in range(bits):
            if bit > 0:
                rows = own[-1].shape[0] // 2
                send = added(own, rows, half if bit == bits - 1 else rows)
                if bit == bits - 1:
                    sent.append(send)
            own.append(lax.ppermute(send, "chan", [(i, i ^ (1 << bit)) for i in range(parts)]))
        sums.append(own)
        got.append(own[-1])
    here = lax.axis_index("vox")
    targets = jnp.arange(owners, dtype=jnp.int32) ^ here

    def pack(chunks, terms, spots, packed=(), later=()):
        sizes = [widths[c] for c in chunks]
        spec = (len(later), bits) if later else None
        if chunks[-1] == CHUNKS - 1:
            outs = [jax.ShapeDtypeStruct((half, send_cap), jnp.bfloat16)] * owners
        else:
            outs = [jax.ShapeDtypeStruct((owners, half, spread * SLOT_TILE), jnp.bfloat16)]
        more = []
        if later:
            more = [jax.ShapeDtypeStruct((half, voxels), jnp.bfloat16), pltpu.VMEM((half, voxels), jnp.bfloat16)]
        return pl.pallas_call(
            functools.partial(
                pack_kernel, spread, sizes, spots, sum(widths[: chunks[0]]) // VOX_BLOCK, spec, len(outs)
            ),
            in_specs=[SMEM(), SMEM(), VMEM(), VMEM()] + [VMEM()] * (len(packed) + len(terms) + len(later)),
            out_specs=[VMEM()] * (len(outs) + len(more)),
            out_shape=outs + more,
            scratch_shapes=[
                pltpu.VMEM((half, sum(sizes)), jnp.bfloat16),
                pltpu.VMEM((owners, half, spread * SLOT_TILE), jnp.bfloat16),
            ],
            compiler_params=pltpu.CompilerParams(vmem_limit_bytes=8 * MIB),
            cost_estimate=cost(2 * half * owners * VOX_BLOCK * sum(sizes), 4 * half * sum(sizes)),
            name="pack",
        )(targets, starts, inner, tiles, *packed, *terms, *later)

    def deliver(packed):
        got = list(packed)
        far, near = range(owners - 1, owners // 2 - 1, -1), range(owners // 2 - 1, -1, -1)
        for d in [d for pair in zip(far, near) for d in pair if d]:
            got[d] = lax.ppermute(packed[d], "vox", [(i, i ^ d) for i in range(owners)])
        return got

    def early_terms(chunks):
        return [term for c in chunks for term in sums[c]], [[(0, 0)] * len(sums[c]) for c in chunks]

    low, high = range(PACK_FIRST), range(PACK_FIRST, CHUNKS)
    packed = pack(low, *early_terms(low))
    *one, late_send, late_own = pack(
        high, *early_terms(high), packed=packed, later=[term for own in sums for term in own[:-1]]
    )
    late = lax.ppermute(late_send, "chan", [(i, i ^ (1 << (bits - 1))) for i in range(parts)])
    one = deliver(one)
    starting = [sum(widths[:c]) for c in range(CHUNKS)]
    two = pack(range(CHUNKS), [late_own, late] * CHUNKS, [[(0, first)] * 2 for first in starting])
    two = pl.pallas_call(
        gate_kernel,
        in_specs=[VMEM()] * (2 * owners),
        out_specs=[VMEM()] * owners,
        out_shape=[jax.ShapeDtypeStruct((half, send_cap), jnp.bfloat16)] * owners,
        name="gate",
    )(*two, *one)
    two = deliver(two)
    owned = pl.pallas_call(
        functools.partial(assemble_kernel, owners),
        in_specs=[SMEM()] + [VMEM()] * (2 * owners),
        out_specs=HBM(),
        out_shape=jax.ShapeDtypeStruct((owners, time_block, send_cap), jnp.bfloat16),
        scratch_shapes=[pltpu.SemaphoreType.DMA((2 * owners,))],
        name="assemble",
    )(targets, *one, *two)
    return jnp.transpose(owned, (0, 2, 1))


def gate_kernel(*refs):
    count = len(refs) // 3
    for given, out in zip(refs[:count], refs[2 * count :]):
        out[...] = given[...]


def assemble_kernel(owners, order_ref, *refs):
    *parts, out_ref, sems = refs
    half = out_ref.shape[1] // 2
    copies = []
    for i, ref in enumerate(parts):
        rows = pl.ds(i // owners * half, half)
        copies.append(pltpu.make_async_copy(ref, out_ref.at[order_ref[i % owners], rows, :], sems.at[i]))
        copies[-1].start()
    wait_all(copies)


def added(terms, first, rows):
    return sum(term[first : first + rows].astype(jnp.float32) for term in terms).astype(jnp.bfloat16)


def solution(mesh):
    return jax.shard_map(
        shards,
        mesh=mesh,
        in_specs=(P("chan", None), P(None, "chan", None), P(None, "chan", "vox"), P("vox"), P()),
        out_specs=P("vox", None, "chan"),
        check_vma=False,
    )
```

```python
import functools

import jax
import jax.numpy as jnp
from jax import lax
from jax.experimental import pallas as pl
from jax.experimental.pallas import tpu as pltpu
from jax.sharding import PartitionSpec as P

FILTER_TAPS = 16
TAP_SPACING = 2
LANES = 128
SLOT_TILE = 128
VOX_BLOCK = 256
COLUMNS = 512
ROWS = 32
CHUNKS = 4
COPIES = (((0, 4), (1, 5)), ((1, 1), (2, 4)), (), ((2, 2), (3, 1)), ((3, 2), (3, 1)))
PACK_FIRST = 2
GATE = 4
MIB = 1 << 20

VMEM = functools.partial(pl.BlockSpec, memory_space=pltpu.VMEM)
SMEM = functools.partial(pl.BlockSpec, memory_space=pltpu.SMEM)
ANY = functools.partial(pl.BlockSpec, memory_space=pl.ANY)
HBM = functools.partial(pl.BlockSpec, memory_space=pltpu.HBM)


def copy_pieces(weight_ref, piece_refs, sems, first):
    depth, copies = weight_ref.shape[1], []
    for i, ref in enumerate(piece_refs):
        if ref.shape[1] > depth:
            ref[:, depth:, :] = jnp.zeros_like(ref[:, depth:, :])
        copy = pltpu.make_async_copy(
            weight_ref.at[:, :, pl.ds(first, ref.shape[2])], ref.at[:, pl.ds(0, depth), :], sems.at[i]
        )
        copy.start()
        copies.append(copy)
        first += ref.shape[2]
    return copies


def wait_all(copies):
    for copy in copies:
        copy.wait()


def cost(flops, read):
    return pl.CostEstimate(flops=flops, bytes_accessed=read, transcendentals=0)


def places(owners, spread, parcel_ref, table_ref, inner_ref, tile_ref, start_ref):
    rows = parcel_ref.shape[0]
    parcel = parcel_ref[...]
    high, low = parcel >> 7, parcel & 127
    owner = jnp.zeros_like(parcel)
    for entry in range(table_ref.shape[0]):
        line = jnp.broadcast_to(table_ref[entry : entry + 1, :], parcel.shape)
        found = jnp.take_along_axis(line, low, axis=1, mode="promise_in_bounds")
        owner = jnp.where(high == entry, found, owner)

    def below(shape, scale=1):
        less = lax.broadcasted_iota(jnp.int32, shape, 1) < scale * lax.broadcasted_iota(jnp.int32, shape, 0)
        return less.astype(jnp.float32).astype(jnp.bfloat16)

    lane = lax.broadcasted_iota(jnp.int32, (LANES, LANES), 1)
    above = (lax.broadcasted_iota(jnp.int32, (LANES, LANES), 0) < lane).astype(jnp.float32).astype(jnp.bfloat16)
    ones = jnp.ones((LANES, LANES), jnp.bfloat16)
    marks = start_ref.shape[0]
    ahead, block_ahead = below((rows, rows)), below((marks, rows), VOX_BLOCK // LANES)
    mark_lane = lax.broadcasted_iota(jnp.int32, (marks, LANES), 1)
    dot = functools.partial(jnp.dot, preferred_element_type=jnp.float32)
    row_block = lax.broadcasted_iota(jnp.int32, (rows, rows), 0) & -(VOX_BLOCK // LANES)
    before = lax.broadcasted_iota(jnp.int32, (rows, rows), 1) < row_block
    before = before.astype(jnp.float32).astype(jnp.bfloat16)
    slots = jnp.zeros(parcel.shape, jnp.float32)
    bases = jnp.zeros(parcel.shape, jnp.float32)
    starts = jnp.zeros((marks, LANES), jnp.float32)
    for o in range(owners):
        mine = owner == o
        hot = mine.astype(jnp.float32).astype(jnp.bfloat16)
        totals = dot(hot, ones).astype(jnp.bfloat16)
        slots = jnp.where(mine, dot(hot, above) + dot(ahead, totals), slots)
        bases = jnp.where(mine, dot(before, totals), bases)
        starts = jnp.where(mark_lane == o, dot(block_ahead, totals), starts)
    slots = slots.astype(jnp.int32)
    start_ref[...] = starts.astype(jnp.int32)
    tile_ref[...] = owner * spread + (slots >> 7)
    inner_ref[...] = (slots - (bases.astype(jnp.int32) & -SLOT_TILE)) & (2 * SLOT_TILE - 1)


def clear_lead(shifted):
    lead = TAP_SPACING * FILTER_TAPS
    for s in range(shifted.shape[0]):
        shifted[s, : lead + 8, :] = jnp.zeros((lead + 8, LANES), jnp.float32)


def shift(plain, shifted):
    lead, time_len = TAP_SPACING * FILTER_TAPS, plain.shape[0]
    series = plain[...]
    for s in range(shifted.shape[0]):
        shifted[s, lead + s * TAP_SPACING : lead + s * TAP_SPACING + time_len, :] = series


def filter_rows(shifted, filter_ref, column, first):
    lead = TAP_SPACING * FILTER_TAPS
    sums = [jnp.zeros((ROWS, LANES), jnp.float32) for _ in range(filter_ref.shape[0])]
    for tap in range(FILTER_TAPS):
        delay = tap * TAP_SPACING
        start = lead + first - 8 * (delay // 8)
        if not isinstance(start, int):
            start = pl.multiple_of(start, 8)
        lagged = shifted[(delay % 8) // TAP_SPACING, pl.ds(start, ROWS), :]
        for b in range(len(sums)):
            sums[b] = sums[b] + filter_ref[b, tap : tap + 1, column] * lagged
    return sums


def lane_tile(tile):
    return pl.ds(pl.multiple_of(tile * LANES, LANES), LANES)


def early_kernel(owners, spread, order_ref, own_ref, pair_ref, parcel_hbm, table_ref, filter_hbm, weight_ref, *refs):
    inner_ref, tile_ref, start_ref, design_ref, *piece_refs, plain, shifted, filter_ref, parcel_ref, sems, small_sems = refs
    load_filter = pltpu.make_async_copy(filter_hbm, filter_ref, small_sems.at[0])
    load_parcel = pltpu.make_async_copy(parcel_hbm, parcel_ref, small_sems.at[1])
    load_filter.start()
    load_parcel.start()
    copies = copy_pieces(weight_ref, piece_refs, sems, 0)
    block, width = own_ref.shape
    core = lax.rem(order_ref[0], 2)
    own = pl.ds(pl.multiple_of(core * block, block), block)
    pair = pl.ds(pl.multiple_of((1 - core) * block, block), block)
    clear_lead(shifted)
    load_filter.wait()

    def columns(tile, carry):
        column = lane_tile(tile)
        plain[own, :] = own_ref[:, column].astype(jnp.float32)
        plain[pair, :] = pair_ref[:, column].astype(jnp.float32)
        shift(plain, shifted)
        for first in range(ROWS, 2 * block, ROWS):
            for b, rows in enumerate(filter_rows(shifted, filter_ref, column, first)):
                lanes = pl.ds(pl.multiple_of(b * width + tile * LANES, LANES), LANES)
                design_ref[first - ROWS : first, lanes] = rows.astype(jnp.bfloat16)
        return carry

    lax.fori_loop(0, width // LANES, columns, 0)
    load_parcel.wait()
    places(owners, spread, parcel_ref, table_ref, inner_ref, tile_ref, start_ref)
    wait_all(copies)


def design_kernel(parts, first, order_ref, place_ref, early_ref, filter_ref, weight_ref, *refs):
    series_refs, (design_ref, *piece_refs, plain, shifted, sems) = refs[:parts], refs[parts:]
    copies = copy_pieces(weight_ref, piece_refs, sems, first)
    block, width = series_refs[0].shape
    chip = order_ref[0] >> 1
    clear_lead(shifted)

    def place(part, inner):
        return pl.ds(pl.multiple_of(place_ref[part] * block + inner, ROWS), ROWS)

    for first in range(ROWS, 2 * block, ROWS):
        row = place(2 * chip + first // block, first % block)
        design_ref[row, :] = early_ref[first - ROWS : first, :]

    def columns(tile, carry):
        column = lane_tile(tile)
        for d in range(parts):
            row = pl.ds(pl.multiple_of(order_ref[d] * block, block), block)
            plain[row, :] = series_refs[d][:, column].astype(jnp.float32)
        shift(plain, shifted)
        for other in range(parts // 2):
            for inner in range(0, 2 * block if other else ROWS, ROWS):
                part = 2 * (chip ^ other) + inner // block
                start = part * block + inner % block
                row = place(part, inner % block)
                for b, rows in enumerate(filter_rows(shifted, filter_ref, column, start)):
                    lanes = pl.ds(pl.multiple_of(b * width + tile * LANES, LANES), LANES)
                    design_ref[row, lanes] = rows.astype(jnp.bfloat16)
        return carry

    lax.fori_loop(0, width // LANES, columns, 0)
    wait_all(copies)


def filter_scratch(time_len):
    return [
        pltpu.VMEM((time_len, LANES), jnp.float32),
        pltpu.VMEM((8 // TAP_SPACING, time_len + TAP_SPACING * FILTER_TAPS + 8, LANES), jnp.float32),
    ]


def product_kernel(taken, extra, first, design_ref, *refs):
    weight_refs, refs = refs[:taken], refs[taken + extra :]
    copies = []
    if first is not None:
        weight_ref, keep_ref, send_ref, *piece_refs, sems = refs
        copies = copy_pieces(weight_ref, piece_refs, sems, first)
    else:
        keep_ref, send_ref = refs
    half, at = keep_ref.shape[0], 0
    for ref in weight_refs:
        for start in range(0, ref.shape[2], COLUMNS):
            weight = ref[:, :, start : min(start + COLUMNS, ref.shape[2])]
            weight = weight.reshape(-1, weight.shape[2])
            total = jnp.dot(design_ref[...], weight, preferred_element_type=jnp.float32)
            columns = slice(at, at + weight.shape[1])
            keep_ref[:, columns] = total[:half].astype(jnp.bfloat16)
            send_ref[:, columns] = total[half:].astype(jnp.bfloat16)
            at += weight.shape[1]
    wait_all(copies)


def product(design, taken, after, weights, first, ahead):
    time_len, lanes = design.shape
    width = sum(piece.shape[2] for piece in taken)
    half = jax.ShapeDtypeStruct((time_len // 2, width), jnp.bfloat16)
    return pl.pallas_call(
        functools.partial(product_kernel, len(taken), len(after), first if ahead else None),
        in_specs=[VMEM()] * (1 + len(taken)) + [ANY()] * (len(after) + bool(ahead)),
        out_specs=[VMEM()] * (2 + len(ahead)),
        out_shape=[half, half] + ahead,
        scratch_shapes=[pltpu.SemaphoreType.DMA((len(ahead),))] if ahead else [],
        compiler_params=pltpu.CompilerParams(vmem_limit_bytes=8 * MIB),
        cost_estimate=cost(2 * time_len * lanes * width, 2 * lanes * width),
        name="product",
    )(design, *taken, *after, *([weights] if ahead else []))


def add_rows(terms, each, first, out_ref):
    at, rows = 0, out_ref.shape[0]
    for c in range(0, len(terms), each):
        chunk, width = terms[c : c + each], terms[c].shape[1]
        total = sum(term[first : first + rows, :].astype(jnp.float32) for term in chunk)
        out_ref[:, at : at + width] = total.astype(jnp.bfloat16)
        at += width


def pack_kernel(spread, widths, places, first, later, outs, order_ref, start_ref, inner_ref, tile_ref, *refs):
    *refs, summed, packed = refs
    if later:
        count, each = later
        *refs, send_ref, keep_ref = refs
    terms, out_refs = refs[: len(refs) - outs], refs[len(refs) - outs :]
    if later:
        rows = packed.shape[1]
        add_rows(terms[-count:], each, 3 * rows, send_ref)
        add_rows(terms[-count:], each, rows, keep_ref)
        terms = terms[:-count]
    owners, rows = packed.shape[:2]
    if first:
        packed[...] = terms.pop(0)[...]
    else:
        packed[...] = jnp.zeros_like(packed)
    at = 0
    for width, spots in zip(widths, places):
        total = 0.0
        for row, column in spots:
            total = total + terms.pop(0)[row : row + rows, column : column + width].astype(jnp.float32)
        summed[:, at : at + width] = total.astype(jnp.bfloat16)
        at += width
    step = VOX_BLOCK // LANES
    slot_rows = lax.broadcasted_iota(jnp.int32, (2 * SLOT_TILE, VOX_BLOCK), 0)

    def moves(index, far):
        block = first + index
        values = summed[:, pl.ds(pl.multiple_of(index * VOX_BLOCK, VOX_BLOCK), VOX_BLOCK)]
        tiles, inner = (
            jnp.concatenate([ref[pl.ds(block * step + i, 1), :] for i in range(step)], axis=1)
            for ref in (tile_ref, inner_ref)
        )
        onehot = jnp.where(inner == slot_rows, 1.0, 0.0).astype(jnp.bfloat16)
        low = [start_ref[block, o] >> 7 for o in range(owners)]
        chosen = []
        for o in range(owners):
            tile = tiles - (o * spread + low[o])
            hit = jnp.where((tile == 2) if far else ((tile == 0) | (tile == 1)), 1.0, 0.0)
            chosen.append(values * hit.astype(jnp.bfloat16))
        moved = lax.dot_general(
            jnp.concatenate(chosen, axis=0), onehot, (((1,), (1,)), ((), ())), preferred_element_type=jnp.float32
        )
        moved = moved.astype(jnp.bfloat16)
        out = []
        for o in range(owners):
            here = moved[o * rows : (o + 1) * rows]
            tile, here = (low[o] + 2, here[:, :SLOT_TILE]) if far else (low[o], here)
            lanes = pl.ds(pl.multiple_of(tile * SLOT_TILE, SLOT_TILE), here.shape[1])
            out.append((o, lanes, here))
        high = [(start_ref[block + 1, o] - 1) >> 7 for o in range(owners)]
        return out, functools.reduce(jnp.maximum, [high[o] - low[o] for o in range(owners)])

    def add(targets):
        sums = [packed[owner, :, lanes] + moved for owner, lanes, moved in targets]
        for (owner, lanes, _), total in zip(targets, sums):
            packed[owner, :, lanes] = total

    def blocks(indices):
        found = [moves(index, False) for index in indices]
        for targets, _ in found:
            add(targets)
        for index, (_, longest) in zip(indices, found):

            @pl.when(longest > 1)
            def _():
                add(moves(index, True)[0])

    count = sum(widths) // VOX_BLOCK

    def two(i, carry):
        blocks([2 * i, 2 * i + 1])
        return carry

    lax.fori_loop(0, count // 2, two, 0)
    if count % 2:
        blocks([count - 1])
    if outs == 1:
        out_refs[0][...] = packed[...]
    else:
        for d, ref in enumerate(out_refs):
            ref[...] = packed[order_ref[d], :, : ref.shape[1]]


def shards(features, hrf_filters, weights, voxel_parcel, parcel_owner):
    owners, parts = lax.axis_size("vox"), lax.axis_size("chan")
    me = lax.axis_index("chan")
    voxels = voxel_parcel.shape[0]
    send_cap = 2 * voxels // owners
    bases, depth, _ = weights.shape
    blocks = voxels // VOX_BLOCK
    time_block = features.shape[0]
    time_len = time_block * parts

    series = [lax.dynamic_slice_in_dim(features, (me ^ d) * depth, depth, 1) for d in range(parts)]
    for d in range(1, parts):
        series[d] = lax.ppermute(series[d], "chan", [(i, i ^ d) for i in range(parts)])
    filters = jnp.transpose(hrf_filters, (0, 2, 1))
    spare = -depth % LANES
    lanes = bases * (depth + spare)
    unit = voxels // sum(units for pieces in COPIES for _, units in pieces)
    copied = [unit * sum(units for _, units in pieces) for pieces in COPIES]
    firsts = [sum(copied[:i]) for i in range(len(copied))]
    held = [[] for _ in range(CHUNKS)]

    def room(i):
        if i >= len(COPIES):
            return []
        return [pltpu.VMEM((bases, depth + spare, unit * units), jnp.bfloat16) for _, units in COPIES[i]]

    def keep_pieces(i, pieces):
        for (chunk, _), piece in zip(COPIES[i] if i < len(COPIES) else (), pieces):
            held[chunk].append(piece)

    if spare:
        series = [jnp.pad(part, ((0, 0), (0, spare))) for part in series]
        filters = jnp.pad(filters, ((0, 0), (0, 0), (0, spare)))

    table_rows = -(-parcel_owner.shape[0] // LANES)
    table = jnp.pad(parcel_owner, (0, table_rows * LANES - parcel_owner.shape[0])).reshape(table_rows, LANES)
    marks = -(-(blocks + 1) // 8) * 8
    spread = send_cap // SLOT_TILE + 3
    bits = parts.bit_length() - 1
    order = jnp.arange(parts, dtype=jnp.int32) ^ me
    place = sum(((order >> bit) & 1) << (bits - 1 - bit) for bit in range(bits)).astype(jnp.int32)

    early_rows = 2 * time_block - ROWS
    inner, tiles, starts, early, *pieces = pl.pallas_call(
        functools.partial(early_kernel, owners, spread),
        in_specs=[SMEM(), VMEM(), VMEM(), HBM(), VMEM(), HBM(), ANY()],
        out_specs=[VMEM()] * (4 + len(COPIES[0])),
        out_shape=[
            jax.ShapeDtypeStruct((voxels // LANES, LANES), jnp.int32),
            jax.ShapeDtypeStruct((voxels // LANES, LANES), jnp.int32),
            jax.ShapeDtypeStruct((marks, LANES), jnp.int32),
            jax.ShapeDtypeStruct((early_rows, lanes), jnp.bfloat16),
        ]
        + room(0),
        scratch_shapes=filter_scratch(2 * time_block)
        + [
            pltpu.VMEM(filters.shape, jnp.float32),
            pltpu.VMEM((voxels // LANES, LANES), jnp.int32),
            pltpu.SemaphoreType.DMA((len(COPIES[0]),)),
            pltpu.SemaphoreType.DMA((2,)),
        ],
        compiler_params=pltpu.CompilerParams(vmem_limit_bytes=8 * MIB),
        cost_estimate=cost(0, 2 * bases * depth * copied[0]),
        name="early",
    )(
        order,
        series[0],
        series[1],
        pltpu.with_memory_space_constraint(voxel_parcel.reshape(-1, LANES), pltpu.HBM),
        table,
        pltpu.with_memory_space_constraint(filters, pltpu.HBM),
        weights,
    )
    keep_pieces(0, pieces)
    design, *pieces = pl.pallas_call(
        functools.partial(design_kernel, parts, firsts[1]),
        in_specs=[SMEM(), SMEM(), VMEM(), VMEM(), ANY()] + [VMEM()] * parts,
        out_specs=[VMEM()] * (1 + len(COPIES[1])),
        out_shape=[jax.ShapeDtypeStruct((time_len, lanes), jnp.bfloat16)] + room(1),
        scratch_shapes=filter_scratch(time_len) + [pltpu.SemaphoreType.DMA((len(COPIES[1]),))],
        compiler_params=pltpu.CompilerParams(vmem_limit_bytes=8 * MIB),
        cost_estimate=cost(0, 2 * bases * depth * copied[1]),
        name="design",
    )(order, place, early, filters, weights, *series)
    keep_pieces(1, pieces)

    half = time_block // 2
    widths, sums, sent, got = [], [], [], []
    for c in range(CHUNKS):
        after = sent[max(c - 2, 0) : max(c - 1, 0)] + got[max(c - 3, 0) : max(c - 2, 0)]
        ahead = room(c + 2)
        keep, send, *pieces = product(design, held[c], after, weights, firsts[c + 2] if ahead else 0, ahead)
        keep_pieces(c + 2, pieces)
        widths.append(keep.shape[1])
        own = [keep]
        for bit in range(bits):
            if bit > 0:
                rows = own[-1].shape[0] // 2
                send = added(own, rows, half if bit == bits - 1 else rows)
                if bit == bits - 1:
                    sent.append(send)
            own.append(lax.ppermute(send, "chan", [(i, i ^ (1 << bit)) for i in range(parts)]))
        sums.append(own)
        got.append(own[-1])
    here = lax.axis_index("vox")
    targets = jnp.arange(owners, dtype=jnp.int32) ^ here

    def pack(chunks, terms, spots, packed=(), later=()):
        sizes = [widths[c] for c in chunks]
        spec = (len(later), bits) if later else None
        if chunks[-1] == CHUNKS - 1:
            outs = [pltpu.VMEM((half, send_cap), jnp.bfloat16)] * owners
        else:
            outs = [jax.ShapeDtypeStruct((owners, half, spread * SLOT_TILE), jnp.bfloat16)]
        more = []
        if later:
            more = [jax.ShapeDtypeStruct((half, voxels), jnp.bfloat16), pltpu.VMEM((half, voxels), jnp.bfloat16)]
        return pl.pallas_call(
            functools.partial(
                pack_kernel, spread, sizes, spots, sum(widths[: chunks[0]]) // VOX_BLOCK, spec, len(outs)
            ),
            in_specs=[SMEM(), SMEM(), VMEM(), VMEM()] + [VMEM()] * (len(packed) + len(terms) + len(later)),
            out_specs=[VMEM()] * (len(outs) + len(more)),
            out_shape=outs + more,
            scratch_shapes=[
                pltpu.VMEM((half, sum(sizes)), jnp.bfloat16),
                pltpu.VMEM((owners, half, spread * SLOT_TILE), jnp.bfloat16),
            ],
            compiler_params=pltpu.CompilerParams(vmem_limit_bytes=8 * MIB),
            cost_estimate=cost(2 * half * owners * VOX_BLOCK * sum(sizes), 4 * half * sum(sizes)),
            name="pack",
        )(targets, starts, inner, tiles, *packed, *terms, *later)

    far, near = range(owners - 1, owners // 2 - 1, -1), range(owners // 2 - 1, -1, -1)
    turns = [d for pair in zip(far, near) for d in pair if d]

    def deliver(packed):
        got = list(packed)
        for d in turns:
            got[d] = lax.ppermute(packed[d], "vox", [(i, i ^ d) for i in range(owners)])
        return got

    def early_terms(chunks):
        return [term for c in chunks for term in sums[c]], [[(0, 0)] * len(sums[c]) for c in chunks]

    low, high = range(PACK_FIRST), range(PACK_FIRST, CHUNKS)
    packed = pack(low, *early_terms(low))
    *one, late_send, late_own = pack(
        high, *early_terms(high), packed=packed, later=[term for own in sums for term in own[:-1]]
    )
    late = lax.ppermute(late_send, "chan", [(i, i ^ (1 << (bits - 1))) for i in range(parts)])
    one = deliver(one)
    starting = [sum(widths[:c]) for c in range(CHUNKS)]
    two = pack(range(CHUNKS), [late_own, late] * CHUNKS, [[(0, first)] * 2 for first in starting])
    two = pl.pallas_call(
        gate_kernel,
        in_specs=[VMEM()] * (owners + GATE),
        out_specs=[VMEM()] * owners,
        out_shape=[pltpu.VMEM((half, send_cap), jnp.bfloat16)] * owners,
        name="gate",
    )(*two, *(one[d] for d in turns[:GATE]))
    two = deliver(two)
    owned = None
    for first, got in ((0, one), (half, two)):
        given = [] if owned is None else [owned]
        owned = pl.pallas_call(
            functools.partial(assemble_kernel, owners, first),
            in_specs=[SMEM()] + [VMEM()] * owners + [HBM()] * len(given),
            out_specs=HBM(),
            out_shape=jax.ShapeDtypeStruct((owners, time_block, send_cap), jnp.bfloat16),
            scratch_shapes=[pltpu.SemaphoreType.DMA((owners,))],
            input_output_aliases={1 + owners: 0} if given else {},
            name="assemble",
        )(targets, *got, *given)
    return jnp.transpose(owned, (0, 2, 1))


def gate_kernel(*refs):
    count = (len(refs) - GATE) // 2
    for given, out in zip(refs[:count], refs[count + GATE :]):
        out[...] = given[...]


def assemble_kernel(owners, first, order_ref, *refs):
    parts, (out_ref, sems) = refs[:owners], refs[-2:]
    copies = []
    for i, ref in enumerate(parts):
        rows = pl.ds(first, ref.shape[0])
        copies.append(pltpu.make_async_copy(ref, out_ref.at[order_ref[i], rows, :], sems.at[i]))
        copies[-1].start()
    wait_all(copies)


def added(terms, first, rows):
    return sum(term[first : first + rows].astype(jnp.float32) for term in terms).astype(jnp.bfloat16)


def solution(mesh):
    return jax.shard_map(
        shards,
        mesh=mesh,
        in_specs=(P("chan", None), P(None, "chan", None), P(None, "chan", "vox"), P("vox"), P()),
        out_specs=P("vox", None, "chan"),
        check_vma=False,
    )
```

```python
import functools

import jax
import jax.numpy as jnp
from jax import lax
from jax.experimental import pallas as pl
from jax.experimental.pallas import tpu as pltpu
from jax.sharding import PartitionSpec as P

FILTER_TAPS = 16
TAP_SPACING = 2
LANES = 128
SLOT_TILE = 128
VOX_BLOCK = 256
COLUMNS = 512
ROWS = 32
CHUNKS = 4
COPIES = (((0, 4), (1, 5)), ((1, 1), (2, 4)), (), ((2, 2), (3, 1)), ((3, 2), (3, 1)))
PACK_FIRST = 2
GATE = 4
MIB = 1 << 20

VMEM = functools.partial(pl.BlockSpec, memory_space=pltpu.VMEM)
SMEM = functools.partial(pl.BlockSpec, memory_space=pltpu.SMEM)
ANY = functools.partial(pl.BlockSpec, memory_space=pl.ANY)
HBM = functools.partial(pl.BlockSpec, memory_space=pltpu.HBM)


def copy_pieces(weight_ref, piece_refs, sems, first):
    depth, copies = weight_ref.shape[1], []
    for i, ref in enumerate(piece_refs):
        if ref.shape[1] > depth:
            ref[:, depth:, :] = jnp.zeros_like(ref[:, depth:, :])
        copy = pltpu.make_async_copy(
            weight_ref.at[:, :, pl.ds(first, ref.shape[2])], ref.at[:, pl.ds(0, depth), :], sems.at[i]
        )
        copy.start()
        copies.append(copy)
        first += ref.shape[2]
    return copies


def wait_all(copies):
    for copy in copies:
        copy.wait()


def cost(flops, read):
    return pl.CostEstimate(flops=flops, bytes_accessed=read, transcendentals=0)


def places(owners, spread, parcel_ref, table_ref, inner_ref, tile_ref, start_ref):
    rows = parcel_ref.shape[0]
    parcel = parcel_ref[...]
    high, low = parcel >> 7, parcel & 127
    owner = jnp.zeros_like(parcel)
    for entry in range(table_ref.shape[0]):
        line = jnp.broadcast_to(table_ref[entry : entry + 1, :], parcel.shape)
        found = jnp.take_along_axis(line, low, axis=1, mode="promise_in_bounds")
        owner = jnp.where(high == entry, found, owner)

    def below(shape, scale=1):
        less = lax.broadcasted_iota(jnp.int32, shape, 1) < scale * lax.broadcasted_iota(jnp.int32, shape, 0)
        return less.astype(jnp.float32).astype(jnp.bfloat16)

    lane = lax.broadcasted_iota(jnp.int32, (LANES, LANES), 1)
    above = (lax.broadcasted_iota(jnp.int32, (LANES, LANES), 0) < lane).astype(jnp.float32).astype(jnp.bfloat16)
    ones = jnp.ones((LANES, LANES), jnp.bfloat16)
    marks = start_ref.shape[0]
    ahead, block_ahead = below((rows, rows)), below((marks, rows), VOX_BLOCK // LANES)
    mark_lane = lax.broadcasted_iota(jnp.int32, (marks, LANES), 1)
    dot = functools.partial(jnp.dot, preferred_element_type=jnp.float32)
    row_block = lax.broadcasted_iota(jnp.int32, (rows, rows), 0) & -(VOX_BLOCK // LANES)
    before = lax.broadcasted_iota(jnp.int32, (rows, rows), 1) < row_block
    before = before.astype(jnp.float32).astype(jnp.bfloat16)
    slots = jnp.zeros(parcel.shape, jnp.float32)
    bases = jnp.zeros(parcel.shape, jnp.float32)
    starts = jnp.zeros((marks, LANES), jnp.float32)
    for o in range(owners):
        mine = owner == o
        hot = mine.astype(jnp.float32).astype(jnp.bfloat16)
        totals = dot(hot, ones).astype(jnp.bfloat16)
        slots = jnp.where(mine, dot(hot, above) + dot(ahead, totals), slots)
        bases = jnp.where(mine, dot(before, totals), bases)
        starts = jnp.where(mark_lane == o, dot(block_ahead, totals), starts)
    slots = slots.astype(jnp.int32)
    start_ref[...] = starts.astype(jnp.int32)
    tile_ref[...] = owner * spread + (slots >> 7)
    inner_ref[...] = (slots - (bases.astype(jnp.int32) & -SLOT_TILE)) & (2 * SLOT_TILE - 1)


def clear_lead(shifted):
    lead = TAP_SPACING * FILTER_TAPS
    for s in range(shifted.shape[0]):
        shifted[s, : lead + 8, :] = jnp.zeros((lead + 8, LANES), jnp.float32)


def shift(plain, shifted):
    lead, time_len = TAP_SPACING * FILTER_TAPS, plain.shape[0]
    series = plain[...]
    for s in range(shifted.shape[0]):
        shifted[s, lead + s * TAP_SPACING : lead + s * TAP_SPACING + time_len, :] = series


def filter_rows(shifted, filter_ref, column, first):
    lead = TAP_SPACING * FILTER_TAPS
    sums = [jnp.zeros((ROWS, LANES), jnp.float32) for _ in range(filter_ref.shape[0])]
    for tap in range(FILTER_TAPS):
        delay = tap * TAP_SPACING
        start = lead + first - 8 * (delay // 8)
        if not isinstance(start, int):
            start = pl.multiple_of(start, 8)
        lagged = shifted[(delay % 8) // TAP_SPACING, pl.ds(start, ROWS), :]
        for b in range(len(sums)):
            sums[b] = sums[b] + filter_ref[b, tap : tap + 1, column] * lagged
    return sums


def lane_tile(tile):
    return pl.ds(pl.multiple_of(tile * LANES, LANES), LANES)


def early_kernel(owners, spread, order_ref, own_ref, pair_ref, parcel_hbm, table_ref, filter_hbm, weight_ref, *refs):
    inner_ref, tile_ref, start_ref, design_ref, *piece_refs, plain, shifted, filter_ref, parcel_ref, sems, small_sems = refs
    load_filter = pltpu.make_async_copy(filter_hbm, filter_ref, small_sems.at[0])
    load_parcel = pltpu.make_async_copy(parcel_hbm, parcel_ref, small_sems.at[1])
    load_filter.start()
    load_parcel.start()
    copies = copy_pieces(weight_ref, piece_refs, sems, 0)
    block, width = own_ref.shape
    core = lax.rem(order_ref[0], 2)
    own = pl.ds(pl.multiple_of(core * block, block), block)
    pair = pl.ds(pl.multiple_of((1 - core) * block, block), block)
    clear_lead(shifted)
    load_filter.wait()

    def columns(tile, carry):
        column = lane_tile(tile)
        plain[own, :] = own_ref[:, column].astype(jnp.float32)
        plain[pair, :] = pair_ref[:, column].astype(jnp.float32)
        shift(plain, shifted)
        for first in range(ROWS, 2 * block, ROWS):
            for b, rows in enumerate(filter_rows(shifted, filter_ref, column, first)):
                lanes = pl.ds(pl.multiple_of(b * width + tile * LANES, LANES), LANES)
                design_ref[first - ROWS : first, lanes] = rows.astype(jnp.bfloat16)
        return carry

    lax.fori_loop(0, width // LANES, columns, 0)
    load_parcel.wait()
    places(owners, spread, parcel_ref, table_ref, inner_ref, tile_ref, start_ref)
    wait_all(copies)


def design_kernel(parts, first, order_ref, place_ref, early_ref, filter_ref, weight_ref, *refs):
    series_refs, (design_ref, *piece_refs, plain, shifted, sems) = refs[:parts], refs[parts:]
    copies = copy_pieces(weight_ref, piece_refs, sems, first)
    block, width = series_refs[0].shape
    chip = order_ref[0] >> 1
    clear_lead(shifted)

    def place(part, inner):
        return pl.ds(pl.multiple_of(place_ref[part] * block + inner, ROWS), ROWS)

    for first in range(ROWS, 2 * block, ROWS):
        row = place(2 * chip + first // block, first % block)
        design_ref[row, :] = early_ref[first - ROWS : first, :]

    def columns(tile, carry):
        column = lane_tile(tile)
        for d in range(parts):
            row = pl.ds(pl.multiple_of(order_ref[d] * block, block), block)
            plain[row, :] = series_refs[d][:, column].astype(jnp.float32)
        shift(plain, shifted)
        for other in range(parts // 2):
            for inner in range(0, 2 * block if other else ROWS, ROWS):
                part = 2 * (chip ^ other) + inner // block
                start = part * block + inner % block
                row = place(part, inner % block)
                for b, rows in enumerate(filter_rows(shifted, filter_ref, column, start)):
                    lanes = pl.ds(pl.multiple_of(b * width + tile * LANES, LANES), LANES)
                    design_ref[row, lanes] = rows.astype(jnp.bfloat16)
        return carry

    lax.fori_loop(0, width // LANES, columns, 0)
    wait_all(copies)


def filter_scratch(time_len):
    return [
        pltpu.VMEM((time_len, LANES), jnp.float32),
        pltpu.VMEM((8 // TAP_SPACING, time_len + TAP_SPACING * FILTER_TAPS + 8, LANES), jnp.float32),
    ]


def product_kernel(taken, extra, first, design_ref, *refs):
    weight_refs, refs = refs[:taken], refs[taken + extra :]
    copies = []
    if first is not None:
        weight_ref, keep_ref, send_ref, *piece_refs, sems = refs
        copies = copy_pieces(weight_ref, piece_refs, sems, first)
    else:
        keep_ref, send_ref = refs
    half, at = keep_ref.shape[0], 0
    for ref in weight_refs:
        for start in range(0, ref.shape[2], COLUMNS):
            weight = ref[:, :, start : min(start + COLUMNS, ref.shape[2])]
            weight = weight.reshape(-1, weight.shape[2])
            total = jnp.dot(design_ref[...], weight, preferred_element_type=jnp.float32)
            columns = slice(at, at + weight.shape[1])
            keep_ref[:, columns] = total[:half].astype(jnp.bfloat16)
            send_ref[:, columns] = total[half:].astype(jnp.bfloat16)
            at += weight.shape[1]
    wait_all(copies)


def product(design, taken, after, weights, first, ahead):
    time_len, lanes = design.shape
    width = sum(piece.shape[2] for piece in taken)
    half = jax.ShapeDtypeStruct((time_len // 2, width), jnp.bfloat16)
    return pl.pallas_call(
        functools.partial(product_kernel, len(taken), len(after), first if ahead else None),
        in_specs=[VMEM()] * (1 + len(taken)) + [ANY()] * (len(after) + bool(ahead)),
        out_specs=[VMEM()] * (2 + len(ahead)),
        out_shape=[half, half] + ahead,
        scratch_shapes=[pltpu.SemaphoreType.DMA((len(ahead),))] if ahead else [],
        compiler_params=pltpu.CompilerParams(vmem_limit_bytes=8 * MIB),
        cost_estimate=cost(2 * time_len * lanes * width, 2 * lanes * width),
        name="product",
    )(design, *taken, *after, *([weights] if ahead else []))


def add_rows(terms, each, first, out_ref):
    at, rows = 0, out_ref.shape[0]
    for c in range(0, len(terms), each):
        chunk, width = terms[c : c + each], terms[c].shape[1]
        total = sum(term[first : first + rows, :].astype(jnp.float32) for term in chunk)
        out_ref[:, at : at + width] = total.astype(jnp.bfloat16)
        at += width


def pack_kernel(spread, widths, places, first, later, outs, order_ref, start_ref, inner_ref, tile_ref, *refs):
    *refs, summed, packed = refs
    if later:
        count, each = later
        *refs, send_ref, keep_ref = refs
    terms, out_refs = refs[: len(refs) - outs], refs[len(refs) - outs :]
    if later:
        rows = packed.shape[1]
        add_rows(terms[-count:], each, 3 * rows, send_ref)
        add_rows(terms[-count:], each, rows, keep_ref)
        terms = terms[:-count]
    owners, rows = packed.shape[:2]
    if first:
        packed[...] = terms.pop(0)[...]
    else:
        packed[...] = jnp.zeros_like(packed)
    at = 0
    for width, spots in zip(widths, places):
        total = 0.0
        for row, column in spots:
            total = total + terms.pop(0)[row : row + rows, column : column + width].astype(jnp.float32)
        summed[:, at : at + width] = total.astype(jnp.bfloat16)
        at += width
    step = VOX_BLOCK // LANES
    slot_rows = lax.broadcasted_iota(jnp.int32, (2 * SLOT_TILE, VOX_BLOCK), 0)

    def moves(index, far):
        block = first + index
        values = summed[:, pl.ds(pl.multiple_of(index * VOX_BLOCK, VOX_BLOCK), VOX_BLOCK)]
        tiles, inner = (
            jnp.concatenate([ref[pl.ds(block * step + i, 1), :] for i in range(step)], axis=1)
            for ref in (tile_ref, inner_ref)
        )
        onehot = jnp.where(inner == slot_rows, 1.0, 0.0).astype(jnp.bfloat16)
        low = [start_ref[block, o] >> 7 for o in range(owners)]
        chosen = []
        for o in range(owners):
            tile = tiles - (o * spread + low[o])
            hit = jnp.where((tile == 2) if far else ((tile == 0) | (tile == 1)), 1.0, 0.0)
            chosen.append(values * hit.astype(jnp.bfloat16))
        moved = lax.dot_general(
            jnp.concatenate(chosen, axis=0), onehot, (((1,), (1,)), ((), ())), preferred_element_type=jnp.float32
        )
        moved = moved.astype(jnp.bfloat16)
        out = []
        for o in range(owners):
            here = moved[o * rows : (o + 1) * rows]
            tile, here = (low[o] + 2, here[:, :SLOT_TILE]) if far else (low[o], here)
            lanes = pl.ds(pl.multiple_of(tile * SLOT_TILE, SLOT_TILE), here.shape[1])
            out.append((o, lanes, here))
        high = [(start_ref[block + 1, o] - 1) >> 7 for o in range(owners)]
        return out, functools.reduce(jnp.maximum, [high[o] - low[o] for o in range(owners)])

    def add(targets):
        sums = [packed[owner, :, lanes] + moved for owner, lanes, moved in targets]
        for (owner, lanes, _), total in zip(targets, sums):
            packed[owner, :, lanes] = total

    def blocks(indices):
        found = [moves(index, False) for index in indices]
        for targets, _ in found:
            add(targets)
        for index, (_, longest) in zip(indices, found):

            @pl.when(longest > 1)
            def _():
                add(moves(index, True)[0])

    count = sum(widths) // VOX_BLOCK

    def two(i, carry):
        blocks([2 * i, 2 * i + 1])
        return carry

    lax.fori_loop(0, count // 2, two, 0)
    if count % 2:
        blocks([count - 1])
    if outs == 1:
        out_refs[0][...] = packed[...]
    else:
        for d, ref in enumerate(out_refs):
            ref[...] = packed[order_ref[d], :, : ref.shape[1]]


def shards(features, hrf_filters, weights, voxel_parcel, parcel_owner):
    owners, parts = lax.axis_size("vox"), lax.axis_size("chan")
    me = lax.axis_index("chan")
    voxels = voxel_parcel.shape[0]
    send_cap = 2 * voxels // owners
    bases, depth, _ = weights.shape
    blocks = voxels // VOX_BLOCK
    time_block = features.shape[0]
    time_len = time_block * parts

    series = [lax.dynamic_slice_in_dim(features, (me ^ d) * depth, depth, 1) for d in range(parts)]
    for d in range(1, parts):
        series[d] = lax.ppermute(series[d], "chan", [(i, i ^ d) for i in range(parts)])
    filters = jnp.transpose(hrf_filters, (0, 2, 1))
    spare = -depth % LANES
    lanes = bases * (depth + spare)
    unit = voxels // sum(units for pieces in COPIES for _, units in pieces)
    copied = [unit * sum(units for _, units in pieces) for pieces in COPIES]
    firsts = [sum(copied[:i]) for i in range(len(copied))]
    held = [[] for _ in range(CHUNKS)]

    def room(i):
        if i >= len(COPIES):
            return []
        return [pltpu.VMEM((bases, depth + spare, unit * units), jnp.bfloat16) for _, units in COPIES[i]]

    def keep_pieces(i, pieces):
        for (chunk, _), piece in zip(COPIES[i] if i < len(COPIES) else (), pieces):
            held[chunk].append(piece)

    if spare:
        series = [jnp.pad(part, ((0, 0), (0, spare))) for part in series]
        filters = jnp.pad(filters, ((0, 0), (0, 0), (0, spare)))

    table_rows = -(-parcel_owner.shape[0] // LANES)
    table = jnp.pad(parcel_owner, (0, table_rows * LANES - parcel_owner.shape[0])).reshape(table_rows, LANES)
    marks = -(-(blocks + 1) // 8) * 8
    spread = send_cap // SLOT_TILE + 3
    bits = parts.bit_length() - 1
    order = jnp.arange(parts, dtype=jnp.int32) ^ me
    place = sum(((order >> bit) & 1) << (bits - 1 - bit) for bit in range(bits)).astype(jnp.int32)

    early_rows = 2 * time_block - ROWS
    inner, tiles, starts, early, *pieces = pl.pallas_call(
        functools.partial(early_kernel, owners, spread),
        in_specs=[SMEM(), VMEM(), VMEM(), HBM(), VMEM(), HBM(), ANY()],
        out_specs=[VMEM()] * (4 + len(COPIES[0])),
        out_shape=[
            jax.ShapeDtypeStruct((voxels // LANES, LANES), jnp.int32),
            jax.ShapeDtypeStruct((voxels // LANES, LANES), jnp.int32),
            jax.ShapeDtypeStruct((marks, LANES), jnp.int32),
            jax.ShapeDtypeStruct((early_rows, lanes), jnp.bfloat16),
        ]
        + room(0),
        scratch_shapes=filter_scratch(2 * time_block)
        + [
            pltpu.VMEM(filters.shape, jnp.float32),
            pltpu.VMEM((voxels // LANES, LANES), jnp.int32),
            pltpu.SemaphoreType.DMA((len(COPIES[0]),)),
            pltpu.SemaphoreType.DMA((2,)),
        ],
        compiler_params=pltpu.CompilerParams(vmem_limit_bytes=8 * MIB),
        cost_estimate=cost(0, 2 * bases * depth * copied[0]),
        name="early",
    )(
        order,
        series[0],
        series[1],
        pltpu.with_memory_space_constraint(voxel_parcel.reshape(-1, LANES), pltpu.HBM),
        table,
        pltpu.with_memory_space_constraint(filters, pltpu.HBM),
        weights,
    )
    keep_pieces(0, pieces)
    design, *pieces = pl.pallas_call(
        functools.partial(design_kernel, parts, firsts[1]),
        in_specs=[SMEM(), SMEM(), VMEM(), VMEM(), ANY()] + [VMEM()] * parts,
        out_specs=[VMEM()] * (1 + len(COPIES[1])),
        out_shape=[jax.ShapeDtypeStruct((time_len, lanes), jnp.bfloat16)] + room(1),
        scratch_shapes=filter_scratch(time_len) + [pltpu.SemaphoreType.DMA((len(COPIES[1]),))],
        compiler_params=pltpu.CompilerParams(vmem_limit_bytes=8 * MIB),
        cost_estimate=cost(0, 2 * bases * depth * copied[1]),
        name="design",
    )(order, place, early, filters, weights, *series)
    keep_pieces(1, pieces)

    half = time_block // 2
    widths, sums, sent, got = [], [], [], []
    for c in range(CHUNKS):
        after = sent[max(c - 2, 0) : max(c - 1, 0)] + got[max(c - 3, 0) : max(c - 2, 0)]
        ahead = room(c + 2)
        keep, send, *pieces = product(design, held[c], after, weights, firsts[c + 2] if ahead else 0, ahead)
        keep_pieces(c + 2, pieces)
        widths.append(keep.shape[1])
        own = [keep]
        for bit in range(bits):
            if bit > 0:
                rows = own[-1].shape[0] // 2
                send = added(own, rows, half if bit == bits - 1 else rows)
                if bit == bits - 1:
                    sent.append(send)
            own.append(lax.ppermute(send, "chan", [(i, i ^ (1 << bit)) for i in range(parts)]))
        sums.append(own)
        got.append(own[-1])
    here = lax.axis_index("vox")
    targets = jnp.arange(owners, dtype=jnp.int32) ^ here

    def pack(chunks, terms, spots, packed=(), later=()):
        sizes = [widths[c] for c in chunks]
        spec = (len(later), bits) if later else None
        if chunks[-1] == CHUNKS - 1:
            outs = [pltpu.VMEM((half, send_cap), jnp.bfloat16)] * owners
        else:
            outs = [jax.ShapeDtypeStruct((owners, half, spread * SLOT_TILE), jnp.bfloat16)]
        more = []
        if later:
            more = [jax.ShapeDtypeStruct((half, voxels), jnp.bfloat16), pltpu.VMEM((half, voxels), jnp.bfloat16)]
        return pl.pallas_call(
            functools.partial(
                pack_kernel, spread, sizes, spots, sum(widths[: chunks[0]]) // VOX_BLOCK, spec, len(outs)
            ),
            in_specs=[SMEM(), SMEM(), VMEM(), VMEM()] + [VMEM()] * (len(packed) + len(terms) + len(later)),
            out_specs=[VMEM()] * (len(outs) + len(more)),
            out_shape=outs + more,
            scratch_shapes=[
                pltpu.VMEM((half, sum(sizes)), jnp.bfloat16),
                pltpu.VMEM((owners, half, spread * SLOT_TILE), jnp.bfloat16),
            ],
            compiler_params=pltpu.CompilerParams(vmem_limit_bytes=8 * MIB),
            cost_estimate=cost(2 * half * owners * VOX_BLOCK * sum(sizes), 4 * half * sum(sizes)),
            name="pack",
        )(targets, starts, inner, tiles, *packed, *terms, *later)

    far, near = range(owners - 1, owners // 2 - 1, -1), range(owners // 2 - 1, -1, -1)
    turns = [d for pair in zip(far, near) for d in pair if d]

    def deliver(packed):
        got = list(packed)
        for d in turns:
            got[d] = lax.ppermute(packed[d], "vox", [(i, i ^ d) for i in range(owners)])
        return got

    def early_terms(chunks):
        return [term for c in chunks for term in sums[c]], [[(0, 0)] * len(sums[c]) for c in chunks]

    low, high = range(PACK_FIRST), range(PACK_FIRST, CHUNKS)
    packed = pack(low, *early_terms(low))
    *one, late_send, late_own = pack(
        high, *early_terms(high), packed=packed, later=[term for own in sums for term in own[:-1]]
    )
    late = lax.ppermute(late_send, "chan", [(i, i ^ (1 << (bits - 1))) for i in range(parts)])
    one = deliver(one)
    starting = [sum(widths[:c]) for c in range(CHUNKS)]
    two = pack(range(CHUNKS), [late_own, late] * CHUNKS, [[(0, first)] * 2 for first in starting])
    two = pl.pallas_call(
        gate_kernel,
        in_specs=[VMEM()] * (owners + GATE),
        out_specs=[VMEM()] * owners,
        out_shape=[pltpu.VMEM((half, send_cap), jnp.bfloat16)] * owners,
        compiler_params=pltpu.CompilerParams(vmem_limit_bytes=4 * MIB),
        name="gate",
    )(*two, *(one[d] for d in turns[:GATE]))
    two = deliver(two)
    owned = None
    for first, got in ((0, one), (half, two)):
        given = [] if owned is None else [owned]
        owned = pl.pallas_call(
            functools.partial(assemble_kernel, owners, first),
            in_specs=[SMEM()] + [VMEM()] * owners + [HBM()] * len(given),
            out_specs=HBM(),
            out_shape=jax.ShapeDtypeStruct((owners, time_block, send_cap), jnp.bfloat16),
            scratch_shapes=[pltpu.SemaphoreType.DMA((owners,))],
            input_output_aliases={1 + owners: 0} if given else {},
            compiler_params=pltpu.CompilerParams(vmem_limit_bytes=4 * MIB),
            name="assemble",
        )(targets, *got, *given)
    return jnp.transpose(owned, (0, 2, 1))


def gate_kernel(*refs):
    count = (len(refs) - GATE) // 2
    for given, out in zip(refs[:count], refs[count + GATE :]):
        out[...] = given[...]


def assemble_kernel(owners, first, order_ref, *refs):
    parts, (out_ref, sems) = refs[:owners], refs[-2:]
    copies = []
    for i, ref in enumerate(parts):
        rows = pl.ds(first, ref.shape[0])
        copies.append(pltpu.make_async_copy(ref, out_ref.at[order_ref[i], rows, :], sems.at[i]))
        copies[-1].start()
    wait_all(copies)


def added(terms, first, rows):
    return sum(term[first : first + rows].astype(jnp.float32) for term in terms).astype(jnp.bfloat16)


def solution(mesh):
    return jax.shard_map(
        shards,
        mesh=mesh,
        in_specs=(P("chan", None), P(None, "chan", None), P(None, "chan", "vox"), P("vox"), P()),
        out_specs=P("vox", None, "chan"),
        check_vma=False,
    )
```

```python
import functools

import jax
import jax.numpy as jnp
from jax import lax
from jax.experimental import pallas as pl
from jax.experimental.pallas import tpu as pltpu
from jax.sharding import PartitionSpec as P

FILTER_TAPS = 16
TAP_SPACING = 2
LANES = 128
SLOT_TILE = 128
VOX_BLOCK = 256
COLUMNS = 512
ROWS = 32
CHUNKS = 4
COPIES = (((0, 4), (1, 6)), ((2, 2), (2, 2)), (), ((2, 2), (3, 1)), ((3, 2), (3, 1)))
PACKS = (0, 2, 3, 4)
PACK_STEP = 4
GATE = 3
MIB = 1 << 20

VMEM = functools.partial(pl.BlockSpec, memory_space=pltpu.VMEM)
SMEM = functools.partial(pl.BlockSpec, memory_space=pltpu.SMEM)
ANY = functools.partial(pl.BlockSpec, memory_space=pl.ANY)
HBM = functools.partial(pl.BlockSpec, memory_space=pltpu.HBM)


def copy_pieces(weight_ref, piece_refs, sems, first):
    depth, copies = weight_ref.shape[1], []
    for i, ref in enumerate(piece_refs):
        if ref.shape[1] > depth:
            ref[:, depth:, :] = jnp.zeros_like(ref[:, depth:, :])
        copy = pltpu.make_async_copy(
            weight_ref.at[:, :, pl.ds(first, ref.shape[2])], ref.at[:, pl.ds(0, depth), :], sems.at[i]
        )
        copy.start()
        copies.append(copy)
        first += ref.shape[2]
    return copies


def wait_all(copies):
    for copy in copies:
        copy.wait()


def cost(flops, read):
    return pl.CostEstimate(flops=flops, bytes_accessed=read, transcendentals=0)


def places(owners, spread, parcel_ref, table_ref, inner_ref, tile_ref, start_ref):
    rows = parcel_ref.shape[0]
    parcel = parcel_ref[...]
    high, low = parcel >> 7, parcel & 127
    owner = jnp.zeros_like(parcel)
    for entry in range(table_ref.shape[0]):
        line = jnp.broadcast_to(table_ref[entry : entry + 1, :], parcel.shape)
        found = jnp.take_along_axis(line, low, axis=1, mode="promise_in_bounds")
        owner = jnp.where(high == entry, found, owner)

    def below(shape, scale=1):
        less = lax.broadcasted_iota(jnp.int32, shape, 1) < scale * lax.broadcasted_iota(jnp.int32, shape, 0)
        return less.astype(jnp.float32).astype(jnp.bfloat16)

    lane = lax.broadcasted_iota(jnp.int32, (LANES, LANES), 1)
    above = (lax.broadcasted_iota(jnp.int32, (LANES, LANES), 0) < lane).astype(jnp.float32).astype(jnp.bfloat16)
    ones = jnp.ones((LANES, LANES), jnp.bfloat16)
    marks = start_ref.shape[0]
    ahead, block_ahead = below((rows, rows)), below((marks, rows), VOX_BLOCK // LANES)
    mark_lane = lax.broadcasted_iota(jnp.int32, (marks, LANES), 1)
    dot = functools.partial(jnp.dot, preferred_element_type=jnp.float32)
    row_block = lax.broadcasted_iota(jnp.int32, (rows, rows), 0) & -(VOX_BLOCK // LANES)
    before = lax.broadcasted_iota(jnp.int32, (rows, rows), 1) < row_block
    before = before.astype(jnp.float32).astype(jnp.bfloat16)
    slots = jnp.zeros(parcel.shape, jnp.float32)
    bases = jnp.zeros(parcel.shape, jnp.float32)
    starts = jnp.zeros((marks, LANES), jnp.float32)
    for o in range(owners):
        mine = owner == o
        hot = mine.astype(jnp.float32).astype(jnp.bfloat16)
        totals = dot(hot, ones).astype(jnp.bfloat16)
        slots = jnp.where(mine, dot(hot, above) + dot(ahead, totals), slots)
        bases = jnp.where(mine, dot(before, totals), bases)
        starts = jnp.where(mark_lane == o, dot(block_ahead, totals), starts)
    slots = slots.astype(jnp.int32)
    start_ref[...] = starts.astype(jnp.int32)
    tile_ref[...] = owner * spread + (slots >> 7)
    inner_ref[...] = (slots - (bases.astype(jnp.int32) & -SLOT_TILE)) & (2 * SLOT_TILE - 1)


def clear_lead(shifted):
    lead = TAP_SPACING * FILTER_TAPS
    for s in range(shifted.shape[0]):
        shifted[s, : lead + 8, :] = jnp.zeros((lead + 8, LANES), jnp.float32)


def shift(plain, shifted):
    lead, time_len = TAP_SPACING * FILTER_TAPS, plain.shape[0]
    series = plain[...]
    for s in range(shifted.shape[0]):
        shifted[s, lead + s * TAP_SPACING : lead + s * TAP_SPACING + time_len, :] = series


def filter_rows(shifted, filter_ref, column, first):
    lead = TAP_SPACING * FILTER_TAPS
    sums = [jnp.zeros((ROWS, LANES), jnp.float32) for _ in range(filter_ref.shape[0])]
    for tap in range(FILTER_TAPS):
        delay = tap * TAP_SPACING
        start = lead + first - 8 * (delay // 8)
        if not isinstance(start, int):
            start = pl.multiple_of(start, 8)
        lagged = shifted[(delay % 8) // TAP_SPACING, pl.ds(start, ROWS), :]
        for b in range(len(sums)):
            sums[b] = sums[b] + filter_ref[b, tap : tap + 1, column] * lagged
    return sums


def lane_tile(tile):
    return pl.ds(pl.multiple_of(tile * LANES, LANES), LANES)


def early_kernel(owners, spread, order_ref, own_ref, pair_ref, parcel_hbm, table_ref, filter_hbm, weight_ref, *refs):
    inner_ref, tile_ref, start_ref, design_ref, *piece_refs, plain, shifted, filter_ref, parcel_ref, sems, small_sems = refs
    load_filter = pltpu.make_async_copy(filter_hbm, filter_ref, small_sems.at[0])
    load_parcel = pltpu.make_async_copy(parcel_hbm, parcel_ref, small_sems.at[1])
    load_filter.start()
    load_parcel.start()
    copies = copy_pieces(weight_ref, piece_refs, sems, 0)
    block, width = own_ref.shape
    core = lax.rem(order_ref[0], 2)
    own = pl.ds(pl.multiple_of(core * block, block), block)
    pair = pl.ds(pl.multiple_of((1 - core) * block, block), block)
    clear_lead(shifted)
    load_filter.wait()

    def columns(tile, carry):
        column = lane_tile(tile)
        plain[own, :] = own_ref[:, column].astype(jnp.float32)
        plain[pair, :] = pair_ref[:, column].astype(jnp.float32)
        shift(plain, shifted)
        for first in range(ROWS, 2 * block, ROWS):
            for b, rows in enumerate(filter_rows(shifted, filter_ref, column, first)):
                lanes = pl.ds(pl.multiple_of(b * width + tile * LANES, LANES), LANES)
                design_ref[first - ROWS : first, lanes] = rows.astype(jnp.bfloat16)
        return carry

    lax.fori_loop(0, width // LANES, columns, 0)
    load_parcel.wait()
    places(owners, spread, parcel_ref, table_ref, inner_ref, tile_ref, start_ref)
    wait_all(copies)


def design_kernel(parts, first, order_ref, place_ref, early_ref, filter_ref, weight_ref, *refs):
    series_refs, (design_ref, *piece_refs, plain, shifted, sems) = refs[:parts], refs[parts:]
    copies = copy_pieces(weight_ref, piece_refs, sems, first)
    block, width = series_refs[0].shape
    chip = order_ref[0] >> 1
    clear_lead(shifted)

    def place(part, inner):
        return pl.ds(pl.multiple_of(place_ref[part] * block + inner, ROWS), ROWS)

    for first in range(ROWS, 2 * block, ROWS):
        row = place(2 * chip + first // block, first % block)
        design_ref[row, :] = early_ref[first - ROWS : first, :]

    def columns(tile, carry):
        column = lane_tile(tile)
        for d in range(parts):
            row = pl.ds(pl.multiple_of(order_ref[d] * block, block), block)
            plain[row, :] = series_refs[d][:, column].astype(jnp.float32)
        shift(plain, shifted)
        for other in range(parts // 2):
            for inner in range(0, 2 * block if other else ROWS, ROWS):
                part = 2 * (chip ^ other) + inner // block
                start = part * block + inner % block
                row = place(part, inner % block)
                for b, rows in enumerate(filter_rows(shifted, filter_ref, column, start)):
                    lanes = pl.ds(pl.multiple_of(b * width + tile * LANES, LANES), LANES)
                    design_ref[row, lanes] = rows.astype(jnp.bfloat16)
        return carry

    lax.fori_loop(0, width // LANES, columns, 0)
    wait_all(copies)


def filter_scratch(time_len):
    return [
        pltpu.VMEM((time_len, LANES), jnp.float32),
        pltpu.VMEM((8 // TAP_SPACING, time_len + TAP_SPACING * FILTER_TAPS + 8, LANES), jnp.float32),
    ]


def product_kernel(taken, extra, first, design_ref, *refs):
    weight_refs, refs = refs[:taken], refs[taken + extra :]
    copies = []
    if first is not None:
        weight_ref, keep_ref, send_ref, *piece_refs, sems = refs
        copies = copy_pieces(weight_ref, piece_refs, sems, first)
    else:
        keep_ref, send_ref = refs
    half, at = keep_ref.shape[0], 0
    for ref in weight_refs:
        for start in range(0, ref.shape[2], COLUMNS):
            weight = ref[:, :, start : min(start + COLUMNS, ref.shape[2])]
            weight = weight.reshape(-1, weight.shape[2])
            total = jnp.dot(design_ref[...], weight, preferred_element_type=jnp.float32)
            columns = slice(at, at + weight.shape[1])
            keep_ref[:, columns] = total[:half].astype(jnp.bfloat16)
            send_ref[:, columns] = total[half:].astype(jnp.bfloat16)
            at += weight.shape[1]
    wait_all(copies)


def product(design, taken, after, weights, first, ahead):
    time_len, lanes = design.shape
    width = sum(piece.shape[2] for piece in taken)
    half = jax.ShapeDtypeStruct((time_len // 2, width), jnp.bfloat16)
    return pl.pallas_call(
        functools.partial(product_kernel, len(taken), len(after), first if ahead else None),
        in_specs=[VMEM()] * (1 + len(taken)) + [ANY()] * (len(after) + bool(ahead)),
        out_specs=[VMEM()] * (2 + len(ahead)),
        out_shape=[half, half] + ahead,
        scratch_shapes=[pltpu.SemaphoreType.DMA((len(ahead),))] if ahead else [],
        compiler_params=pltpu.CompilerParams(vmem_limit_bytes=8 * MIB),
        cost_estimate=cost(2 * time_len * lanes * width, 2 * lanes * width),
        name="product",
    )(design, *taken, *after, *([weights] if ahead else []))


def add_rows(terms, each, first, out_ref):
    at, rows = 0, out_ref.shape[0]
    for c in range(0, len(terms), each):
        chunk, width = terms[c : c + each], terms[c].shape[1]
        total = sum(term[first : first + rows, :].astype(jnp.float32) for term in chunk)
        out_ref[:, at : at + width] = total.astype(jnp.bfloat16)
        at += width


def pack_kernel(spread, widths, places, first, later, outs, order_ref, start_ref, inner_ref, tile_ref, *refs):
    *refs, summed, packed = refs
    if later:
        count, each = later
        *refs, send_ref, keep_ref = refs
    terms, out_refs = refs[: len(refs) - outs], refs[len(refs) - outs :]
    if later:
        rows = packed.shape[1]
        add_rows(terms[-count:], each, 3 * rows, send_ref)
        add_rows(terms[-count:], each, rows, keep_ref)
        terms = terms[:-count]
    owners, rows = packed.shape[:2]
    if first:
        packed[...] = terms.pop(0)[...]
    else:
        packed[...] = jnp.zeros_like(packed)
    at = 0
    for width, spots in zip(widths, places):
        total = 0.0
        for row, column in spots:
            total = total + terms.pop(0)[row : row + rows, column : column + width].astype(jnp.float32)
        summed[:, at : at + width] = total.astype(jnp.bfloat16)
        at += width
    step = VOX_BLOCK // LANES
    slot_rows = lax.broadcasted_iota(jnp.int32, (2 * SLOT_TILE, VOX_BLOCK), 0)

    def moves(index, far):
        block = first + index
        values = summed[:, pl.ds(pl.multiple_of(index * VOX_BLOCK, VOX_BLOCK), VOX_BLOCK)]
        tiles, inner = (
            jnp.concatenate([ref[pl.ds(block * step + i, 1), :] for i in range(step)], axis=1)
            for ref in (tile_ref, inner_ref)
        )
        onehot = jnp.where(inner == slot_rows, 1.0, 0.0).astype(jnp.bfloat16)
        low = [start_ref[block, o] >> 7 for o in range(owners)]
        chosen = []
        for o in range(owners):
            tile = tiles - (o * spread + low[o])
            hit = jnp.where((tile == 2) if far else ((tile == 0) | (tile == 1)), 1.0, 0.0)
            chosen.append(values * hit.astype(jnp.bfloat16))
        moved = lax.dot_general(
            jnp.concatenate(chosen, axis=0), onehot, (((1,), (1,)), ((), ())), preferred_element_type=jnp.float32
        )
        moved = moved.astype(jnp.bfloat16)
        out = []
        for o in range(owners):
            here = moved[o * rows : (o + 1) * rows]
            tile, here = (low[o] + 2, here[:, :SLOT_TILE]) if far else (low[o], here)
            lanes = pl.ds(pl.multiple_of(tile * SLOT_TILE, SLOT_TILE), here.shape[1])
            out.append((o, lanes, here))
        high = [(start_ref[block + 1, o] - 1) >> 7 for o in range(owners)]
        return out, functools.reduce(jnp.maximum, [high[o] - low[o] for o in range(owners)])

    def add(targets):
        sums = [packed[owner, :, lanes] + moved for owner, lanes, moved in targets]
        for (owner, lanes, _), total in zip(targets, sums):
            packed[owner, :, lanes] = total

    def blocks(indices):
        found = [moves(index, False) for index in indices]
        for targets, _ in found:
            add(targets)
        for index, (_, longest) in zip(indices, found):

            @pl.when(longest > 1)
            def _():
                add(moves(index, True)[0])

    count = sum(widths) // VOX_BLOCK

    def some(i, carry):
        blocks([PACK_STEP * i + j for j in range(PACK_STEP)])
        return carry

    lax.fori_loop(0, count // PACK_STEP, some, 0)
    if count % PACK_STEP:
        blocks(range(count - count % PACK_STEP, count))
    if outs == 1:
        out_refs[0][...] = packed[...]
    else:
        for d, ref in enumerate(out_refs):
            ref[...] = packed[order_ref[d], :, : ref.shape[1]]


def shards(features, hrf_filters, weights, voxel_parcel, parcel_owner):
    owners, parts = lax.axis_size("vox"), lax.axis_size("chan")
    me = lax.axis_index("chan")
    voxels = voxel_parcel.shape[0]
    send_cap = 2 * voxels // owners
    bases, depth, _ = weights.shape
    blocks = voxels // VOX_BLOCK
    time_block = features.shape[0]
    time_len = time_block * parts

    series = [lax.dynamic_slice_in_dim(features, (me ^ d) * depth, depth, 1) for d in range(parts)]
    for d in range(1, parts):
        series[d] = lax.ppermute(series[d], "chan", [(i, i ^ d) for i in range(parts)])
    filters = jnp.transpose(hrf_filters, (0, 2, 1))
    spare = -depth % LANES
    lanes = bases * (depth + spare)
    unit = voxels // sum(units for pieces in COPIES for _, units in pieces)
    copied = [unit * sum(units for _, units in pieces) for pieces in COPIES]
    firsts = [sum(copied[:i]) for i in range(len(copied))]
    held = [[] for _ in range(CHUNKS)]

    def room(i):
        if i >= len(COPIES):
            return []
        return [pltpu.VMEM((bases, depth + spare, unit * units), jnp.bfloat16) for _, units in COPIES[i]]

    def keep_pieces(i, pieces):
        for (chunk, _), piece in zip(COPIES[i] if i < len(COPIES) else (), pieces):
            held[chunk].append(piece)

    if spare:
        series = [jnp.pad(part, ((0, 0), (0, spare))) for part in series]
        filters = jnp.pad(filters, ((0, 0), (0, 0), (0, spare)))

    table_rows = -(-parcel_owner.shape[0] // LANES)
    table = jnp.pad(parcel_owner, (0, table_rows * LANES - parcel_owner.shape[0])).reshape(table_rows, LANES)
    marks = -(-(blocks + 1) // 8) * 8
    spread = send_cap // SLOT_TILE + 3
    bits = parts.bit_length() - 1
    order = jnp.arange(parts, dtype=jnp.int32) ^ me
    place = sum(((order >> bit) & 1) << (bits - 1 - bit) for bit in range(bits)).astype(jnp.int32)

    early_rows = 2 * time_block - ROWS
    inner, tiles, starts, early, *pieces = pl.pallas_call(
        functools.partial(early_kernel, owners, spread),
        in_specs=[SMEM(), VMEM(), VMEM(), HBM(), VMEM(), HBM(), ANY()],
        out_specs=[VMEM()] * (4 + len(COPIES[0])),
        out_shape=[
            jax.ShapeDtypeStruct((voxels // LANES, LANES), jnp.int32),
            jax.ShapeDtypeStruct((voxels // LANES, LANES), jnp.int32),
            jax.ShapeDtypeStruct((marks, LANES), jnp.int32),
            jax.ShapeDtypeStruct((early_rows, lanes), jnp.bfloat16),
        ]
        + room(0),
        scratch_shapes=filter_scratch(2 * time_block)
        + [
            pltpu.VMEM(filters.shape, jnp.float32),
            pltpu.VMEM((voxels // LANES, LANES), jnp.int32),
            pltpu.SemaphoreType.DMA((len(COPIES[0]),)),
            pltpu.SemaphoreType.DMA((2,)),
        ],
        compiler_params=pltpu.CompilerParams(vmem_limit_bytes=8 * MIB),
        cost_estimate=cost(0, 2 * bases * depth * copied[0]),
        name="early",
    )(
        order,
        series[0],
        series[1],
        pltpu.with_memory_space_constraint(voxel_parcel.reshape(-1, LANES), pltpu.HBM),
        table,
        pltpu.with_memory_space_constraint(filters, pltpu.HBM),
        weights,
    )
    keep_pieces(0, pieces)
    design, *pieces = pl.pallas_call(
        functools.partial(design_kernel, parts, firsts[1]),
        in_specs=[SMEM(), SMEM(), VMEM(), VMEM(), ANY()] + [VMEM()] * parts,
        out_specs=[VMEM()] * (1 + len(COPIES[1])),
        out_shape=[jax.ShapeDtypeStruct((time_len, lanes), jnp.bfloat16)] + room(1),
        scratch_shapes=filter_scratch(time_len) + [pltpu.SemaphoreType.DMA((len(COPIES[1]),))],
        compiler_params=pltpu.CompilerParams(vmem_limit_bytes=8 * MIB),
        cost_estimate=cost(0, 2 * bases * depth * copied[1]),
        name="design",
    )(order, place, early, filters, weights, *series)
    keep_pieces(1, pieces)

    half = time_block // 2
    widths, sums, sent, got = [], [], [], []
    for c in range(CHUNKS):
        after = sent[max(c - 2, 0) : max(c - 1, 0)] + got[max(c - 3, 0) : max(c - 2, 0)]
        ahead = room(c + 2)
        keep, send, *pieces = product(design, held[c], after, weights, firsts[c + 2] if ahead else 0, ahead)
        keep_pieces(c + 2, pieces)
        widths.append(keep.shape[1])
        own = [keep]
        for bit in range(bits):
            if bit > 0:
                rows = own[-1].shape[0] // 2
                send = added(own, rows, half if bit == bits - 1 else rows)
                if bit == bits - 1:
                    sent.append(send)
            own.append(lax.ppermute(send, "chan", [(i, i ^ (1 << bit)) for i in range(parts)]))
        sums.append(own)
        got.append(own[-1])
    here = lax.axis_index("vox")
    targets = jnp.arange(owners, dtype=jnp.int32) ^ here

    def pack(chunks, terms, spots, packed=(), later=()):
        sizes = [widths[c] for c in chunks]
        spec = (len(later), bits) if later else None
        if chunks[-1] == CHUNKS - 1:
            outs = [pltpu.VMEM((half, send_cap), jnp.bfloat16)] * owners
        else:
            outs = [jax.ShapeDtypeStruct((owners, half, spread * SLOT_TILE), jnp.bfloat16)]
        more = []
        if later:
            more = [jax.ShapeDtypeStruct((half, voxels), jnp.bfloat16), pltpu.VMEM((half, voxels), jnp.bfloat16)]
        return pl.pallas_call(
            functools.partial(
                pack_kernel, spread, sizes, spots, sum(widths[: chunks[0]]) // VOX_BLOCK, spec, len(outs)
            ),
            in_specs=[SMEM(), SMEM(), VMEM(), VMEM()] + [VMEM()] * (len(packed) + len(terms) + len(later)),
            out_specs=[VMEM()] * (len(outs) + len(more)),
            out_shape=outs + more,
            scratch_shapes=[
                pltpu.VMEM((half, sum(sizes)), jnp.bfloat16),
                pltpu.VMEM((owners, half, spread * SLOT_TILE), jnp.bfloat16),
            ],
            compiler_params=pltpu.CompilerParams(vmem_limit_bytes=8 * MIB),
            cost_estimate=cost(2 * half * owners * VOX_BLOCK * sum(sizes), 4 * half * sum(sizes)),
            name="pack",
        )(targets, starts, inner, tiles, *packed, *terms, *later)

    turns = range(owners - 1, 0, -1)

    def deliver(packed):
        got = list(packed)
        for d in turns:
            got[d] = lax.ppermute(packed[d], "vox", [(i, i ^ d) for i in range(owners)])
        return got

    def early_terms(chunks):
        return [term for c in chunks for term in sums[c]], [[(0, 0)] * len(sums[c]) for c in chunks]

    packed = []
    for low, high in zip(PACKS, PACKS[1:]):
        chunks = range(low, high)
        later = [term for own in sums for term in own[:-1]] if high == CHUNKS else []
        packed = pack(chunks, *early_terms(chunks), packed=packed, later=later)
    *one, late_send, late_own = packed
    late = lax.ppermute(late_send, "chan", [(i, i ^ (1 << (bits - 1))) for i in range(parts)])
    one = deliver(one)
    starting = [sum(widths[:c]) for c in range(CHUNKS)]
    two = pack(range(CHUNKS), [late_own, late] * CHUNKS, [[(0, first)] * 2 for first in starting])
    two = pl.pallas_call(
        gate_kernel,
        in_specs=[VMEM()] * (owners + GATE),
        out_specs=[VMEM()] * owners,
        out_shape=[pltpu.VMEM((half, send_cap), jnp.bfloat16)] * owners,
        compiler_params=pltpu.CompilerParams(vmem_limit_bytes=4 * MIB),
        name="gate",
    )(*two, *(one[d] for d in turns[:GATE]))
    two = deliver(two)
    owned = None
    for first, got in ((0, one), (half, two)):
        given = [] if owned is None else [owned]
        owned = pl.pallas_call(
            functools.partial(assemble_kernel, owners, first),
            in_specs=[SMEM()] + [VMEM()] * owners + [HBM()] * len(given),
            out_specs=HBM(),
            out_shape=jax.ShapeDtypeStruct((owners, time_block, send_cap), jnp.bfloat16),
            scratch_shapes=[pltpu.SemaphoreType.DMA((owners,))],
            input_output_aliases={1 + owners: 0} if given else {},
            compiler_params=pltpu.CompilerParams(vmem_limit_bytes=4 * MIB),
            name="assemble",
        )(targets, *got, *given)
    return jnp.transpose(owned, (0, 2, 1))


def gate_kernel(*refs):
    count = (len(refs) - GATE) // 2
    for given, out in zip(refs[:count], refs[count + GATE :]):
        out[...] = given[...]


def assemble_kernel(owners, first, order_ref, *refs):
    parts, (out_ref, sems) = refs[:owners], refs[-2:]
    copies = []
    for i, ref in enumerate(parts):
        rows = pl.ds(first, ref.shape[0])
        copies.append(pltpu.make_async_copy(ref, out_ref.at[order_ref[i], rows, :], sems.at[i]))
        copies[-1].start()
    wait_all(copies)


def added(terms, first, rows):
    return sum(term[first : first + rows].astype(jnp.float32) for term in terms).astype(jnp.bfloat16)


def solution(mesh):
    return jax.shard_map(
        shards,
        mesh=mesh,
        in_specs=(P("chan", None), P(None, "chan", None), P(None, "chan", "vox"), P("vox"), P()),
        out_specs=P("vox", None, "chan"),
        check_vma=False,
    )
```

```python
import functools

import jax
import jax.numpy as jnp
from jax import lax
from jax.experimental import pallas as pl
from jax.experimental.pallas import tpu as pltpu
from jax.sharding import PartitionSpec as P

FILTER_TAPS = 16
TAP_SPACING = 2
LANES = 128
SLOT_TILE = 128
VOX_BLOCK = 256
COLUMNS = 512
ROWS = 32
CHUNKS = 4
COPIES = (((0, 4), (1, 6)), ((2, 2), (2, 2)), (), ((2, 2), (3, 1)), ((3, 2), (3, 1)))
PACKS = (0, 2, 3, 4)
PACK_STEP = 4
GATE = 3
MIB = 1 << 20

VMEM = functools.partial(pl.BlockSpec, memory_space=pltpu.VMEM)
SMEM = functools.partial(pl.BlockSpec, memory_space=pltpu.SMEM)
ANY = functools.partial(pl.BlockSpec, memory_space=pl.ANY)
HBM = functools.partial(pl.BlockSpec, memory_space=pltpu.HBM)


def copy_pieces(weight_ref, piece_refs, sems, first):
    depth, copies = weight_ref.shape[1], []
    for i, ref in enumerate(piece_refs):
        if ref.shape[1] > depth:
            ref[:, depth:, :] = jnp.zeros_like(ref[:, depth:, :])
        copy = pltpu.make_async_copy(
            weight_ref.at[:, :, pl.ds(first, ref.shape[2])], ref.at[:, pl.ds(0, depth), :], sems.at[i]
        )
        copy.start()
        copies.append(copy)
        first += ref.shape[2]
    return copies


def wait_all(copies):
    for copy in copies:
        copy.wait()


def cost(flops, read):
    return pl.CostEstimate(flops=flops, bytes_accessed=read, transcendentals=0)


def places(owners, spread, parcel_ref, table_ref, inner_ref, tile_ref, start_ref):
    rows = parcel_ref.shape[0]
    parcel = parcel_ref[...]
    high, low = parcel >> 7, parcel & 127
    owner = jnp.zeros_like(parcel)
    for entry in range(table_ref.shape[0]):
        line = jnp.broadcast_to(table_ref[entry : entry + 1, :], parcel.shape)
        found = jnp.take_along_axis(line, low, axis=1, mode="promise_in_bounds")
        owner = jnp.where(high == entry, found, owner)

    def below(shape, scale=1):
        less = lax.broadcasted_iota(jnp.int32, shape, 1) < scale * lax.broadcasted_iota(jnp.int32, shape, 0)
        return less.astype(jnp.float32).astype(jnp.bfloat16)

    lane = lax.broadcasted_iota(jnp.int32, (LANES, LANES), 1)
    above = (lax.broadcasted_iota(jnp.int32, (LANES, LANES), 0) < lane).astype(jnp.float32).astype(jnp.bfloat16)
    ones = jnp.ones((LANES, LANES), jnp.bfloat16)
    marks = start_ref.shape[0]
    ahead, block_ahead = below((rows, rows)), below((marks, rows), VOX_BLOCK // LANES)
    mark_lane = lax.broadcasted_iota(jnp.int32, (marks, LANES), 1)
    dot = functools.partial(jnp.dot, preferred_element_type=jnp.float32)
    row_block = lax.broadcasted_iota(jnp.int32, (rows, rows), 0) & -(VOX_BLOCK // LANES)
    before = lax.broadcasted_iota(jnp.int32, (rows, rows), 1) < row_block
    before = before.astype(jnp.float32).astype(jnp.bfloat16)
    slots = jnp.zeros(parcel.shape, jnp.float32)
    bases = jnp.zeros(parcel.shape, jnp.float32)
    starts = jnp.zeros((marks, LANES), jnp.float32)
    for o in range(owners):
        mine = owner == o
        hot = mine.astype(jnp.float32).astype(jnp.bfloat16)
        totals = dot(hot, ones).astype(jnp.bfloat16)
        slots = jnp.where(mine, dot(hot, above) + dot(ahead, totals), slots)
        bases = jnp.where(mine, dot(before, totals), bases)
        starts = jnp.where(mark_lane == o, dot(block_ahead, totals), starts)
    slots = slots.astype(jnp.int32)
    start_ref[...] = starts.astype(jnp.int32)
    tile_ref[...] = owner * spread + (slots >> 7)
    inner_ref[...] = (slots - (bases.astype(jnp.int32) & -SLOT_TILE)) & (2 * SLOT_TILE - 1)


def clear_lead(shifted):
    lead = TAP_SPACING * FILTER_TAPS
    for s in range(shifted.shape[0]):
        shifted[s, : lead + 8, :] = jnp.zeros((lead + 8, LANES), jnp.float32)


def shift(plain, shifted):
    lead, time_len = TAP_SPACING * FILTER_TAPS, plain.shape[0]
    series = plain[...]
    for s in range(shifted.shape[0]):
        shifted[s, lead + s * TAP_SPACING : lead + s * TAP_SPACING + time_len, :] = series


def filter_rows(shifted, filter_ref, column, first):
    lead = TAP_SPACING * FILTER_TAPS
    sums = [jnp.zeros((ROWS, LANES), jnp.float32) for _ in range(filter_ref.shape[0])]
    for tap in range(FILTER_TAPS):
        delay = tap * TAP_SPACING
        start = lead + first - 8 * (delay // 8)
        if not isinstance(start, int):
            start = pl.multiple_of(start, 8)
        lagged = shifted[(delay % 8) // TAP_SPACING, pl.ds(start, ROWS), :]
        for b in range(len(sums)):
            sums[b] = sums[b] + filter_ref[b, tap : tap + 1, column] * lagged
    return sums


def lane_tile(tile):
    return pl.ds(pl.multiple_of(tile * LANES, LANES), LANES)


def early_kernel(owners, spread, order_ref, own_ref, pair_ref, parcel_hbm, table_ref, filter_hbm, weight_ref, *refs):
    inner_ref, tile_ref, start_ref, design_ref, *piece_refs, plain, shifted, filter_ref, parcel_ref, sems, small_sems = refs
    load_filter = pltpu.make_async_copy(filter_hbm, filter_ref, small_sems.at[0])
    load_parcel = pltpu.make_async_copy(parcel_hbm, parcel_ref, small_sems.at[1])
    load_filter.start()
    load_parcel.start()
    copies = copy_pieces(weight_ref, piece_refs, sems, 0)
    block, width = own_ref.shape
    core = lax.rem(order_ref[0], 2)
    own = pl.ds(pl.multiple_of(core * block, block), block)
    pair = pl.ds(pl.multiple_of((1 - core) * block, block), block)
    clear_lead(shifted)
    load_filter.wait()

    def columns(tile, carry):
        column = lane_tile(tile)
        plain[own, :] = own_ref[:, column].astype(jnp.float32)
        plain[pair, :] = pair_ref[:, column].astype(jnp.float32)
        shift(plain, shifted)
        for first in range(ROWS, 2 * block, ROWS):
            for b, rows in enumerate(filter_rows(shifted, filter_ref, column, first)):
                lanes = pl.ds(pl.multiple_of(b * width + tile * LANES, LANES), LANES)
                design_ref[first - ROWS : first, lanes] = rows.astype(jnp.bfloat16)
        return carry

    lax.fori_loop(0, width // LANES, columns, 0)
    load_parcel.wait()
    places(owners, spread, parcel_ref, table_ref, inner_ref, tile_ref, start_ref)
    wait_all(copies)


def design_kernel(parts, first, order_ref, place_ref, early_ref, filter_ref, weight_ref, *refs):
    series_refs, (design_ref, *piece_refs, plain, shifted, sems) = refs[:parts], refs[parts:]
    copies = copy_pieces(weight_ref, piece_refs, sems, first)
    block, width = series_refs[0].shape
    chip = order_ref[0] >> 1
    clear_lead(shifted)

    def place(part, inner):
        return pl.ds(pl.multiple_of(place_ref[part] * block + inner, ROWS), ROWS)

    for first in range(ROWS, 2 * block, ROWS):
        row = place(2 * chip + first // block, first % block)
        design_ref[row, :] = early_ref[first - ROWS : first, :]

    def columns(tile, carry):
        column = lane_tile(tile)
        for d in range(parts):
            row = pl.ds(pl.multiple_of(order_ref[d] * block, block), block)
            plain[row, :] = series_refs[d][:, column].astype(jnp.float32)
        shift(plain, shifted)
        for other in range(parts // 2):
            for inner in range(0, 2 * block if other else ROWS, ROWS):
                part = 2 * (chip ^ other) + inner // block
                start = part * block + inner % block
                row = place(part, inner % block)
                for b, rows in enumerate(filter_rows(shifted, filter_ref, column, start)):
                    lanes = pl.ds(pl.multiple_of(b * width + tile * LANES, LANES), LANES)
                    design_ref[row, lanes] = rows.astype(jnp.bfloat16)
        return carry

    lax.fori_loop(0, width // LANES, columns, 0)
    wait_all(copies)


def filter_scratch(time_len):
    return [
        pltpu.VMEM((time_len, LANES), jnp.float32),
        pltpu.VMEM((8 // TAP_SPACING, time_len + TAP_SPACING * FILTER_TAPS + 8, LANES), jnp.float32),
    ]


def product_kernel(taken, extra, first, design_ref, *refs):
    weight_refs, refs = refs[:taken], refs[taken + extra :]
    copies = []
    if first is not None:
        weight_ref, keep_ref, send_ref, *piece_refs, sems = refs
        copies = copy_pieces(weight_ref, piece_refs, sems, first)
    else:
        keep_ref, send_ref = refs
    half, at = keep_ref.shape[0], 0
    for ref in weight_refs:
        for start in range(0, ref.shape[2], COLUMNS):
            weight = ref[:, :, start : min(start + COLUMNS, ref.shape[2])]
            weight = weight.reshape(-1, weight.shape[2])
            total = jnp.dot(design_ref[...], weight, preferred_element_type=jnp.float32)
            columns = slice(at, at + weight.shape[1])
            keep_ref[:, columns] = total[:half].astype(jnp.bfloat16)
            send_ref[:, columns] = total[half:].astype(jnp.bfloat16)
            at += weight.shape[1]
    wait_all(copies)


def product(design, taken, after, weights, first, ahead):
    time_len, lanes = design.shape
    width = sum(piece.shape[2] for piece in taken)
    half = jax.ShapeDtypeStruct((time_len // 2, width), jnp.bfloat16)
    return pl.pallas_call(
        functools.partial(product_kernel, len(taken), len(after), first if ahead else None),
        in_specs=[VMEM()] * (1 + len(taken)) + [ANY()] * (len(after) + bool(ahead)),
        out_specs=[VMEM()] * (2 + len(ahead)),
        out_shape=[half, half] + ahead,
        scratch_shapes=[pltpu.SemaphoreType.DMA((len(ahead),))] if ahead else [],
        compiler_params=pltpu.CompilerParams(vmem_limit_bytes=8 * MIB),
        cost_estimate=cost(2 * time_len * lanes * width, 2 * lanes * width),
        name="product",
    )(design, *taken, *after, *([weights] if ahead else []))


def add_rows(terms, each, first, out_ref):
    at, rows = 0, out_ref.shape[0]
    for c in range(0, len(terms), each):
        chunk, width = terms[c : c + each], terms[c].shape[1]
        total = sum(term[first : first + rows, :].astype(jnp.float32) for term in chunk)
        out_ref[:, at : at + width] = total.astype(jnp.bfloat16)
        at += width


def pack_kernel(spread, widths, places, first, later, outs, order_ref, start_ref, inner_ref, tile_ref, *refs):
    *refs, summed, packed = refs
    if later:
        count, each = later
        *refs, send_ref, keep_ref = refs
    terms, out_refs = refs[: len(refs) - outs], refs[len(refs) - outs :]
    if later:
        rows = packed.shape[1]
        add_rows(terms[-count:], each, 3 * rows, send_ref)
        add_rows(terms[-count:], each, rows, keep_ref)
        terms = terms[:-count]
    owners, rows = packed.shape[:2]
    if first:
        packed[...] = terms.pop(0)[...]
    else:
        packed[...] = jnp.zeros_like(packed)
    at = 0
    for width, spots in zip(widths, places):
        total = 0.0
        for row, column in spots:
            total = total + terms.pop(0)[row : row + rows, column : column + width].astype(jnp.float32)
        summed[:, at : at + width] = total.astype(jnp.bfloat16)
        at += width
    step = VOX_BLOCK // LANES
    slot_rows = lax.broadcasted_iota(jnp.int32, (2 * SLOT_TILE, VOX_BLOCK), 0)

    def moves(index, far):
        block = first + index
        values = summed[:, pl.ds(pl.multiple_of(index * VOX_BLOCK, VOX_BLOCK), VOX_BLOCK)]
        tiles, inner = (
            jnp.concatenate([ref[pl.ds(block * step + i, 1), :] for i in range(step)], axis=1)
            for ref in (tile_ref, inner_ref)
        )
        onehot = jnp.where(inner == slot_rows, 1.0, 0.0).astype(jnp.bfloat16)
        low = [start_ref[block, o] >> 7 for o in range(owners)]
        chosen = []
        for o in range(owners):
            tile = tiles - (o * spread + low[o])
            hit = jnp.where((tile == 2) if far else ((tile == 0) | (tile == 1)), 1.0, 0.0)
            chosen.append(values * hit.astype(jnp.bfloat16))
        moved = lax.dot_general(
            jnp.concatenate(chosen, axis=0), onehot, (((1,), (1,)), ((), ())), preferred_element_type=jnp.float32
        )
        moved = moved.astype(jnp.bfloat16)
        out = []
        for o in range(owners):
            here = moved[o * rows : (o + 1) * rows]
            tile, here = (low[o] + 2, here[:, :SLOT_TILE]) if far else (low[o], here)
            lanes = pl.ds(pl.multiple_of(tile * SLOT_TILE, SLOT_TILE), here.shape[1])
            out.append((o, lanes, here))
        high = [(start_ref[block + 1, o] - 1) >> 7 for o in range(owners)]
        return out, functools.reduce(jnp.maximum, [high[o] - low[o] for o in range(owners)])

    def add(targets):
        sums = [packed[owner, :, lanes] + moved for owner, lanes, moved in targets]
        for (owner, lanes, _), total in zip(targets, sums):
            packed[owner, :, lanes] = total

    def blocks(indices):
        found = [moves(index, False) for index in indices]
        for targets, _ in found:
            add(targets)
        for index, (_, longest) in zip(indices, found):

            @pl.when(longest > 1)
            def _():
                add(moves(index, True)[0])

    count = sum(widths) // VOX_BLOCK

    def some(i, carry):
        blocks([PACK_STEP * i + j for j in range(PACK_STEP)])
        return carry

    lax.fori_loop(0, count // PACK_STEP, some, 0)
    if count % PACK_STEP:
        blocks(range(count - count % PACK_STEP, count))
    if outs == 1:
        out_refs[0][...] = packed[...]
    else:
        for d, ref in enumerate(out_refs):
            ref[...] = packed[order_ref[d], :, : ref.shape[1]]


def shards(features, hrf_filters, weights, voxel_parcel, parcel_owner):
    owners, parts = lax.axis_size("vox"), lax.axis_size("chan")
    me = lax.axis_index("chan")
    voxels = voxel_parcel.shape[0]
    send_cap = 2 * voxels // owners
    bases, depth, _ = weights.shape
    blocks = voxels // VOX_BLOCK
    time_block = features.shape[0]
    time_len = time_block * parts

    series = [lax.dynamic_slice_in_dim(features, (me ^ d) * depth, depth, 1) for d in range(parts)]
    for d in range(1, parts):
        series[d] = lax.ppermute(series[d], "chan", [(i, i ^ d) for i in range(parts)])
    filters = jnp.transpose(hrf_filters, (0, 2, 1))
    spare = -depth % LANES
    lanes = bases * (depth + spare)
    unit = voxels // sum(units for pieces in COPIES for _, units in pieces)
    copied = [unit * sum(units for _, units in pieces) for pieces in COPIES]
    firsts = [sum(copied[:i]) for i in range(len(copied))]
    held = [[] for _ in range(CHUNKS)]

    def room(i):
        if i >= len(COPIES):
            return []
        return [pltpu.VMEM((bases, depth + spare, unit * units), jnp.bfloat16) for _, units in COPIES[i]]

    def keep_pieces(i, pieces):
        for (chunk, _), piece in zip(COPIES[i] if i < len(COPIES) else (), pieces):
            held[chunk].append(piece)

    if spare:
        series = [jnp.pad(part, ((0, 0), (0, spare))) for part in series]
        filters = jnp.pad(filters, ((0, 0), (0, 0), (0, spare)))

    table_rows = -(-parcel_owner.shape[0] // LANES)
    table = jnp.pad(parcel_owner, (0, table_rows * LANES - parcel_owner.shape[0])).reshape(table_rows, LANES)
    marks = -(-(blocks + 1) // 8) * 8
    spread = send_cap // SLOT_TILE + 3
    bits = parts.bit_length() - 1
    order = jnp.arange(parts, dtype=jnp.int32) ^ me
    place = sum(((order >> bit) & 1) << (bits - 1 - bit) for bit in range(bits)).astype(jnp.int32)

    early_rows = 2 * time_block - ROWS
    inner, tiles, starts, early, *pieces = pl.pallas_call(
        functools.partial(early_kernel, owners, spread),
        in_specs=[SMEM(), VMEM(), VMEM(), HBM(), VMEM(), HBM(), ANY()],
        out_specs=[VMEM()] * (4 + len(COPIES[0])),
        out_shape=[
            jax.ShapeDtypeStruct((voxels // LANES, LANES), jnp.int32),
            jax.ShapeDtypeStruct((voxels // LANES, LANES), jnp.int32),
            jax.ShapeDtypeStruct((marks, LANES), jnp.int32),
            jax.ShapeDtypeStruct((early_rows, lanes), jnp.bfloat16),
        ]
        + room(0),
        scratch_shapes=filter_scratch(2 * time_block)
        + [
            pltpu.VMEM(filters.shape, jnp.float32),
            pltpu.VMEM((voxels // LANES, LANES), jnp.int32),
            pltpu.SemaphoreType.DMA((len(COPIES[0]),)),
            pltpu.SemaphoreType.DMA((2,)),
        ],
        compiler_params=pltpu.CompilerParams(vmem_limit_bytes=8 * MIB),
        cost_estimate=cost(0, 2 * bases * depth * copied[0]),
        name="early",
    )(
        order,
        series[0],
        series[1],
        pltpu.with_memory_space_constraint(voxel_parcel.reshape(-1, LANES), pltpu.HBM),
        table,
        pltpu.with_memory_space_constraint(filters, pltpu.HBM),
        weights,
    )
    keep_pieces(0, pieces)
    design, *pieces = pl.pallas_call(
        functools.partial(design_kernel, parts, firsts[1]),
        in_specs=[SMEM(), SMEM(), VMEM(), VMEM(), ANY()] + [VMEM()] * parts,
        out_specs=[VMEM()] * (1 + len(COPIES[1])),
        out_shape=[jax.ShapeDtypeStruct((time_len, lanes), jnp.bfloat16)] + room(1),
        scratch_shapes=filter_scratch(time_len) + [pltpu.SemaphoreType.DMA((len(COPIES[1]),))],
        compiler_params=pltpu.CompilerParams(vmem_limit_bytes=8 * MIB),
        cost_estimate=cost(0, 2 * bases * depth * copied[1]),
        name="design",
    )(order, place, early, filters, weights, *series)
    keep_pieces(1, pieces)

    half = time_block // 2
    widths, sums, sent, got = [], [], [], []
    for c in range(CHUNKS):
        after = sent[max(c - 2, 0) : max(c - 1, 0)] + got[max(c - 3, 0) : max(c - 2, 0)]
        ahead = room(c + 2)
        keep, send, *pieces = product(design, held[c], after, weights, firsts[c + 2] if ahead else 0, ahead)
        keep_pieces(c + 2, pieces)
        widths.append(keep.shape[1])
        own = [keep]
        for bit in range(bits):
            if bit > 0:
                rows = own[-1].shape[0] // 2
                send = added(own, rows, half if bit == bits - 1 else rows)
                if bit == bits - 1:
                    sent.append(send)
            own.append(lax.ppermute(send, "chan", [(i, i ^ (1 << bit)) for i in range(parts)]))
        sums.append(own)
        got.append(own[-1])
    here = lax.axis_index("vox")
    targets = jnp.arange(owners, dtype=jnp.int32) ^ here

    def pack(chunks, terms, spots, packed=(), later=()):
        sizes = [widths[c] for c in chunks]
        spec = (len(later), bits) if later else None
        if chunks[-1] == CHUNKS - 1:
            outs = [pltpu.VMEM((half, send_cap), jnp.bfloat16)] * owners
        else:
            outs = [jax.ShapeDtypeStruct((owners, half, spread * SLOT_TILE), jnp.bfloat16)]
        more = []
        if later:
            more = [jax.ShapeDtypeStruct((half, voxels), jnp.bfloat16), pltpu.VMEM((half, voxels), jnp.bfloat16)]
        return pl.pallas_call(
            functools.partial(
                pack_kernel, spread, sizes, spots, sum(widths[: chunks[0]]) // VOX_BLOCK, spec, len(outs)
            ),
            in_specs=[SMEM(), SMEM(), VMEM(), VMEM()] + [VMEM()] * (len(packed) + len(terms) + len(later)),
            out_specs=[VMEM()] * (len(outs) + len(more)),
            out_shape=outs + more,
            scratch_shapes=[
                pltpu.VMEM((half, sum(sizes)), jnp.bfloat16),
                pltpu.VMEM((owners, half, spread * SLOT_TILE), jnp.bfloat16),
            ],
            compiler_params=pltpu.CompilerParams(vmem_limit_bytes=8 * MIB),
            cost_estimate=cost(2 * half * owners * VOX_BLOCK * sum(sizes), 4 * half * sum(sizes)),
            name="pack",
        )(targets, starts, inner, tiles, *packed, *terms, *later)

    turns = range(owners - 1, 0, -1)

    def deliver(packed):
        got = list(packed)
        for d in turns:
            got[d] = lax.ppermute(packed[d], "vox", [(i, i ^ d) for i in range(owners)])
        return got

    def early_terms(chunks):
        return [term for c in chunks for term in sums[c]], [[(0, 0)] * len(sums[c]) for c in chunks]

    packed = []
    for low, high in zip(PACKS, PACKS[1:]):
        chunks = range(low, high)
        later = [term for own in sums for term in own[:-1]] if high == CHUNKS else []
        packed = pack(chunks, *early_terms(chunks), packed=packed, later=later)
    *one, late_send, late_own = packed
    late = lax.ppermute(late_send, "chan", [(i, i ^ (1 << (bits - 1))) for i in range(parts)])
    one = deliver(one)
    starting = [sum(widths[:c]) for c in range(CHUNKS)]
    two = pack(range(CHUNKS), [late_own, late] * CHUNKS, [[(0, first)] * 2 for first in starting])
    two = pl.pallas_call(
        gate_kernel,
        in_specs=[VMEM()] * (owners + GATE),
        out_specs=[VMEM()] * owners,
        out_shape=[pltpu.VMEM((half, send_cap), jnp.bfloat16)] * owners,
        compiler_params=pltpu.CompilerParams(vmem_limit_bytes=4 * MIB),
        name="gate",
    )(*two, *(one[d] for d in turns[:GATE]))
    two = deliver(two)
    owned = None
    everyone = [*turns, 0]
    middle = owners // 2
    for first, got, which in ((0, one, everyone), (half, two, [0, *turns[: middle - 1]]), (half, two, turns[middle - 1 :])):
        given = [] if owned is None else [owned]
        count = len(which)
        owned = pl.pallas_call(
            functools.partial(assemble_kernel, tuple(which), first),
            in_specs=[SMEM()] + [VMEM()] * count + [HBM()] * len(given),
            out_specs=HBM(),
            out_shape=jax.ShapeDtypeStruct((owners, time_block, send_cap), jnp.bfloat16),
            scratch_shapes=[pltpu.SemaphoreType.DMA((count,))],
            input_output_aliases={1 + count: 0} if given else {},
            compiler_params=pltpu.CompilerParams(vmem_limit_bytes=4 * MIB),
            name="assemble",
        )(targets, *(got[d] for d in which), *given)
    return jnp.transpose(owned, (0, 2, 1))


def gate_kernel(*refs):
    count = (len(refs) - GATE) // 2
    for given, out in zip(refs[:count], refs[count + GATE :]):
        out[...] = given[...]


def assemble_kernel(which, first, order_ref, *refs):
    parts, (out_ref, sems) = refs[: len(which)], refs[-2:]
    copies = []
    for i, (d, ref) in enumerate(zip(which, parts)):
        rows = pl.ds(first, ref.shape[0])
        copies.append(pltpu.make_async_copy(ref, out_ref.at[order_ref[d], rows, :], sems.at[i]))
        copies[-1].start()
    wait_all(copies)


def added(terms, first, rows):
    return sum(term[first : first + rows].astype(jnp.float32) for term in terms).astype(jnp.bfloat16)


def solution(mesh):
    return jax.shard_map(
        shards,
        mesh=mesh,
        in_specs=(P("chan", None), P(None, "chan", None), P(None, "chan", "vox"), P("vox"), P()),
        out_specs=P("vox", None, "chan"),
        check_vma=False,
    )
```

```python
import functools

import jax
import jax.numpy as jnp
from jax import lax
from jax.experimental import pallas as pl
from jax.experimental.pallas import tpu as pltpu
from jax.sharding import PartitionSpec as P

FILTER_TAPS = 16
TAP_SPACING = 2
LANES = 128
SLOT_TILE = 128
VOX_BLOCK = 256
COLUMNS = 512
ROWS = 32
CHUNKS = 4
COPIES = (((0, 4), (1, 6)), ((2, 2), (2, 2)), (), ((2, 2), (3, 1)), ((3, 2), (3, 1)))
PACKS = (0, 2, 3, 4)
PACK_STEP = 4
GATE = 2
MIB = 1 << 20

VMEM = functools.partial(pl.BlockSpec, memory_space=pltpu.VMEM)
SMEM = functools.partial(pl.BlockSpec, memory_space=pltpu.SMEM)
ANY = functools.partial(pl.BlockSpec, memory_space=pl.ANY)
HBM = functools.partial(pl.BlockSpec, memory_space=pltpu.HBM)


def copy_pieces(weight_ref, piece_refs, sems, first):
    depth, copies = weight_ref.shape[1], []
    for i, ref in enumerate(piece_refs):
        if ref.shape[1] > depth:
            ref[:, depth:, :] = jnp.zeros_like(ref[:, depth:, :])
        copy = pltpu.make_async_copy(
            weight_ref.at[:, :, pl.ds(first, ref.shape[2])], ref.at[:, pl.ds(0, depth), :], sems.at[i]
        )
        copy.start()
        copies.append(copy)
        first += ref.shape[2]
    return copies


def wait_all(copies):
    for copy in copies:
        copy.wait()


def cost(flops, read):
    return pl.CostEstimate(flops=flops, bytes_accessed=read, transcendentals=0)


def places(owners, spread, parcel_ref, table_ref, inner_ref, tile_ref, start_ref):
    rows = parcel_ref.shape[0]
    parcel = parcel_ref[...]
    high, low = parcel >> 7, parcel & 127
    owner = jnp.zeros_like(parcel)
    for entry in range(table_ref.shape[0]):
        line = jnp.broadcast_to(table_ref[entry : entry + 1, :], parcel.shape)
        found = jnp.take_along_axis(line, low, axis=1, mode="promise_in_bounds")
        owner = jnp.where(high == entry, found, owner)

    def below(shape, scale=1):
        less = lax.broadcasted_iota(jnp.int32, shape, 1) < scale * lax.broadcasted_iota(jnp.int32, shape, 0)
        return less.astype(jnp.float32).astype(jnp.bfloat16)

    lane = lax.broadcasted_iota(jnp.int32, (LANES, LANES), 1)
    above = (lax.broadcasted_iota(jnp.int32, (LANES, LANES), 0) < lane).astype(jnp.float32).astype(jnp.bfloat16)
    ones = jnp.ones((LANES, LANES), jnp.bfloat16)
    marks = start_ref.shape[0]
    ahead, block_ahead = below((rows, rows)), below((marks, rows), VOX_BLOCK // LANES)
    mark_lane = lax.broadcasted_iota(jnp.int32, (marks, LANES), 1)
    dot = functools.partial(jnp.dot, preferred_element_type=jnp.float32)
    row_block = lax.broadcasted_iota(jnp.int32, (rows, rows), 0) & -(VOX_BLOCK // LANES)
    before = lax.broadcasted_iota(jnp.int32, (rows, rows), 1) < row_block
    before = before.astype(jnp.float32).astype(jnp.bfloat16)
    slots = jnp.zeros(parcel.shape, jnp.float32)
    bases = jnp.zeros(parcel.shape, jnp.float32)
    starts = jnp.zeros((marks, LANES), jnp.float32)
    for o in range(owners):
        mine = owner == o
        hot = mine.astype(jnp.float32).astype(jnp.bfloat16)
        totals = dot(hot, ones).astype(jnp.bfloat16)
        slots = jnp.where(mine, dot(hot, above) + dot(ahead, totals), slots)
        bases = jnp.where(mine, dot(before, totals), bases)
        starts = jnp.where(mark_lane == o, dot(block_ahead, totals), starts)
    slots = slots.astype(jnp.int32)
    start_ref[...] = starts.astype(jnp.int32)
    tile_ref[...] = owner * spread + (slots >> 7)
    inner_ref[...] = (slots - (bases.astype(jnp.int32) & -SLOT_TILE)) & (2 * SLOT_TILE - 1)


def clear_lead(shifted):
    lead = TAP_SPACING * FILTER_TAPS
    for s in range(shifted.shape[0]):
        shifted[s, : lead + 8, :] = jnp.zeros((lead + 8, LANES), jnp.float32)


def shift(plain, shifted):
    lead, time_len = TAP_SPACING * FILTER_TAPS, plain.shape[0]
    series = plain[...]
    for s in range(shifted.shape[0]):
        shifted[s, lead + s * TAP_SPACING : lead + s * TAP_SPACING + time_len, :] = series


def filter_rows(shifted, filter_ref, column, first):
    lead = TAP_SPACING * FILTER_TAPS
    sums = [jnp.zeros((ROWS, LANES), jnp.float32) for _ in range(filter_ref.shape[0])]
    for tap in range(FILTER_TAPS):
        delay = tap * TAP_SPACING
        start = lead + first - 8 * (delay // 8)
        if not isinstance(start, int):
            start = pl.multiple_of(start, 8)
        lagged = shifted[(delay % 8) // TAP_SPACING, pl.ds(start, ROWS), :]
        for b in range(len(sums)):
            sums[b] = sums[b] + filter_ref[b, tap : tap + 1, column] * lagged
    return sums


def lane_tile(tile):
    return pl.ds(pl.multiple_of(tile * LANES, LANES), LANES)


def early_kernel(owners, spread, order_ref, own_ref, pair_ref, parcel_hbm, table_ref, filter_hbm, weight_ref, *refs):
    inner_ref, tile_ref, start_ref, design_ref, *piece_refs, plain, shifted, filter_ref, parcel_ref, sems, small_sems = refs
    load_filter = pltpu.make_async_copy(filter_hbm, filter_ref, small_sems.at[0])
    load_parcel = pltpu.make_async_copy(parcel_hbm, parcel_ref, small_sems.at[1])
    load_filter.start()
    load_parcel.start()
    copies = copy_pieces(weight_ref, piece_refs, sems, 0)
    block, width = own_ref.shape
    core = lax.rem(order_ref[0], 2)
    own = pl.ds(pl.multiple_of(core * block, block), block)
    pair = pl.ds(pl.multiple_of((1 - core) * block, block), block)
    clear_lead(shifted)
    load_filter.wait()

    def columns(tile, carry):
        column = lane_tile(tile)
        plain[own, :] = own_ref[:, column].astype(jnp.float32)
        plain[pair, :] = pair_ref[:, column].astype(jnp.float32)
        shift(plain, shifted)
        for first in range(ROWS, 2 * block, ROWS):
            for b, rows in enumerate(filter_rows(shifted, filter_ref, column, first)):
                lanes = pl.ds(pl.multiple_of(b * width + tile * LANES, LANES), LANES)
                design_ref[first - ROWS : first, lanes] = rows.astype(jnp.bfloat16)
        return carry

    lax.fori_loop(0, width // LANES, columns, 0)
    load_parcel.wait()
    places(owners, spread, parcel_ref, table_ref, inner_ref, tile_ref, start_ref)
    wait_all(copies)


def design_kernel(parts, first, order_ref, place_ref, early_ref, filter_ref, weight_ref, *refs):
    series_refs, (design_ref, *piece_refs, plain, shifted, sems) = refs[:parts], refs[parts:]
    copies = copy_pieces(weight_ref, piece_refs, sems, first)
    block, width = series_refs[0].shape
    chip = order_ref[0] >> 1
    clear_lead(shifted)

    def place(part, inner):
        return pl.ds(pl.multiple_of(place_ref[part] * block + inner, ROWS), ROWS)

    for first in range(ROWS, 2 * block, ROWS):
        row = place(2 * chip + first // block, first % block)
        design_ref[row, :] = early_ref[first - ROWS : first, :]

    def columns(tile, carry):
        column = lane_tile(tile)
        for d in range(parts):
            row = pl.ds(pl.multiple_of(order_ref[d] * block, block), block)
            plain[row, :] = series_refs[d][:, column].astype(jnp.float32)
        shift(plain, shifted)
        for other in range(parts // 2):
            for inner in range(0, 2 * block if other else ROWS, ROWS):
                part = 2 * (chip ^ other) + inner // block
                start = part * block + inner % block
                row = place(part, inner % block)
                for b, rows in enumerate(filter_rows(shifted, filter_ref, column, start)):
                    lanes = pl.ds(pl.multiple_of(b * width + tile * LANES, LANES), LANES)
                    design_ref[row, lanes] = rows.astype(jnp.bfloat16)
        return carry

    lax.fori_loop(0, width // LANES, columns, 0)
    wait_all(copies)


def filter_scratch(time_len):
    return [
        pltpu.VMEM((time_len, LANES), jnp.float32),
        pltpu.VMEM((8 // TAP_SPACING, time_len + TAP_SPACING * FILTER_TAPS + 8, LANES), jnp.float32),
    ]


def product_kernel(taken, extra, first, design_ref, *refs):
    weight_refs, refs = refs[:taken], refs[taken + extra :]
    copies = []
    if first is not None:
        weight_ref, keep_ref, send_ref, *piece_refs, sems = refs
        copies = copy_pieces(weight_ref, piece_refs, sems, first)
    else:
        keep_ref, send_ref = refs
    half, at = keep_ref.shape[0], 0
    for ref in weight_refs:
        for start in range(0, ref.shape[2], COLUMNS):
            weight = ref[:, :, start : min(start + COLUMNS, ref.shape[2])]
            weight = weight.reshape(-1, weight.shape[2])
            total = jnp.dot(design_ref[...], weight, preferred_element_type=jnp.float32)
            columns = slice(at, at + weight.shape[1])
            keep_ref[:, columns] = total[:half].astype(jnp.bfloat16)
            send_ref[:, columns] = total[half:].astype(jnp.bfloat16)
            at += weight.shape[1]
    wait_all(copies)


def product(design, taken, after, weights, first, ahead):
    time_len, lanes = design.shape
    width = sum(piece.shape[2] for piece in taken)
    half = jax.ShapeDtypeStruct((time_len // 2, width), jnp.bfloat16)
    return pl.pallas_call(
        functools.partial(product_kernel, len(taken), len(after), first if ahead else None),
        in_specs=[VMEM()] * (1 + len(taken)) + [ANY()] * (len(after) + bool(ahead)),
        out_specs=[VMEM()] * (2 + len(ahead)),
        out_shape=[half, half] + ahead,
        scratch_shapes=[pltpu.SemaphoreType.DMA((len(ahead),))] if ahead else [],
        compiler_params=pltpu.CompilerParams(vmem_limit_bytes=8 * MIB),
        cost_estimate=cost(2 * time_len * lanes * width, 2 * lanes * width),
        name="product",
    )(design, *taken, *after, *([weights] if ahead else []))


def add_rows(terms, each, first, out_ref):
    at, rows = 0, out_ref.shape[0]
    for c in range(0, len(terms), each):
        chunk, width = terms[c : c + each], terms[c].shape[1]
        total = sum(term[first : first + rows, :].astype(jnp.float32) for term in chunk)
        out_ref[:, at : at + width] = total.astype(jnp.bfloat16)
        at += width


def pack_kernel(spread, widths, places, first, later, outs, order_ref, start_ref, inner_ref, tile_ref, *refs):
    *refs, summed, packed = refs
    if later:
        count, each = later
        *refs, send_ref, keep_ref = refs
    terms, out_refs = refs[: len(refs) - outs], refs[len(refs) - outs :]
    if later:
        rows = packed.shape[1]
        add_rows(terms[-count:], each, 3 * rows, send_ref)
        add_rows(terms[-count:], each, rows, keep_ref)
        terms = terms[:-count]
    owners, rows = packed.shape[:2]
    if first:
        packed[...] = terms.pop(0)[...]
    else:
        packed[...] = jnp.zeros_like(packed)
    at = 0
    for width, spots in zip(widths, places):
        total = 0.0
        for row, column in spots:
            total = total + terms.pop(0)[row : row + rows, column : column + width].astype(jnp.float32)
        summed[:, at : at + width] = total.astype(jnp.bfloat16)
        at += width
    step = VOX_BLOCK // LANES
    slot_rows = lax.broadcasted_iota(jnp.int32, (2 * SLOT_TILE, VOX_BLOCK), 0)

    def moves(index, far):
        block = first + index
        values = summed[:, pl.ds(pl.multiple_of(index * VOX_BLOCK, VOX_BLOCK), VOX_BLOCK)]
        tiles, inner = (
            jnp.concatenate([ref[pl.ds(block * step + i, 1), :] for i in range(step)], axis=1)
            for ref in (tile_ref, inner_ref)
        )
        onehot = jnp.where(inner == slot_rows, 1.0, 0.0).astype(jnp.bfloat16)
        low = [start_ref[block, o] >> 7 for o in range(owners)]
        chosen = []
        for o in range(owners):
            tile = tiles - (o * spread + low[o])
            hit = jnp.where((tile == 2) if far else ((tile == 0) | (tile == 1)), 1.0, 0.0)
            chosen.append(values * hit.astype(jnp.bfloat16))
        moved = lax.dot_general(
            jnp.concatenate(chosen, axis=0), onehot, (((1,), (1,)), ((), ())), preferred_element_type=jnp.float32
        )
        moved = moved.astype(jnp.bfloat16)
        out = []
        for o in range(owners):
            here = moved[o * rows : (o + 1) * rows]
            tile, here = (low[o] + 2, here[:, :SLOT_TILE]) if far else (low[o], here)
            lanes = pl.ds(pl.multiple_of(tile * SLOT_TILE, SLOT_TILE), here.shape[1])
            out.append((o, lanes, here))
        high = [(start_ref[block + 1, o] - 1) >> 7 for o in range(owners)]
        return out, functools.reduce(jnp.maximum, [high[o] - low[o] for o in range(owners)])

    def add(targets):
        sums = [packed[owner, :, lanes] + moved for owner, lanes, moved in targets]
        for (owner, lanes, _), total in zip(targets, sums):
            packed[owner, :, lanes] = total

    def blocks(indices):
        found = [moves(index, False) for index in indices]
        for targets, _ in found:
            add(targets)
        for index, (_, longest) in zip(indices, found):

            @pl.when(longest > 1)
            def _():
                add(moves(index, True)[0])

    count = sum(widths) // VOX_BLOCK

    def some(i, carry):
        blocks([PACK_STEP * i + j for j in range(PACK_STEP)])
        return carry

    lax.fori_loop(0, count // PACK_STEP, some, 0)
    if count % PACK_STEP:
        blocks(range(count - count % PACK_STEP, count))
    if outs == 1:
        out_refs[0][...] = packed[...]
    else:
        for d, ref in enumerate(out_refs):
            ref[...] = packed[order_ref[d], :, : ref.shape[1]]


def shards(features, hrf_filters, weights, voxel_parcel, parcel_owner):
    owners, parts = lax.axis_size("vox"), lax.axis_size("chan")
    me = lax.axis_index("chan")
    voxels = voxel_parcel.shape[0]
    send_cap = 2 * voxels // owners
    bases, depth, _ = weights.shape
    blocks = voxels // VOX_BLOCK
    time_block = features.shape[0]
    time_len = time_block * parts

    series = [lax.dynamic_slice_in_dim(features, (me ^ d) * depth, depth, 1) for d in range(parts)]
    for d in range(1, parts):
        series[d] = lax.ppermute(series[d], "chan", [(i, i ^ d) for i in range(parts)])
    filters = jnp.transpose(hrf_filters, (0, 2, 1))
    spare = -depth % LANES
    lanes = bases * (depth + spare)
    unit = voxels // sum(units for pieces in COPIES for _, units in pieces)
    copied = [unit * sum(units for _, units in pieces) for pieces in COPIES]
    firsts = [sum(copied[:i]) for i in range(len(copied))]
    held = [[] for _ in range(CHUNKS)]

    def room(i):
        if i >= len(COPIES):
            return []
        return [pltpu.VMEM((bases, depth + spare, unit * units), jnp.bfloat16) for _, units in COPIES[i]]

    def keep_pieces(i, pieces):
        for (chunk, _), piece in zip(COPIES[i] if i < len(COPIES) else (), pieces):
            held[chunk].append(piece)

    if spare:
        series = [jnp.pad(part, ((0, 0), (0, spare))) for part in series]
        filters = jnp.pad(filters, ((0, 0), (0, 0), (0, spare)))

    table_rows = -(-parcel_owner.shape[0] // LANES)
    table = jnp.pad(parcel_owner, (0, table_rows * LANES - parcel_owner.shape[0])).reshape(table_rows, LANES)
    marks = -(-(blocks + 1) // 8) * 8
    spread = send_cap // SLOT_TILE + 3
    bits = parts.bit_length() - 1
    order = jnp.arange(parts, dtype=jnp.int32) ^ me
    place = sum(((order >> bit) & 1) << (bits - 1 - bit) for bit in range(bits)).astype(jnp.int32)

    early_rows = 2 * time_block - ROWS
    inner, tiles, starts, early, *pieces = pl.pallas_call(
        functools.partial(early_kernel, owners, spread),
        in_specs=[SMEM(), VMEM(), VMEM(), HBM(), VMEM(), HBM(), ANY()],
        out_specs=[VMEM()] * (4 + len(COPIES[0])),
        out_shape=[
            jax.ShapeDtypeStruct((voxels // LANES, LANES), jnp.int32),
            jax.ShapeDtypeStruct((voxels // LANES, LANES), jnp.int32),
            jax.ShapeDtypeStruct((marks, LANES), jnp.int32),
            jax.ShapeDtypeStruct((early_rows, lanes), jnp.bfloat16),
        ]
        + room(0),
        scratch_shapes=filter_scratch(2 * time_block)
        + [
            pltpu.VMEM(filters.shape, jnp.float32),
            pltpu.VMEM((voxels // LANES, LANES), jnp.int32),
            pltpu.SemaphoreType.DMA((len(COPIES[0]),)),
            pltpu.SemaphoreType.DMA((2,)),
        ],
        compiler_params=pltpu.CompilerParams(vmem_limit_bytes=8 * MIB),
        cost_estimate=cost(0, 2 * bases * depth * copied[0]),
        name="early",
    )(
        order,
        series[0],
        series[1],
        pltpu.with_memory_space_constraint(voxel_parcel.reshape(-1, LANES), pltpu.HBM),
        table,
        pltpu.with_memory_space_constraint(filters, pltpu.HBM),
        weights,
    )
    keep_pieces(0, pieces)
    design, *pieces = pl.pallas_call(
        functools.partial(design_kernel, parts, firsts[1]),
        in_specs=[SMEM(), SMEM(), VMEM(), VMEM(), ANY()] + [VMEM()] * parts,
        out_specs=[VMEM()] * (1 + len(COPIES[1])),
        out_shape=[jax.ShapeDtypeStruct((time_len, lanes), jnp.bfloat16)] + room(1),
        scratch_shapes=filter_scratch(time_len) + [pltpu.SemaphoreType.DMA((len(COPIES[1]),))],
        compiler_params=pltpu.CompilerParams(vmem_limit_bytes=8 * MIB),
        cost_estimate=cost(0, 2 * bases * depth * copied[1]),
        name="design",
    )(order, place, early, filters, weights, *series)
    keep_pieces(1, pieces)

    half = time_block // 2
    widths, sums, sent, got = [], [], [], []
    for c in range(CHUNKS):
        after = sent[max(c - 2, 0) : max(c - 1, 0)] + got[max(c - 3, 0) : max(c - 2, 0)]
        ahead = room(c + 2)
        keep, send, *pieces = product(design, held[c], after, weights, firsts[c + 2] if ahead else 0, ahead)
        keep_pieces(c + 2, pieces)
        widths.append(keep.shape[1])
        own = [keep]
        for bit in range(bits):
            if bit > 0:
                rows = own[-1].shape[0] // 2
                send = added(own, rows, half if bit == bits - 1 else rows)
                if bit == bits - 1:
                    sent.append(send)
            own.append(lax.ppermute(send, "chan", [(i, i ^ (1 << bit)) for i in range(parts)]))
        sums.append(own)
        got.append(own[-1])
    here = lax.axis_index("vox")
    targets = jnp.arange(owners, dtype=jnp.int32) ^ here

    def pack(chunks, terms, spots, packed=(), later=()):
        sizes = [widths[c] for c in chunks]
        spec = (len(later), bits) if later else None
        if chunks[-1] == CHUNKS - 1:
            outs = [pltpu.VMEM((half, send_cap), jnp.bfloat16)] * owners
        else:
            outs = [jax.ShapeDtypeStruct((owners, half, spread * SLOT_TILE), jnp.bfloat16)]
        more = []
        if later:
            more = [jax.ShapeDtypeStruct((half, voxels), jnp.bfloat16), pltpu.VMEM((half, voxels), jnp.bfloat16)]
        return pl.pallas_call(
            functools.partial(
                pack_kernel, spread, sizes, spots, sum(widths[: chunks[0]]) // VOX_BLOCK, spec, len(outs)
            ),
            in_specs=[SMEM(), SMEM(), VMEM(), VMEM()] + [VMEM()] * (len(packed) + len(terms) + len(later)),
            out_specs=[VMEM()] * (len(outs) + len(more)),
            out_shape=outs + more,
            scratch_shapes=[
                pltpu.VMEM((half, sum(sizes)), jnp.bfloat16),
                pltpu.VMEM((owners, half, spread * SLOT_TILE), jnp.bfloat16),
            ],
            compiler_params=pltpu.CompilerParams(vmem_limit_bytes=8 * MIB),
            cost_estimate=cost(2 * half * owners * VOX_BLOCK * sum(sizes), 4 * half * sum(sizes)),
            name="pack",
        )(targets, starts, inner, tiles, *packed, *terms, *later)

    turns = range(owners - 1, 0, -1)

    def deliver(packed):
        got = list(packed)
        for d in turns:
            got[d] = lax.ppermute(packed[d], "vox", [(i, i ^ d) for i in range(owners)])
        return got

    def early_terms(chunks):
        return [term for c in chunks for term in sums[c]], [[(0, 0)] * len(sums[c]) for c in chunks]

    packed = []
    for low, high in zip(PACKS, PACKS[1:]):
        chunks = range(low, high)
        later = [term for own in sums for term in own[:-1]] if high == CHUNKS else []
        packed = pack(chunks, *early_terms(chunks), packed=packed, later=later)
    *one, late_send, late_own = packed
    late = lax.ppermute(late_send, "chan", [(i, i ^ (1 << (bits - 1))) for i in range(parts)])
    one = deliver(one)
    starting = [sum(widths[:c]) for c in range(CHUNKS)]
    two = pack(range(CHUNKS), [late_own, late] * CHUNKS, [[(0, first)] * 2 for first in starting])
    two = pl.pallas_call(
        gate_kernel,
        in_specs=[VMEM()] * (owners + GATE),
        out_specs=[VMEM()] * owners,
        out_shape=[pltpu.VMEM((half, send_cap), jnp.bfloat16)] * owners,
        compiler_params=pltpu.CompilerParams(vmem_limit_bytes=4 * MIB),
        name="gate",
    )(*two, *(one[d] for d in turns[:GATE]))
    two = deliver(two)
    owned = None
    everyone = [*turns, 0]
    for first, got, which in ((0, one, everyone), (half, two, everyone)):
        given = [] if owned is None else [owned]
        count = len(which)
        owned = pl.pallas_call(
            functools.partial(assemble_kernel, tuple(which), first),
            in_specs=[SMEM()] + [VMEM()] * count + [HBM()] * len(given),
            out_specs=HBM(),
            out_shape=jax.ShapeDtypeStruct((owners, time_block, send_cap), jnp.bfloat16),
            scratch_shapes=[pltpu.SemaphoreType.DMA((count,))],
            input_output_aliases={1 + count: 0} if given else {},
            compiler_params=pltpu.CompilerParams(vmem_limit_bytes=4 * MIB),
            name="assemble",
        )(targets, *(got[d] for d in which), *given)
    return jnp.transpose(owned, (0, 2, 1))


def gate_kernel(*refs):
    count = (len(refs) - GATE) // 2
    for given, out in zip(refs[:count], refs[count + GATE :]):
        out[...] = given[...]


def assemble_kernel(which, first, order_ref, *refs):
    parts, (out_ref, sems) = refs[: len(which)], refs[-2:]
    copies = []
    for i, (d, ref) in enumerate(zip(which, parts)):
        rows = pl.ds(first, ref.shape[0])
        copies.append(pltpu.make_async_copy(ref, out_ref.at[order_ref[d], rows, :], sems.at[i]))
        copies[-1].start()
    wait_all(copies)


def added(terms, first, rows):
    return sum(term[first : first + rows].astype(jnp.float32) for term in terms).astype(jnp.bfloat16)


def solution(mesh):
    return jax.shard_map(
        shards,
        mesh=mesh,
        in_specs=(P("chan", None), P(None, "chan", None), P(None, "chan", "vox"), P("vox"), P()),
        out_specs=P("vox", None, "chan"),
        check_vma=False,
    )
```

```python
import functools

import jax
import jax.numpy as jnp
from jax import lax
from jax.experimental import pallas as pl
from jax.experimental.pallas import tpu as pltpu
from jax.sharding import PartitionSpec as P

FILTER_TAPS = 16
TAP_SPACING = 2
LANES = 128
SLOT_TILE = 128
VOX_BLOCK = 256
COLUMNS = 512
ROWS = 32
CHUNKS = 4
COPIES = (((0, 4), (1, 6)), ((2, 2), (2, 2)), (), ((2, 2), (3, 1)), ((3, 2), (3, 1)))
PACKS = (0, 2, 3, 4)
PACK_STEP = 4
MIB = 1 << 20

VMEM = functools.partial(pl.BlockSpec, memory_space=pltpu.VMEM)
SMEM = functools.partial(pl.BlockSpec, memory_space=pltpu.SMEM)
ANY = functools.partial(pl.BlockSpec, memory_space=pl.ANY)
HBM = functools.partial(pl.BlockSpec, memory_space=pltpu.HBM)


def copy_pieces(weight_ref, piece_refs, sems, first):
    depth, copies = weight_ref.shape[1], []
    for i, ref in enumerate(piece_refs):
        if ref.shape[1] > depth:
            ref[:, depth:, :] = jnp.zeros_like(ref[:, depth:, :])
        copy = pltpu.make_async_copy(
            weight_ref.at[:, :, pl.ds(first, ref.shape[2])], ref.at[:, pl.ds(0, depth), :], sems.at[i]
        )
        copy.start()
        copies.append(copy)
        first += ref.shape[2]
    return copies


def wait_all(copies):
    for copy in copies:
        copy.wait()


def cost(flops, read):
    return pl.CostEstimate(flops=flops, bytes_accessed=read, transcendentals=0)


def places(owners, spread, parcel_ref, table_ref, inner_ref, tile_ref, start_ref):
    rows = parcel_ref.shape[0]
    parcel = parcel_ref[...]
    high, low = parcel >> 7, parcel & 127
    owner = jnp.zeros_like(parcel)
    for entry in range(table_ref.shape[0]):
        line = jnp.broadcast_to(table_ref[entry : entry + 1, :], parcel.shape)
        found = jnp.take_along_axis(line, low, axis=1, mode="promise_in_bounds")
        owner = jnp.where(high == entry, found, owner)

    def below(shape, scale=1):
        less = lax.broadcasted_iota(jnp.int32, shape, 1) < scale * lax.broadcasted_iota(jnp.int32, shape, 0)
        return less.astype(jnp.float32).astype(jnp.bfloat16)

    lane = lax.broadcasted_iota(jnp.int32, (LANES, LANES), 1)
    above = (lax.broadcasted_iota(jnp.int32, (LANES, LANES), 0) < lane).astype(jnp.float32).astype(jnp.bfloat16)
    ones = jnp.ones((LANES, LANES), jnp.bfloat16)
    marks = start_ref.shape[0]
    ahead, block_ahead = below((rows, rows)), below((marks, rows), VOX_BLOCK // LANES)
    mark_lane = lax.broadcasted_iota(jnp.int32, (marks, LANES), 1)
    dot = functools.partial(jnp.dot, preferred_element_type=jnp.float32)
    row_block = lax.broadcasted_iota(jnp.int32, (rows, rows), 0) & -(VOX_BLOCK // LANES)
    before = lax.broadcasted_iota(jnp.int32, (rows, rows), 1) < row_block
    before = before.astype(jnp.float32).astype(jnp.bfloat16)
    slots = jnp.zeros(parcel.shape, jnp.float32)
    bases = jnp.zeros(parcel.shape, jnp.float32)
    starts = jnp.zeros((marks, LANES), jnp.float32)
    for o in range(owners):
        mine = owner == o
        hot = mine.astype(jnp.float32).astype(jnp.bfloat16)
        totals = dot(hot, ones).astype(jnp.bfloat16)
        slots = jnp.where(mine, dot(hot, above) + dot(ahead, totals), slots)
        bases = jnp.where(mine, dot(before, totals), bases)
        starts = jnp.where(mark_lane == o, dot(block_ahead, totals), starts)
    slots = slots.astype(jnp.int32)
    start_ref[...] = starts.astype(jnp.int32)
    tile_ref[...] = owner * spread + (slots >> 7)
    inner_ref[...] = (slots - (bases.astype(jnp.int32) & -SLOT_TILE)) & (2 * SLOT_TILE - 1)


def clear_lead(shifted):
    lead = TAP_SPACING * FILTER_TAPS
    for s in range(shifted.shape[0]):
        shifted[s, : lead + 8, :] = jnp.zeros((lead + 8, LANES), jnp.float32)


def shift(plain, shifted):
    lead, time_len = TAP_SPACING * FILTER_TAPS, plain.shape[0]
    series = plain[...]
    for s in range(shifted.shape[0]):
        shifted[s, lead + s * TAP_SPACING : lead + s * TAP_SPACING + time_len, :] = series


def filter_rows(shifted, filter_ref, column, first):
    lead = TAP_SPACING * FILTER_TAPS
    sums = [jnp.zeros((ROWS, LANES), jnp.float32) for _ in range(filter_ref.shape[0])]
    for tap in range(FILTER_TAPS):
        delay = tap * TAP_SPACING
        start = lead + first - 8 * (delay // 8)
        if not isinstance(start, int):
            start = pl.multiple_of(start, 8)
        lagged = shifted[(delay % 8) // TAP_SPACING, pl.ds(start, ROWS), :]
        for b in range(len(sums)):
            sums[b] = sums[b] + filter_ref[b, tap : tap + 1, column] * lagged
    return sums


def lane_tile(tile):
    return pl.ds(pl.multiple_of(tile * LANES, LANES), LANES)


def early_kernel(owners, spread, order_ref, own_ref, pair_ref, parcel_hbm, table_ref, filter_hbm, weight_ref, *refs):
    inner_ref, tile_ref, start_ref, design_ref, *piece_refs, plain, shifted, filter_ref, parcel_ref, sems, small_sems = refs
    load_filter = pltpu.make_async_copy(filter_hbm, filter_ref, small_sems.at[0])
    load_parcel = pltpu.make_async_copy(parcel_hbm, parcel_ref, small_sems.at[1])
    load_filter.start()
    load_parcel.start()
    copies = copy_pieces(weight_ref, piece_refs, sems, 0)
    block, width = own_ref.shape
    core = lax.rem(order_ref[0], 2)
    own = pl.ds(pl.multiple_of(core * block, block), block)
    pair = pl.ds(pl.multiple_of((1 - core) * block, block), block)
    clear_lead(shifted)
    load_filter.wait()

    def columns(tile, carry):
        column = lane_tile(tile)
        plain[own, :] = own_ref[:, column].astype(jnp.float32)
        plain[pair, :] = pair_ref[:, column].astype(jnp.float32)
        shift(plain, shifted)
        for first in range(ROWS, 2 * block, ROWS):
            for b, rows in enumerate(filter_rows(shifted, filter_ref, column, first)):
                lanes = pl.ds(pl.multiple_of(b * width + tile * LANES, LANES), LANES)
                design_ref[first - ROWS : first, lanes] = rows.astype(jnp.bfloat16)
        return carry

    lax.fori_loop(0, width // LANES, columns, 0)
    load_parcel.wait()
    places(owners, spread, parcel_ref, table_ref, inner_ref, tile_ref, start_ref)
    wait_all(copies)


def design_kernel(parts, first, order_ref, place_ref, early_ref, filter_ref, weight_ref, *refs):
    series_refs, (design_ref, *piece_refs, plain, shifted, sems) = refs[:parts], refs[parts:]
    copies = copy_pieces(weight_ref, piece_refs, sems, first)
    block, width = series_refs[0].shape
    chip = order_ref[0] >> 1
    clear_lead(shifted)

    def place(part, inner):
        return pl.ds(pl.multiple_of(place_ref[part] * block + inner, ROWS), ROWS)

    for first in range(ROWS, 2 * block, ROWS):
        row = place(2 * chip + first // block, first % block)
        design_ref[row, :] = early_ref[first - ROWS : first, :]

    def columns(tile, carry):
        column = lane_tile(tile)
        for d in range(parts):
            row = pl.ds(pl.multiple_of(order_ref[d] * block, block), block)
            plain[row, :] = series_refs[d][:, column].astype(jnp.float32)
        shift(plain, shifted)
        for other in range(parts // 2):
            for inner in range(0, 2 * block if other else ROWS, ROWS):
                part = 2 * (chip ^ other) + inner // block
                start = part * block + inner % block
                row = place(part, inner % block)
                for b, rows in enumerate(filter_rows(shifted, filter_ref, column, start)):
                    lanes = pl.ds(pl.multiple_of(b * width + tile * LANES, LANES), LANES)
                    design_ref[row, lanes] = rows.astype(jnp.bfloat16)
        return carry

    lax.fori_loop(0, width // LANES, columns, 0)
    wait_all(copies)


def filter_scratch(time_len):
    return [
        pltpu.VMEM((time_len, LANES), jnp.float32),
        pltpu.VMEM((8 // TAP_SPACING, time_len + TAP_SPACING * FILTER_TAPS + 8, LANES), jnp.float32),
    ]


def product_kernel(taken, extra, first, design_ref, *refs):
    weight_refs, refs = refs[:taken], refs[taken + extra :]
    copies = []
    if first is not None:
        weight_ref, keep_ref, send_ref, *piece_refs, sems = refs
        copies = copy_pieces(weight_ref, piece_refs, sems, first)
    else:
        keep_ref, send_ref = refs
    half, at = keep_ref.shape[0], 0
    for ref in weight_refs:
        for start in range(0, ref.shape[2], COLUMNS):
            weight = ref[:, :, start : min(start + COLUMNS, ref.shape[2])]
            weight = weight.reshape(-1, weight.shape[2])
            total = jnp.dot(design_ref[...], weight, preferred_element_type=jnp.float32)
            columns = slice(at, at + weight.shape[1])
            keep_ref[:, columns] = total[:half].astype(jnp.bfloat16)
            send_ref[:, columns] = total[half:].astype(jnp.bfloat16)
            at += weight.shape[1]
    wait_all(copies)


def product(design, taken, after, weights, first, ahead):
    time_len, lanes = design.shape
    width = sum(piece.shape[2] for piece in taken)
    half = jax.ShapeDtypeStruct((time_len // 2, width), jnp.bfloat16)
    return pl.pallas_call(
        functools.partial(product_kernel, len(taken), len(after), first if ahead else None),
        in_specs=[VMEM()] * (1 + len(taken)) + [ANY()] * (len(after) + bool(ahead)),
        out_specs=[VMEM()] * (2 + len(ahead)),
        out_shape=[half, half] + ahead,
        scratch_shapes=[pltpu.SemaphoreType.DMA((len(ahead),))] if ahead else [],
        compiler_params=pltpu.CompilerParams(vmem_limit_bytes=8 * MIB),
        cost_estimate=cost(2 * time_len * lanes * width, 2 * lanes * width),
        name="product",
    )(design, *taken, *after, *([weights] if ahead else []))


def pack_kernel(spread, widths, places, first, outs, order_ref, start_ref, inner_ref, tile_ref, *refs):
    *refs, summed, packed = refs
    terms, out_refs = refs[: len(refs) - outs], refs[len(refs) - outs :]
    owners, rows = packed.shape[:2]
    if first:
        packed[...] = terms.pop(0)[...]
    else:
        packed[...] = jnp.zeros_like(packed)
    at = 0
    for width, count in zip(widths, places):
        total = sum(terms.pop(0)[:rows, :].astype(jnp.float32) for _ in range(count))
        summed[:, at : at + width] = total.astype(jnp.bfloat16)
        at += width
    step = VOX_BLOCK // LANES
    slot_rows = lax.broadcasted_iota(jnp.int32, (2 * SLOT_TILE, VOX_BLOCK), 0)

    def moves(index, far):
        block = first + index
        values = summed[:, pl.ds(pl.multiple_of(index * VOX_BLOCK, VOX_BLOCK), VOX_BLOCK)]
        tiles, inner = (
            jnp.concatenate([ref[pl.ds(block * step + i, 1), :] for i in range(step)], axis=1)
            for ref in (tile_ref, inner_ref)
        )
        onehot = jnp.where(inner == slot_rows, 1.0, 0.0).astype(jnp.bfloat16)
        low = [start_ref[block, o] >> 7 for o in range(owners)]
        chosen = []
        for o in range(owners):
            tile = tiles - (o * spread + low[o])
            hit = jnp.where((tile == 2) if far else ((tile == 0) | (tile == 1)), 1.0, 0.0)
            chosen.append(values * hit.astype(jnp.bfloat16))
        moved = lax.dot_general(
            jnp.concatenate(chosen, axis=0), onehot, (((1,), (1,)), ((), ())), preferred_element_type=jnp.float32
        )
        moved = moved.astype(jnp.bfloat16)
        out = []
        for o in range(owners):
            here = moved[o * rows : (o + 1) * rows]
            tile, here = (low[o] + 2, here[:, :SLOT_TILE]) if far else (low[o], here)
            lanes = pl.ds(pl.multiple_of(tile * SLOT_TILE, SLOT_TILE), here.shape[1])
            out.append((o, lanes, here))
        high = [(start_ref[block + 1, o] - 1) >> 7 for o in range(owners)]
        return out, functools.reduce(jnp.maximum, [high[o] - low[o] for o in range(owners)])

    def add(targets):
        sums = [packed[owner, :, lanes] + moved for owner, lanes, moved in targets]
        for (owner, lanes, _), total in zip(targets, sums):
            packed[owner, :, lanes] = total

    def blocks(indices):
        found = [moves(index, False) for index in indices]
        for targets, _ in found:
            add(targets)
        for index, (_, longest) in zip(indices, found):

            @pl.when(longest > 1)
            def _():
                add(moves(index, True)[0])

    count = sum(widths) // VOX_BLOCK

    def some(i, carry):
        blocks([PACK_STEP * i + j for j in range(PACK_STEP)])
        return carry

    lax.fori_loop(0, count // PACK_STEP, some, 0)
    if count % PACK_STEP:
        blocks(range(count - count % PACK_STEP, count))
    if outs == 1:
        out_refs[0][...] = packed[...]
    else:
        for d, ref in enumerate(out_refs):
            ref[...] = packed[order_ref[d], :, : ref.shape[1]]


def shards(features, hrf_filters, weights, voxel_parcel, parcel_owner):
    owners, parts = lax.axis_size("vox"), lax.axis_size("chan")
    me = lax.axis_index("chan")
    voxels = voxel_parcel.shape[0]
    send_cap = 2 * voxels // owners
    bases, depth, _ = weights.shape
    blocks = voxels // VOX_BLOCK
    time_block = features.shape[0]
    time_len = time_block * parts

    series = [lax.dynamic_slice_in_dim(features, (me ^ d) * depth, depth, 1) for d in range(parts)]
    for d in range(1, parts):
        series[d] = lax.ppermute(series[d], "chan", [(i, i ^ d) for i in range(parts)])
    filters = jnp.transpose(hrf_filters, (0, 2, 1))
    spare = -depth % LANES
    lanes = bases * (depth + spare)
    unit = voxels // sum(units for pieces in COPIES for _, units in pieces)
    copied = [unit * sum(units for _, units in pieces) for pieces in COPIES]
    firsts = [sum(copied[:i]) for i in range(len(copied))]
    held = [[] for _ in range(CHUNKS)]

    def room(i):
        if i >= len(COPIES):
            return []
        return [pltpu.VMEM((bases, depth + spare, unit * units), jnp.bfloat16) for _, units in COPIES[i]]

    def keep_pieces(i, pieces):
        for (chunk, _), piece in zip(COPIES[i] if i < len(COPIES) else (), pieces):
            held[chunk].append(piece)

    if spare:
        series = [jnp.pad(part, ((0, 0), (0, spare))) for part in series]
        filters = jnp.pad(filters, ((0, 0), (0, 0), (0, spare)))

    table_rows = -(-parcel_owner.shape[0] // LANES)
    table = jnp.pad(parcel_owner, (0, table_rows * LANES - parcel_owner.shape[0])).reshape(table_rows, LANES)
    marks = -(-(blocks + 1) // 8) * 8
    spread = send_cap // SLOT_TILE + 3
    bits = parts.bit_length() - 1
    order = jnp.arange(parts, dtype=jnp.int32) ^ me
    place = sum(((order >> bit) & 1) << (bits - 1 - bit) for bit in range(bits)).astype(jnp.int32)

    early_rows = 2 * time_block - ROWS
    inner, tiles, starts, early, *pieces = pl.pallas_call(
        functools.partial(early_kernel, owners, spread),
        in_specs=[SMEM(), VMEM(), VMEM(), HBM(), VMEM(), HBM(), ANY()],
        out_specs=[VMEM()] * (4 + len(COPIES[0])),
        out_shape=[
            jax.ShapeDtypeStruct((voxels // LANES, LANES), jnp.int32),
            jax.ShapeDtypeStruct((voxels // LANES, LANES), jnp.int32),
            jax.ShapeDtypeStruct((marks, LANES), jnp.int32),
            jax.ShapeDtypeStruct((early_rows, lanes), jnp.bfloat16),
        ]
        + room(0),
        scratch_shapes=filter_scratch(2 * time_block)
        + [
            pltpu.VMEM(filters.shape, jnp.float32),
            pltpu.VMEM((voxels // LANES, LANES), jnp.int32),
            pltpu.SemaphoreType.DMA((len(COPIES[0]),)),
            pltpu.SemaphoreType.DMA((2,)),
        ],
        compiler_params=pltpu.CompilerParams(vmem_limit_bytes=8 * MIB),
        cost_estimate=cost(0, 2 * bases * depth * copied[0]),
        name="early",
    )(
        order,
        series[0],
        series[1],
        pltpu.with_memory_space_constraint(voxel_parcel.reshape(-1, LANES), pltpu.HBM),
        table,
        pltpu.with_memory_space_constraint(filters, pltpu.HBM),
        weights,
    )
    keep_pieces(0, pieces)
    design, *pieces = pl.pallas_call(
        functools.partial(design_kernel, parts, firsts[1]),
        in_specs=[SMEM(), SMEM(), VMEM(), VMEM(), ANY()] + [VMEM()] * parts,
        out_specs=[VMEM()] * (1 + len(COPIES[1])),
        out_shape=[jax.ShapeDtypeStruct((time_len, lanes), jnp.bfloat16)] + room(1),
        scratch_shapes=filter_scratch(time_len) + [pltpu.SemaphoreType.DMA((len(COPIES[1]),))],
        compiler_params=pltpu.CompilerParams(vmem_limit_bytes=8 * MIB),
        cost_estimate=cost(0, 2 * bases * depth * copied[1]),
        name="design",
    )(order, place, early, filters, weights, *series)
    keep_pieces(1, pieces)

    widths, sums, sent, got = [], [], [], []
    for c in range(CHUNKS):
        after = sent[max(c - 2, 0) : max(c - 1, 0)] + got[max(c - 3, 0) : max(c - 2, 0)]
        ahead = room(c + 2)
        keep, send, *pieces = product(design, held[c], after, weights, firsts[c + 2] if ahead else 0, ahead)
        keep_pieces(c + 2, pieces)
        widths.append(keep.shape[1])
        own = [keep]
        for bit in range(bits):
            if bit > 0:
                rows = own[-1].shape[0] // 2
                send = added(own, rows, rows)
                if bit == bits - 1:
                    sent.append(send)
            own.append(lax.ppermute(send, "chan", [(i, i ^ (1 << bit)) for i in range(parts)]))
        sums.append(own)
        got.append(own[-1])
    here = lax.axis_index("vox")
    targets = jnp.arange(owners, dtype=jnp.int32) ^ here

    def pack(chunks, packed):
        sizes = [widths[c] for c in chunks]
        terms = [term for c in chunks for term in sums[c]]
        if chunks[-1] == CHUNKS - 1:
            outs = [pltpu.VMEM((time_block, send_cap), jnp.bfloat16)] * owners
        else:
            outs = [jax.ShapeDtypeStruct((owners, time_block, spread * SLOT_TILE), jnp.bfloat16)]
        counts = [len(sums[c]) for c in chunks]
        return pl.pallas_call(
            functools.partial(
                pack_kernel, spread, sizes, counts, sum(widths[: chunks[0]]) // VOX_BLOCK, len(outs)
            ),
            in_specs=[SMEM(), SMEM(), VMEM(), VMEM()] + [VMEM()] * (len(packed) + len(terms)),
            out_specs=[VMEM()] * len(outs),
            out_shape=outs,
            scratch_shapes=[
                pltpu.VMEM((time_block, sum(sizes)), jnp.bfloat16),
                pltpu.VMEM((owners, time_block, spread * SLOT_TILE), jnp.bfloat16),
            ],
            compiler_params=pltpu.CompilerParams(vmem_limit_bytes=8 * MIB),
            cost_estimate=cost(2 * time_block * owners * VOX_BLOCK * sum(sizes), 4 * time_block * sum(sizes)),
            name="pack",
        )(targets, starts, inner, tiles, *packed, *terms)

    turns = range(owners - 1, 0, -1)

    def deliver(packed):
        got = list(packed)
        for d in turns:
            got[d] = lax.ppermute(packed[d], "vox", [(i, i ^ d) for i in range(owners)])
        return got

    packed = []
    for low, high in zip(PACKS, PACKS[1:]):
        packed = pack(range(low, high), packed)
    got = deliver(packed)
    owned, middle = None, owners // 2
    for which in ([0, *turns[: middle - 1]], turns[middle - 1 :]):
        given = [] if owned is None else [owned]
        count = len(which)
        owned = pl.pallas_call(
            functools.partial(assemble_kernel, tuple(which)),
            in_specs=[SMEM()] + [VMEM()] * count + [HBM()] * len(given),
            out_specs=HBM(),
            out_shape=jax.ShapeDtypeStruct((owners, time_block, send_cap), jnp.bfloat16),
            scratch_shapes=[pltpu.SemaphoreType.DMA((count,))],
            input_output_aliases={1 + count: 0} if given else {},
            compiler_params=pltpu.CompilerParams(vmem_limit_bytes=4 * MIB),
            name="assemble",
        )(targets, *(got[d] for d in which), *given)
    return jnp.transpose(owned, (0, 2, 1))


def assemble_kernel(which, order_ref, *refs):
    parts, (out_ref, sems) = refs[: len(which)], refs[-2:]
    copies = []
    for i, (d, ref) in enumerate(zip(which, parts)):
        copies.append(pltpu.make_async_copy(ref, out_ref.at[order_ref[d]], sems.at[i]))
        copies[-1].start()
    wait_all(copies)


def added(terms, first, rows):
    return sum(term[first : first + rows].astype(jnp.float32) for term in terms).astype(jnp.bfloat16)


def solution(mesh):
    return jax.shard_map(
        shards,
        mesh=mesh,
        in_specs=(P("chan", None), P(None, "chan", None), P(None, "chan", "vox"), P("vox"), P()),
        out_specs=P("vox", None, "chan"),
        check_vma=False,
    )
```

```python
import functools

import jax
import jax.numpy as jnp
from jax import lax
from jax.experimental import pallas as pl
from jax.experimental.pallas import tpu as pltpu
from jax.sharding import PartitionSpec as P

FILTER_TAPS = 16
TAP_SPACING = 2
LANES = 128
SLOT_TILE = 128
VOX_BLOCK = 256
COLUMNS = 512
ROWS = 32
CHUNKS = 3
COPIES = (((0, 6), (1, 4)), ((1, 2), (1, 2)), ((2, 2), (2, 1)), ((2, 2), (2, 1)))
PACKS = (0, 1, 2, 3)
PACK_STEP = 4
GATE = 2
MIB = 1 << 20

VMEM = functools.partial(pl.BlockSpec, memory_space=pltpu.VMEM)
SMEM = functools.partial(pl.BlockSpec, memory_space=pltpu.SMEM)
ANY = functools.partial(pl.BlockSpec, memory_space=pl.ANY)
HBM = functools.partial(pl.BlockSpec, memory_space=pltpu.HBM)


def copy_pieces(weight_ref, piece_refs, sems, first):
    depth, copies = weight_ref.shape[1], []
    for i, ref in enumerate(piece_refs):
        if ref.shape[1] > depth:
            ref[:, depth:, :] = jnp.zeros_like(ref[:, depth:, :])
        copy = pltpu.make_async_copy(
            weight_ref.at[:, :, pl.ds(first, ref.shape[2])], ref.at[:, pl.ds(0, depth), :], sems.at[i]
        )
        copy.start()
        copies.append(copy)
        first += ref.shape[2]
    return copies


def wait_all(copies):
    for copy in copies:
        copy.wait()


def cost(flops, read):
    return pl.CostEstimate(flops=flops, bytes_accessed=read, transcendentals=0)


def places(owners, spread, parcel_ref, table_ref, inner_ref, tile_ref, start_ref):
    rows = parcel_ref.shape[0]
    parcel = parcel_ref[...]
    high, low = parcel >> 7, parcel & 127
    owner = jnp.zeros_like(parcel)
    for entry in range(table_ref.shape[0]):
        line = jnp.broadcast_to(table_ref[entry : entry + 1, :], parcel.shape)
        found = jnp.take_along_axis(line, low, axis=1, mode="promise_in_bounds")
        owner = jnp.where(high == entry, found, owner)

    def below(shape, scale=1):
        less = lax.broadcasted_iota(jnp.int32, shape, 1) < scale * lax.broadcasted_iota(jnp.int32, shape, 0)
        return less.astype(jnp.float32).astype(jnp.bfloat16)

    lane = lax.broadcasted_iota(jnp.int32, (LANES, LANES), 1)
    above = (lax.broadcasted_iota(jnp.int32, (LANES, LANES), 0) < lane).astype(jnp.float32).astype(jnp.bfloat16)
    ones = jnp.ones((LANES, LANES), jnp.bfloat16)
    marks = start_ref.shape[0]
    ahead, block_ahead = below((rows, rows)), below((marks, rows), VOX_BLOCK // LANES)
    mark_lane = lax.broadcasted_iota(jnp.int32, (marks, LANES), 1)
    dot = functools.partial(jnp.dot, preferred_element_type=jnp.float32)
    row_block = lax.broadcasted_iota(jnp.int32, (rows, rows), 0) & -(VOX_BLOCK // LANES)
    before = lax.broadcasted_iota(jnp.int32, (rows, rows), 1) < row_block
    before = before.astype(jnp.float32).astype(jnp.bfloat16)
    slots = jnp.zeros(parcel.shape, jnp.float32)
    bases = jnp.zeros(parcel.shape, jnp.float32)
    starts = jnp.zeros((marks, LANES), jnp.float32)
    for o in range(owners):
        mine = owner == o
        hot = mine.astype(jnp.float32).astype(jnp.bfloat16)
        totals = dot(hot, ones).astype(jnp.bfloat16)
        slots = jnp.where(mine, dot(hot, above) + dot(ahead, totals), slots)
        bases = jnp.where(mine, dot(before, totals), bases)
        starts = jnp.where(mark_lane == o, dot(block_ahead, totals), starts)
    slots = slots.astype(jnp.int32)
    start_ref[...] = starts.astype(jnp.int32)
    tile_ref[...] = owner * spread + (slots >> 7)
    inner_ref[...] = (slots - (bases.astype(jnp.int32) & -SLOT_TILE)) & (2 * SLOT_TILE - 1)


def clear_lead(shifted):
    lead = TAP_SPACING * FILTER_TAPS
    for s in range(shifted.shape[0]):
        shifted[s, : lead + 8, :] = jnp.zeros((lead + 8, LANES), jnp.float32)


def shift(plain, shifted):
    lead, time_len = TAP_SPACING * FILTER_TAPS, plain.shape[0]
    series = plain[...]
    for s in range(shifted.shape[0]):
        shifted[s, lead + s * TAP_SPACING : lead + s * TAP_SPACING + time_len, :] = series


def filter_rows(shifted, filter_ref, column, first):
    lead = TAP_SPACING * FILTER_TAPS
    sums = [jnp.zeros((ROWS, LANES), jnp.float32) for _ in range(filter_ref.shape[0])]
    for tap in range(FILTER_TAPS):
        delay = tap * TAP_SPACING
        start = lead + first - 8 * (delay // 8)
        if not isinstance(start, int):
            start = pl.multiple_of(start, 8)
        lagged = shifted[(delay % 8) // TAP_SPACING, pl.ds(start, ROWS), :]
        for b in range(len(sums)):
            sums[b] = sums[b] + filter_ref[b, tap : tap + 1, column] * lagged
    return sums


def lane_tile(tile):
    return pl.ds(pl.multiple_of(tile * LANES, LANES), LANES)


def early_kernel(owners, spread, order_ref, own_ref, pair_ref, parcel_hbm, table_ref, filter_hbm, weight_ref, *refs):
    inner_ref, tile_ref, start_ref, design_ref, *piece_refs, plain, shifted, filter_ref, parcel_ref, sems, small_sems = refs
    load_filter = pltpu.make_async_copy(filter_hbm, filter_ref, small_sems.at[0])
    load_parcel = pltpu.make_async_copy(parcel_hbm, parcel_ref, small_sems.at[1])
    load_filter.start()
    load_parcel.start()
    copies = copy_pieces(weight_ref, piece_refs, sems, 0)
    block, width = own_ref.shape
    core = lax.rem(order_ref[0], 2)
    own = pl.ds(pl.multiple_of(core * block, block), block)
    pair = pl.ds(pl.multiple_of((1 - core) * block, block), block)
    clear_lead(shifted)
    load_filter.wait()

    def columns(tile, carry):
        column = lane_tile(tile)
        plain[own, :] = own_ref[:, column].astype(jnp.float32)
        plain[pair, :] = pair_ref[:, column].astype(jnp.float32)
        shift(plain, shifted)
        for first in range(ROWS, 2 * block, ROWS):
            for b, rows in enumerate(filter_rows(shifted, filter_ref, column, first)):
                lanes = pl.ds(pl.multiple_of(b * width + tile * LANES, LANES), LANES)
                design_ref[first - ROWS : first, lanes] = rows.astype(jnp.bfloat16)
        return carry

    lax.fori_loop(0, width // LANES, columns, 0)
    load_parcel.wait()
    places(owners, spread, parcel_ref, table_ref, inner_ref, tile_ref, start_ref)
    wait_all(copies)


def design_kernel(parts, first, order_ref, place_ref, early_ref, filter_ref, weight_ref, *refs):
    series_refs, (design_ref, *piece_refs, plain, shifted, sems) = refs[:parts], refs[parts:]
    copies = copy_pieces(weight_ref, piece_refs, sems, first)
    block, width = series_refs[0].shape
    chip = order_ref[0] >> 1
    clear_lead(shifted)

    def place(part, inner):
        return pl.ds(pl.multiple_of(place_ref[part] * block + inner, ROWS), ROWS)

    for first in range(ROWS, 2 * block, ROWS):
        row = place(2 * chip + first // block, first % block)
        design_ref[row, :] = early_ref[first - ROWS : first, :]

    def columns(tile, carry):
        column = lane_tile(tile)
        for d in range(parts):
            row = pl.ds(pl.multiple_of(order_ref[d] * block, block), block)
            plain[row, :] = series_refs[d][:, column].astype(jnp.float32)
        shift(plain, shifted)
        for other in range(parts // 2):
            for inner in range(0, 2 * block if other else ROWS, ROWS):
                part = 2 * (chip ^ other) + inner // block
                start = part * block + inner % block
                row = place(part, inner % block)
                for b, rows in enumerate(filter_rows(shifted, filter_ref, column, start)):
                    lanes = pl.ds(pl.multiple_of(b * width + tile * LANES, LANES), LANES)
                    design_ref[row, lanes] = rows.astype(jnp.bfloat16)
        return carry

    lax.fori_loop(0, width // LANES, columns, 0)
    wait_all(copies)


def filter_scratch(time_len):
    return [
        pltpu.VMEM((time_len, LANES), jnp.float32),
        pltpu.VMEM((8 // TAP_SPACING, time_len + TAP_SPACING * FILTER_TAPS + 8, LANES), jnp.float32),
    ]


def product_kernel(taken, extra, first, design_ref, *refs):
    weight_refs, refs = refs[:taken], refs[taken + extra :]
    copies = []
    if first is not None:
        weight_ref, keep_ref, send_ref, *piece_refs, sems = refs
        copies = copy_pieces(weight_ref, piece_refs, sems, first)
    else:
        keep_ref, send_ref = refs
    half, at = keep_ref.shape[0], 0
    for ref in weight_refs:
        for start in range(0, ref.shape[2], COLUMNS):
            weight = ref[:, :, start : min(start + COLUMNS, ref.shape[2])]
            weight = weight.reshape(-1, weight.shape[2])
            total = jnp.dot(design_ref[...], weight, preferred_element_type=jnp.float32)
            columns = slice(at, at + weight.shape[1])
            keep_ref[:, columns] = total[:half].astype(jnp.bfloat16)
            send_ref[:, columns] = total[half:].astype(jnp.bfloat16)
            at += weight.shape[1]
    wait_all(copies)


def product(design, taken, after, weights, first, ahead):
    time_len, lanes = design.shape
    width = sum(piece.shape[2] for piece in taken)
    half = jax.ShapeDtypeStruct((time_len // 2, width), jnp.bfloat16)
    return pl.pallas_call(
        functools.partial(product_kernel, len(taken), len(after), first if ahead else None),
        in_specs=[VMEM()] * (1 + len(taken)) + [ANY()] * (len(after) + bool(ahead)),
        out_specs=[VMEM()] * (2 + len(ahead)),
        out_shape=[half, half] + ahead,
        scratch_shapes=[pltpu.SemaphoreType.DMA((len(ahead),))] if ahead else [],
        compiler_params=pltpu.CompilerParams(vmem_limit_bytes=8 * MIB),
        cost_estimate=cost(2 * time_len * lanes * width, 2 * lanes * width),
        name="product",
    )(design, *taken, *after, *([weights] if ahead else []))


def add_rows(terms, each, first, out_ref):
    at, rows = 0, out_ref.shape[0]
    for c in range(0, len(terms), each):
        chunk, width = terms[c : c + each], terms[c].shape[1]
        total = sum(term[first : first + rows, :].astype(jnp.float32) for term in chunk)
        out_ref[:, at : at + width] = total.astype(jnp.bfloat16)
        at += width


def pack_kernel(spread, widths, places, first, later, outs, order_ref, start_ref, inner_ref, tile_ref, *refs):
    *refs, summed, packed = refs
    if later:
        count, each = later
        *refs, send_ref, keep_ref = refs
    terms, out_refs = refs[: len(refs) - outs], refs[len(refs) - outs :]
    if later:
        rows = packed.shape[1]
        add_rows(terms[-count:], each, 3 * rows, send_ref)
        add_rows(terms[-count:], each, rows, keep_ref)
        terms = terms[:-count]
    owners, rows = packed.shape[:2]
    if first:
        packed[...] = terms.pop(0)[...]
    else:
        packed[...] = jnp.zeros_like(packed)
    at = 0
    for width, spots in zip(widths, places):
        total = 0.0
        for row, column in spots:
            total = total + terms.pop(0)[row : row + rows, column : column + width].astype(jnp.float32)
        summed[:, at : at + width] = total.astype(jnp.bfloat16)
        at += width
    step = VOX_BLOCK // LANES
    slot_rows = lax.broadcasted_iota(jnp.int32, (2 * SLOT_TILE, VOX_BLOCK), 0)

    def moves(index, far):
        block = first + index
        values = summed[:, pl.ds(pl.multiple_of(index * VOX_BLOCK, VOX_BLOCK), VOX_BLOCK)]
        tiles, inner = (
            jnp.concatenate([ref[pl.ds(block * step + i, 1), :] for i in range(step)], axis=1)
            for ref in (tile_ref, inner_ref)
        )
        onehot = jnp.where(inner == slot_rows, 1.0, 0.0).astype(jnp.bfloat16)
        low = [start_ref[block, o] >> 7 for o in range(owners)]
        chosen = []
        for o in range(owners):
            tile = tiles - (o * spread + low[o])
            hit = jnp.where((tile == 2) if far else ((tile == 0) | (tile == 1)), 1.0, 0.0)
            chosen.append(values * hit.astype(jnp.bfloat16))
        moved = lax.dot_general(
            jnp.concatenate(chosen, axis=0), onehot, (((1,), (1,)), ((), ())), preferred_element_type=jnp.float32
        )
        moved = moved.astype(jnp.bfloat16)
        out = []
        for o in range(owners):
            here = moved[o * rows : (o + 1) * rows]
            tile, here = (low[o] + 2, here[:, :SLOT_TILE]) if far else (low[o], here)
            lanes = pl.ds(pl.multiple_of(tile * SLOT_TILE, SLOT_TILE), here.shape[1])
            out.append((o, lanes, here))
        high = [(start_ref[block + 1, o] - 1) >> 7 for o in range(owners)]
        return out, functools.reduce(jnp.maximum, [high[o] - low[o] for o in range(owners)])

    def add(targets):
        sums = [packed[owner, :, lanes] + moved for owner, lanes, moved in targets]
        for (owner, lanes, _), total in zip(targets, sums):
            packed[owner, :, lanes] = total

    def blocks(indices):
        found = [moves(index, False) for index in indices]
        for targets, _ in found:
            add(targets)
        for index, (_, longest) in zip(indices, found):

            @pl.when(longest > 1)
            def _():
                add(moves(index, True)[0])

    count = sum(widths) // VOX_BLOCK

    def some(i, carry):
        blocks([PACK_STEP * i + j for j in range(PACK_STEP)])
        return carry

    lax.fori_loop(0, count // PACK_STEP, some, 0)
    if count % PACK_STEP:
        blocks(range(count - count % PACK_STEP, count))
    if outs == 1:
        out_refs[0][...] = packed[...]
    else:
        for d, ref in enumerate(out_refs):
            ref[...] = packed[order_ref[d], :, : ref.shape[1]]


def shards(features, hrf_filters, weights, voxel_parcel, parcel_owner):
    owners, parts = lax.axis_size("vox"), lax.axis_size("chan")
    me = lax.axis_index("chan")
    voxels = voxel_parcel.shape[0]
    send_cap = 2 * voxels // owners
    bases, depth, _ = weights.shape
    blocks = voxels // VOX_BLOCK
    time_block = features.shape[0]
    time_len = time_block * parts

    series = [lax.dynamic_slice_in_dim(features, (me ^ d) * depth, depth, 1) for d in range(parts)]
    for d in range(1, parts):
        series[d] = lax.ppermute(series[d], "chan", [(i, i ^ d) for i in range(parts)])
    filters = jnp.transpose(hrf_filters, (0, 2, 1))
    spare = -depth % LANES
    lanes = bases * (depth + spare)
    unit = voxels // sum(units for pieces in COPIES for _, units in pieces)
    copied = [unit * sum(units for _, units in pieces) for pieces in COPIES]
    firsts = [sum(copied[:i]) for i in range(len(copied))]
    held = [[] for _ in range(CHUNKS)]

    def room(i):
        if i >= len(COPIES):
            return []
        return [pltpu.VMEM((bases, depth + spare, unit * units), jnp.bfloat16) for _, units in COPIES[i]]

    def keep_pieces(i, pieces):
        for (chunk, _), piece in zip(COPIES[i] if i < len(COPIES) else (), pieces):
            held[chunk].append(piece)

    if spare:
        series = [jnp.pad(part, ((0, 0), (0, spare))) for part in series]
        filters = jnp.pad(filters, ((0, 0), (0, 0), (0, spare)))

    table_rows = -(-parcel_owner.shape[0] // LANES)
    table = jnp.pad(parcel_owner, (0, table_rows * LANES - parcel_owner.shape[0])).reshape(table_rows, LANES)
    marks = -(-(blocks + 1) // 8) * 8
    spread = send_cap // SLOT_TILE + 3
    bits = parts.bit_length() - 1
    order = jnp.arange(parts, dtype=jnp.int32) ^ me
    place = sum(((order >> bit) & 1) << (bits - 1 - bit) for bit in range(bits)).astype(jnp.int32)

    early_rows = 2 * time_block - ROWS
    inner, tiles, starts, early, *pieces = pl.pallas_call(
        functools.partial(early_kernel, owners, spread),
        in_specs=[SMEM(), VMEM(), VMEM(), HBM(), VMEM(), HBM(), ANY()],
        out_specs=[VMEM()] * (4 + len(COPIES[0])),
        out_shape=[
            jax.ShapeDtypeStruct((voxels // LANES, LANES), jnp.int32),
            jax.ShapeDtypeStruct((voxels // LANES, LANES), jnp.int32),
            jax.ShapeDtypeStruct((marks, LANES), jnp.int32),
            jax.ShapeDtypeStruct((early_rows, lanes), jnp.bfloat16),
        ]
        + room(0),
        scratch_shapes=filter_scratch(2 * time_block)
        + [
            pltpu.VMEM(filters.shape, jnp.float32),
            pltpu.VMEM((voxels // LANES, LANES), jnp.int32),
            pltpu.SemaphoreType.DMA((len(COPIES[0]),)),
            pltpu.SemaphoreType.DMA((2,)),
        ],
        compiler_params=pltpu.CompilerParams(vmem_limit_bytes=8 * MIB),
        cost_estimate=cost(0, 2 * bases * depth * copied[0]),
        name="early",
    )(
        order,
        series[0],
        series[1],
        pltpu.with_memory_space_constraint(voxel_parcel.reshape(-1, LANES), pltpu.HBM),
        table,
        pltpu.with_memory_space_constraint(filters, pltpu.HBM),
        weights,
    )
    keep_pieces(0, pieces)
    design, *pieces = pl.pallas_call(
        functools.partial(design_kernel, parts, firsts[1]),
        in_specs=[SMEM(), SMEM(), VMEM(), VMEM(), ANY()] + [VMEM()] * parts,
        out_specs=[VMEM()] * (1 + len(COPIES[1])),
        out_shape=[jax.ShapeDtypeStruct((time_len, lanes), jnp.bfloat16)] + room(1),
        scratch_shapes=filter_scratch(time_len) + [pltpu.SemaphoreType.DMA((len(COPIES[1]),))],
        compiler_params=pltpu.CompilerParams(vmem_limit_bytes=8 * MIB),
        cost_estimate=cost(0, 2 * bases * depth * copied[1]),
        name="design",
    )(order, place, early, filters, weights, *series)
    keep_pieces(1, pieces)

    half = time_block // 2
    widths, sums, sent, got = [], [], [], []
    for c in range(CHUNKS):
        after = sent[max(c - 2, 0) : max(c - 1, 0)] + got[max(c - 3, 0) : max(c - 2, 0)]
        ahead = room(c + 2)
        keep, send, *pieces = product(design, held[c], after, weights, firsts[c + 2] if ahead else 0, ahead)
        keep_pieces(c + 2, pieces)
        widths.append(keep.shape[1])
        own = [keep]
        for bit in range(bits):
            if bit > 0:
                rows = own[-1].shape[0] // 2
                send = added(own, rows, half if bit == bits - 1 else rows)
                if bit == bits - 1:
                    sent.append(send)
            own.append(lax.ppermute(send, "chan", [(i, i ^ (1 << bit)) for i in range(parts)]))
        sums.append(own)
        got.append(own[-1])
    here = lax.axis_index("vox")
    targets = jnp.arange(owners, dtype=jnp.int32) ^ here

    def pack(chunks, terms, spots, packed=(), later=()):
        sizes = [widths[c] for c in chunks]
        spec = (len(later), bits) if later else None
        if chunks[-1] == CHUNKS - 1:
            outs = [pltpu.VMEM((half, send_cap), jnp.bfloat16)] * owners
        else:
            outs = [jax.ShapeDtypeStruct((owners, half, spread * SLOT_TILE), jnp.bfloat16)]
        more = []
        if later:
            more = [jax.ShapeDtypeStruct((half, voxels), jnp.bfloat16), pltpu.VMEM((half, voxels), jnp.bfloat16)]
        return pl.pallas_call(
            functools.partial(
                pack_kernel, spread, sizes, spots, sum(widths[: chunks[0]]) // VOX_BLOCK, spec, len(outs)
            ),
            in_specs=[SMEM(), SMEM(), VMEM(), VMEM()] + [VMEM()] * (len(packed) + len(terms) + len(later)),
            out_specs=[VMEM()] * (len(outs) + len(more)),
            out_shape=outs + more,
            scratch_shapes=[
                pltpu.VMEM((half, sum(sizes)), jnp.bfloat16),
                pltpu.VMEM((owners, half, spread * SLOT_TILE), jnp.bfloat16),
            ],
            compiler_params=pltpu.CompilerParams(vmem_limit_bytes=8 * MIB),
            cost_estimate=cost(2 * half * owners * VOX_BLOCK * sum(sizes), 4 * half * sum(sizes)),
            name="pack",
        )(targets, starts, inner, tiles, *packed, *terms, *later)

    turns = range(owners - 1, 0, -1)

    def deliver(packed):
        got = list(packed)
        for d in turns:
            got[d] = lax.ppermute(packed[d], "vox", [(i, i ^ d) for i in range(owners)])
        return got

    def early_terms(chunks):
        return [term for c in chunks for term in sums[c]], [[(0, 0)] * len(sums[c]) for c in chunks]

    packed = []
    for low, high in zip(PACKS, PACKS[1:]):
        chunks = range(low, high)
        later = [term for own in sums for term in own[:-1]] if high == CHUNKS else []
        packed = pack(chunks, *early_terms(chunks), packed=packed, later=later)
    *one, late_send, late_own = packed
    late = lax.ppermute(late_send, "chan", [(i, i ^ (1 << (bits - 1))) for i in range(parts)])
    one = deliver(one)
    starting = [sum(widths[:c]) for c in range(CHUNKS)]
    two = pack(range(CHUNKS), [late_own, late] * CHUNKS, [[(0, first)] * 2 for first in starting])
    two = pl.pallas_call(
        gate_kernel,
        in_specs=[VMEM()] * (owners + GATE),
        out_specs=[VMEM()] * owners,
        out_shape=[pltpu.VMEM((half, send_cap), jnp.bfloat16)] * owners,
        compiler_params=pltpu.CompilerParams(vmem_limit_bytes=4 * MIB),
        name="gate",
    )(*two, *(one[d] for d in turns[:GATE]))
    two = deliver(two)
    owned = None
    everyone = [*turns, 0]
    for first, got, which in ((0, one, everyone), (half, two, everyone)):
        given = [] if owned is None else [owned]
        count = len(which)
        owned = pl.pallas_call(
            functools.partial(assemble_kernel, tuple(which), first),
            in_specs=[SMEM()] + [VMEM()] * count + [HBM()] * len(given),
            out_specs=HBM(),
            out_shape=jax.ShapeDtypeStruct((owners, time_block, send_cap), jnp.bfloat16),
            scratch_shapes=[pltpu.SemaphoreType.DMA((count,))],
            input_output_aliases={1 + count: 0} if given else {},
            compiler_params=pltpu.CompilerParams(vmem_limit_bytes=4 * MIB),
            name="assemble",
        )(targets, *(got[d] for d in which), *given)
    return jnp.transpose(owned, (0, 2, 1))


def gate_kernel(*refs):
    count = (len(refs) - GATE) // 2
    for given, out in zip(refs[:count], refs[count + GATE :]):
        out[...] = given[...]


def assemble_kernel(which, first, order_ref, *refs):
    parts, (out_ref, sems) = refs[: len(which)], refs[-2:]
    copies = []
    for i, (d, ref) in enumerate(zip(which, parts)):
        rows = pl.ds(first, ref.shape[0])
        copies.append(pltpu.make_async_copy(ref, out_ref.at[order_ref[d], rows, :], sems.at[i]))
        copies[-1].start()
    wait_all(copies)


def added(terms, first, rows):
    return sum(term[first : first + rows].astype(jnp.float32) for term in terms).astype(jnp.bfloat16)


def solution(mesh):
    return jax.shard_map(
        shards,
        mesh=mesh,
        in_specs=(P("chan", None), P(None, "chan", None), P(None, "chan", "vox"), P("vox"), P()),
        out_specs=P("vox", None, "chan"),
        check_vma=False,
    )
```

```python
import functools

import jax
import jax.numpy as jnp
from jax import lax
from jax.experimental import pallas as pl
from jax.experimental.pallas import tpu as pltpu
from jax.sharding import PartitionSpec as P

FILTER_TAPS = 16
TAP_SPACING = 2
LANES = 128
SLOT_TILE = 128
VOX_BLOCK = 256
COLUMNS = 512
ROWS = 32
CHUNKS = 4
COPIES = (((0, 4), (1, 6)), ((2, 2), (2, 2)), (), ((2, 2), (3, 1)), ((3, 2), (3, 1)))
PACKS = (0, 2, 3, 4)
PACK_STEP = 4
GATE = 2
MIB = 1 << 20

VMEM = functools.partial(pl.BlockSpec, memory_space=pltpu.VMEM)
SMEM = functools.partial(pl.BlockSpec, memory_space=pltpu.SMEM)
ANY = functools.partial(pl.BlockSpec, memory_space=pl.ANY)
HBM = functools.partial(pl.BlockSpec, memory_space=pltpu.HBM)


def copy_pieces(weight_ref, piece_refs, sems, first):
    depth, copies = weight_ref.shape[1], []
    for i, ref in enumerate(piece_refs):
        if ref.shape[1] > depth:
            ref[:, depth:, :] = jnp.zeros_like(ref[:, depth:, :])
        copy = pltpu.make_async_copy(
            weight_ref.at[:, :, pl.ds(first, ref.shape[2])], ref.at[:, pl.ds(0, depth), :], sems.at[i]
        )
        copy.start()
        copies.append(copy)
        first += ref.shape[2]
    return copies


def wait_all(copies):
    for copy in copies:
        copy.wait()


def cost(flops, read):
    return pl.CostEstimate(flops=flops, bytes_accessed=read, transcendentals=0)


def places(owners, spread, parcel_ref, table_ref, inner_ref, tile_ref, start_ref):
    rows = parcel_ref.shape[0]
    parcel = parcel_ref[...]
    high, low = parcel >> 7, parcel & 127
    owner = jnp.zeros_like(parcel)
    for entry in range(table_ref.shape[0]):
        line = jnp.broadcast_to(table_ref[entry : entry + 1, :], parcel.shape)
        found = jnp.take_along_axis(line, low, axis=1, mode="promise_in_bounds")
        owner = jnp.where(high == entry, found, owner)

    def below(shape, scale=1):
        less = lax.broadcasted_iota(jnp.int32, shape, 1) < scale * lax.broadcasted_iota(jnp.int32, shape, 0)
        return less.astype(jnp.float32).astype(jnp.bfloat16)

    lane = lax.broadcasted_iota(jnp.int32, (LANES, LANES), 1)
    above = (lax.broadcasted_iota(jnp.int32, (LANES, LANES), 0) < lane).astype(jnp.float32).astype(jnp.bfloat16)
    ones = jnp.ones((LANES, LANES), jnp.bfloat16)
    marks = start_ref.shape[0]
    ahead, block_ahead = below((rows, rows)), below((marks, rows), VOX_BLOCK // LANES)
    mark_lane = lax.broadcasted_iota(jnp.int32, (marks, LANES), 1)
    dot = functools.partial(jnp.dot, preferred_element_type=jnp.float32)
    row_block = lax.broadcasted_iota(jnp.int32, (rows, rows), 0) & -(VOX_BLOCK // LANES)
    before = lax.broadcasted_iota(jnp.int32, (rows, rows), 1) < row_block
    before = before.astype(jnp.float32).astype(jnp.bfloat16)
    slots = jnp.zeros(parcel.shape, jnp.float32)
    bases = jnp.zeros(parcel.shape, jnp.float32)
    starts = jnp.zeros((marks, LANES), jnp.float32)
    for o in range(owners):
        mine = owner == o
        hot = mine.astype(jnp.float32).astype(jnp.bfloat16)
        totals = dot(hot, ones).astype(jnp.bfloat16)
        slots = jnp.where(mine, dot(hot, above) + dot(ahead, totals), slots)
        bases = jnp.where(mine, dot(before, totals), bases)
        starts = jnp.where(mark_lane == o, dot(block_ahead, totals), starts)
    slots = slots.astype(jnp.int32)
    start_ref[...] = starts.astype(jnp.int32)[:, :owners]
    tile_ref[...] = owner * spread + (slots >> 7)
    inner_ref[...] = (slots - (bases.astype(jnp.int32) & -SLOT_TILE)) & (2 * SLOT_TILE - 1)


def clear_lead(shifted):
    lead = TAP_SPACING * FILTER_TAPS
    for s in range(shifted.shape[0]):
        shifted[s, : lead + 8, :] = jnp.zeros((lead + 8, LANES), jnp.float32)


def shift(plain, shifted):
    lead, time_len = TAP_SPACING * FILTER_TAPS, plain.shape[0]
    series = plain[...]
    for s in range(shifted.shape[0]):
        shifted[s, lead + s * TAP_SPACING : lead + s * TAP_SPACING + time_len, :] = series


def filter_rows(shifted, filter_ref, column, first):
    lead = TAP_SPACING * FILTER_TAPS
    sums = [jnp.zeros((ROWS, LANES), jnp.float32) for _ in range(filter_ref.shape[0])]
    for tap in range(FILTER_TAPS):
        delay = tap * TAP_SPACING
        start = lead + first - 8 * (delay // 8)
        if not isinstance(start, int):
            start = pl.multiple_of(start, 8)
        lagged = shifted[(delay % 8) // TAP_SPACING, pl.ds(start, ROWS), :]
        for b in range(len(sums)):
            sums[b] = sums[b] + filter_ref[b, tap : tap + 1, column] * lagged
    return sums


def lane_tile(tile):
    return pl.ds(pl.multiple_of(tile * LANES, LANES), LANES)


def early_kernel(owners, spread, order_ref, own_ref, pair_ref, parcel_hbm, table_ref, filter_hbm, weight_ref, *refs):
    inner_ref, tile_ref, start_ref, design_ref, *piece_refs, plain, shifted, filter_ref, parcel_ref, sems, small_sems = refs
    load_filter = pltpu.make_async_copy(filter_hbm, filter_ref, small_sems.at[0])
    load_parcel = pltpu.make_async_copy(parcel_hbm, parcel_ref, small_sems.at[1])
    load_filter.start()
    load_parcel.start()
    copies = copy_pieces(weight_ref, piece_refs, sems, 0)
    block, width = own_ref.shape
    core = lax.rem(order_ref[0], 2)
    own = pl.ds(pl.multiple_of(core * block, block), block)
    pair = pl.ds(pl.multiple_of((1 - core) * block, block), block)
    clear_lead(shifted)
    load_filter.wait()

    def columns(tile, carry):
        column = lane_tile(tile)
        plain[own, :] = own_ref[:, column].astype(jnp.float32)
        plain[pair, :] = pair_ref[:, column].astype(jnp.float32)
        shift(plain, shifted)
        for first in range(ROWS, 2 * block, ROWS):
            for b, rows in enumerate(filter_rows(shifted, filter_ref, column, first)):
                lanes = pl.ds(pl.multiple_of(b * width + tile * LANES, LANES), LANES)
                design_ref[first - ROWS : first, lanes] = rows.astype(jnp.bfloat16)
        return carry

    lax.fori_loop(0, width // LANES, columns, 0)
    load_parcel.wait()
    places(owners, spread, parcel_ref, table_ref, inner_ref, tile_ref, start_ref)
    wait_all(copies)


def design_kernel(parts, first, order_ref, place_ref, early_ref, filter_ref, weight_ref, *refs):
    series_refs, (design_ref, *piece_refs, plain, shifted, sems) = refs[:parts], refs[parts:]
    copies = copy_pieces(weight_ref, piece_refs, sems, first)
    block, width = series_refs[0].shape
    chip = order_ref[0] >> 1
    clear_lead(shifted)

    def place(part, inner):
        return pl.ds(pl.multiple_of(place_ref[part] * block + inner, ROWS), ROWS)

    for first in range(ROWS, 2 * block, ROWS):
        row = place(2 * chip + first // block, first % block)
        design_ref[row, :] = early_ref[first - ROWS : first, :]

    def columns(tile, carry):
        column = lane_tile(tile)
        for d in range(parts):
            row = pl.ds(pl.multiple_of(order_ref[d] * block, block), block)
            plain[row, :] = series_refs[d][:, column].astype(jnp.float32)
        shift(plain, shifted)
        for other in range(parts // 2):
            for inner in range(0, 2 * block if other else ROWS, ROWS):
                part = 2 * (chip ^ other) + inner // block
                start = part * block + inner % block
                row = place(part, inner % block)
                for b, rows in enumerate(filter_rows(shifted, filter_ref, column, start)):
                    lanes = pl.ds(pl.multiple_of(b * width + tile * LANES, LANES), LANES)
                    design_ref[row, lanes] = rows.astype(jnp.bfloat16)
        return carry

    lax.fori_loop(0, width // LANES, columns, 0)
    wait_all(copies)


def filter_scratch(time_len):
    return [
        pltpu.VMEM((time_len, LANES), jnp.float32),
        pltpu.VMEM((8 // TAP_SPACING, time_len + TAP_SPACING * FILTER_TAPS + 8, LANES), jnp.float32),
    ]


def product_kernel(taken, extra, first, design_ref, *refs):
    weight_refs, refs = refs[:taken], refs[taken + extra :]
    copies = []
    if first is not None:
        weight_ref, keep_ref, send_ref, *piece_refs, sems = refs
        copies = copy_pieces(weight_ref, piece_refs, sems, first)
    else:
        keep_ref, send_ref = refs
    half, at = keep_ref.shape[0], 0
    for ref in weight_refs:
        for start in range(0, ref.shape[2], COLUMNS):
            weight = ref[:, :, start : min(start + COLUMNS, ref.shape[2])]
            weight = weight.reshape(-1, weight.shape[2])
            total = jnp.dot(design_ref[...], weight, preferred_element_type=jnp.float32)
            columns = slice(at, at + weight.shape[1])
            keep_ref[:, columns] = total[:half].astype(jnp.bfloat16)
            send_ref[:, columns] = total[half:].astype(jnp.bfloat16)
            at += weight.shape[1]
    wait_all(copies)


def product(design, taken, after, weights, first, ahead):
    time_len, lanes = design.shape
    width = sum(piece.shape[2] for piece in taken)
    half = jax.ShapeDtypeStruct((time_len // 2, width), jnp.bfloat16)
    return pl.pallas_call(
        functools.partial(product_kernel, len(taken), len(after), first if ahead else None),
        in_specs=[VMEM()] * (1 + len(taken)) + [ANY()] * (len(after) + bool(ahead)),
        out_specs=[VMEM()] * (2 + len(ahead)),
        out_shape=[half, half] + ahead,
        scratch_shapes=[pltpu.SemaphoreType.DMA((len(ahead),))] if ahead else [],
        compiler_params=pltpu.CompilerParams(vmem_limit_bytes=8 * MIB),
        cost_estimate=cost(2 * time_len * lanes * width, 2 * lanes * width),
        name="product",
    )(design, *taken, *after, *([weights] if ahead else []))


def add_rows(terms, each, first, out_ref):
    at, rows = 0, out_ref.shape[0]
    for c in range(0, len(terms), each):
        chunk, width = terms[c : c + each], terms[c].shape[1]
        total = sum(term[first : first + rows, :].astype(jnp.float32) for term in chunk)
        out_ref[:, at : at + width] = total.astype(jnp.bfloat16)
        at += width


def pack_kernel(spread, widths, places, first, later, outs, order_ref, start_ref, inner_ref, tile_ref, *refs):
    *refs, summed, packed = refs
    if later:
        count, each = later
        *refs, send_ref, keep_ref = refs
    terms, out_refs = refs[: len(refs) - outs], refs[len(refs) - outs :]
    if later:
        rows = packed.shape[1]
        add_rows(terms[-count:], each, 3 * rows, send_ref)
        add_rows(terms[-count:], each, rows, keep_ref)
        terms = terms[:-count]
    if outs == 1:
        packed = out_refs[0]
    owners, rows = packed.shape[:2]
    if first:
        packed[...] = terms.pop(0)[...]
    else:
        packed[...] = jnp.zeros_like(packed)
    at = 0
    for width, spots in zip(widths, places):
        total = 0.0
        for row, column in spots:
            total = total + terms.pop(0)[row : row + rows, column : column + width].astype(jnp.float32)
        summed[:, at : at + width] = total.astype(jnp.bfloat16)
        at += width
    step = VOX_BLOCK // LANES
    slot_rows = lax.broadcasted_iota(jnp.int32, (2 * SLOT_TILE, VOX_BLOCK), 0)

    def moves(index, far):
        block = first + index
        values = summed[:, pl.ds(pl.multiple_of(index * VOX_BLOCK, VOX_BLOCK), VOX_BLOCK)]
        tiles, inner = (
            jnp.concatenate([ref[pl.ds(block * step + i, 1), :] for i in range(step)], axis=1)
            for ref in (tile_ref, inner_ref)
        )
        onehot = jnp.where(inner == slot_rows, 1.0, 0.0).astype(jnp.bfloat16)
        low = [start_ref[block, o] >> 7 for o in range(owners)]
        chosen = []
        for o in range(owners):
            tile = tiles - (o * spread + low[o])
            hit = jnp.where((tile == 2) if far else ((tile == 0) | (tile == 1)), 1.0, 0.0)
            chosen.append(values * hit.astype(jnp.bfloat16))
        moved = lax.dot_general(
            jnp.concatenate(chosen, axis=0), onehot, (((1,), (1,)), ((), ())), preferred_element_type=jnp.float32
        )
        moved = moved.astype(jnp.bfloat16)
        out = []
        for o in range(owners):
            here = moved[o * rows : (o + 1) * rows]
            tile, here = (low[o] + 2, here[:, :SLOT_TILE]) if far else (low[o], here)
            lanes = pl.ds(pl.multiple_of(tile * SLOT_TILE, SLOT_TILE), here.shape[1])
            out.append((o, lanes, here))
        high = [(start_ref[block + 1, o] - 1) >> 7 for o in range(owners)]
        return out, functools.reduce(jnp.maximum, [high[o] - low[o] for o in range(owners)])

    def add(targets):
        sums = [packed[owner, :, lanes] + moved for owner, lanes, moved in targets]
        for (owner, lanes, _), total in zip(targets, sums):
            packed[owner, :, lanes] = total

    def blocks(indices):
        found = [moves(index, False) for index in indices]
        for targets, _ in found:
            add(targets)
        for index, (_, longest) in zip(indices, found):

            @pl.when(longest > 1)
            def _():
                add(moves(index, True)[0])

    count = sum(widths) // VOX_BLOCK

    def some(i, carry):
        blocks([PACK_STEP * i + j for j in range(PACK_STEP)])
        return carry

    lax.fori_loop(0, count // PACK_STEP, some, 0)
    if count % PACK_STEP:
        blocks(range(count - count % PACK_STEP, count))
    if outs > 1:
        for d, ref in enumerate(out_refs):
            ref[...] = packed[order_ref[d], :, : ref.shape[1]]


def shards(features, hrf_filters, weights, voxel_parcel, parcel_owner):
    owners, parts = lax.axis_size("vox"), lax.axis_size("chan")
    me = lax.axis_index("chan")
    voxels = voxel_parcel.shape[0]
    send_cap = 2 * voxels // owners
    bases, depth, _ = weights.shape
    blocks = voxels // VOX_BLOCK
    time_block = features.shape[0]
    time_len = time_block * parts

    series = [lax.dynamic_slice_in_dim(features, (me ^ d) * depth, depth, 1) for d in range(parts)]
    for d in range(1, parts):
        series[d] = lax.ppermute(series[d], "chan", [(i, i ^ d) for i in range(parts)])
    filters = jnp.transpose(hrf_filters, (0, 2, 1))
    spare = -depth % LANES
    lanes = bases * (depth + spare)
    unit = voxels // sum(units for pieces in COPIES for _, units in pieces)
    copied = [unit * sum(units for _, units in pieces) for pieces in COPIES]
    firsts = [sum(copied[:i]) for i in range(len(copied))]
    held = [[] for _ in range(CHUNKS)]

    def room(i):
        if i >= len(COPIES):
            return []
        return [pltpu.VMEM((bases, depth + spare, unit * units), jnp.bfloat16) for _, units in COPIES[i]]

    def keep_pieces(i, pieces):
        for (chunk, _), piece in zip(COPIES[i] if i < len(COPIES) else (), pieces):
            held[chunk].append(piece)

    if spare:
        series = [jnp.pad(part, ((0, 0), (0, spare))) for part in series]
        filters = jnp.pad(filters, ((0, 0), (0, 0), (0, spare)))

    table_rows = -(-parcel_owner.shape[0] // LANES)
    table = jnp.pad(parcel_owner, (0, table_rows * LANES - parcel_owner.shape[0])).reshape(table_rows, LANES)
    marks = -(-(blocks + 1) // 8) * 8
    spread = send_cap // SLOT_TILE + 3
    bits = parts.bit_length() - 1
    order = jnp.arange(parts, dtype=jnp.int32) ^ me
    place = sum(((order >> bit) & 1) << (bits - 1 - bit) for bit in range(bits)).astype(jnp.int32)

    early_rows = 2 * time_block - ROWS
    inner, tiles, starts, early, *pieces = pl.pallas_call(
        functools.partial(early_kernel, owners, spread),
        in_specs=[SMEM(), VMEM(), VMEM(), HBM(), VMEM(), HBM(), ANY()],
        out_specs=[VMEM()] * (4 + len(COPIES[0])),
        out_shape=[
            jax.ShapeDtypeStruct((voxels // LANES, LANES), jnp.int32),
            jax.ShapeDtypeStruct((voxels // LANES, LANES), jnp.int32),
            jax.ShapeDtypeStruct((marks, owners), jnp.int32),
            jax.ShapeDtypeStruct((early_rows, lanes), jnp.bfloat16),
        ]
        + room(0),
        scratch_shapes=filter_scratch(2 * time_block)
        + [
            pltpu.VMEM(filters.shape, jnp.float32),
            pltpu.VMEM((voxels // LANES, LANES), jnp.int32),
            pltpu.SemaphoreType.DMA((len(COPIES[0]),)),
            pltpu.SemaphoreType.DMA((2,)),
        ],
        compiler_params=pltpu.CompilerParams(vmem_limit_bytes=8 * MIB),
        cost_estimate=cost(0, 2 * bases * depth * copied[0]),
        name="early",
    )(
        order,
        series[0],
        series[1],
        pltpu.with_memory_space_constraint(voxel_parcel.reshape(-1, LANES), pltpu.HBM),
        table,
        pltpu.with_memory_space_constraint(filters, pltpu.HBM),
        weights,
    )
    keep_pieces(0, pieces)
    design, *pieces = pl.pallas_call(
        functools.partial(design_kernel, parts, firsts[1]),
        in_specs=[SMEM(), SMEM(), VMEM(), VMEM(), ANY()] + [VMEM()] * parts,
        out_specs=[VMEM()] * (1 + len(COPIES[1])),
        out_shape=[jax.ShapeDtypeStruct((time_len, lanes), jnp.bfloat16)] + room(1),
        scratch_shapes=filter_scratch(time_len) + [pltpu.SemaphoreType.DMA((len(COPIES[1]),))],
        compiler_params=pltpu.CompilerParams(vmem_limit_bytes=8 * MIB),
        cost_estimate=cost(0, 2 * bases * depth * copied[1]),
        name="design",
    )(order, place, early, filters, weights, *series)
    keep_pieces(1, pieces)

    half = time_block // 2
    widths, sums, sent, got = [], [], [], []
    for c in range(CHUNKS):
        after = sent[max(c - 2, 0) : max(c - 1, 0)] + got[max(c - 3, 0) : max(c - 2, 0)]
        ahead = room(c + 2)
        keep, send, *pieces = product(design, held[c], after, weights, firsts[c + 2] if ahead else 0, ahead)
        keep_pieces(c + 2, pieces)
        widths.append(keep.shape[1])
        own = [keep]
        for bit in range(bits):
            if bit > 0:
                rows = own[-1].shape[0] // 2
                send = added(own, rows, half if bit == bits - 1 else rows)
                if bit == bits - 1:
                    sent.append(send)
            own.append(lax.ppermute(send, "chan", [(i, i ^ (1 << bit)) for i in range(parts)]))
        sums.append(own)
        got.append(own[-1])
    here = lax.axis_index("vox")
    targets = jnp.arange(owners, dtype=jnp.int32) ^ here

    def pack(chunks, terms, spots, packed=(), later=()):
        sizes = [widths[c] for c in chunks]
        spec = (len(later), bits) if later else None
        if chunks[-1] == CHUNKS - 1:
            outs = [pltpu.VMEM((half, send_cap), jnp.bfloat16)] * owners
        else:
            outs = [jax.ShapeDtypeStruct((owners, half, spread * SLOT_TILE), jnp.bfloat16)]
        more = []
        if later:
            more = [jax.ShapeDtypeStruct((half, voxels), jnp.bfloat16), pltpu.VMEM((half, voxels), jnp.bfloat16)]
        return pl.pallas_call(
            functools.partial(
                pack_kernel, spread, sizes, spots, sum(widths[: chunks[0]]) // VOX_BLOCK, spec, len(outs)
            ),
            in_specs=[SMEM(), SMEM(), VMEM(), VMEM()] + [VMEM()] * (len(packed) + len(terms) + len(later)),
            out_specs=[VMEM()] * (len(outs) + len(more)),
            out_shape=outs + more,
            scratch_shapes=[
                pltpu.VMEM((half, sum(sizes)), jnp.bfloat16),
                pltpu.VMEM((owners, half, spread * SLOT_TILE), jnp.bfloat16),
            ],
            compiler_params=pltpu.CompilerParams(vmem_limit_bytes=8 * MIB),
            cost_estimate=cost(2 * half * owners * VOX_BLOCK * sum(sizes), 4 * half * sum(sizes)),
            name="pack",
        )(targets, starts, inner, tiles, *packed, *terms, *later)

    turns = range(owners - 1, 0, -1)

    def deliver(packed):
        got = list(packed)
        for d in turns:
            got[d] = lax.ppermute(packed[d], "vox", [(i, i ^ d) for i in range(owners)])
        return got

    def early_terms(chunks):
        return [term for c in chunks for term in sums[c]], [[(0, 0)] * len(sums[c]) for c in chunks]

    packed = []
    for low, high in zip(PACKS, PACKS[1:]):
        chunks = range(low, high)
        later = [term for own in sums for term in own[:-1]] if high == CHUNKS else []
        packed = pack(chunks, *early_terms(chunks), packed=packed, later=later)
    *one, late_send, late_own = packed
    late = lax.ppermute(late_send, "chan", [(i, i ^ (1 << (bits - 1))) for i in range(parts)])
    one = deliver(one)
    starting = [sum(widths[:c]) for c in range(CHUNKS)]
    two = pack(range(CHUNKS), [late_own, late] * CHUNKS, [[(0, first)] * 2 for first in starting])
    two = pl.pallas_call(
        gate_kernel,
        in_specs=[VMEM()] * (owners + GATE),
        out_specs=[VMEM()] * owners,
        out_shape=[pltpu.VMEM((half, send_cap), jnp.bfloat16)] * owners,
        compiler_params=pltpu.CompilerParams(vmem_limit_bytes=4 * MIB),
        name="gate",
    )(*two, *(one[d] for d in turns[:GATE]))
    two = deliver(two)
    owned = None
    everyone = [*turns, 0]
    for first, got, which in ((0, one, everyone), (half, two, everyone)):
        given = [] if owned is None else [owned]
        count = len(which)
        owned = pl.pallas_call(
            functools.partial(assemble_kernel, tuple(which), first),
            in_specs=[SMEM()] + [VMEM()] * count + [HBM()] * len(given),
            out_specs=HBM(),
            out_shape=jax.ShapeDtypeStruct((owners, time_block, send_cap), jnp.bfloat16),
            scratch_shapes=[pltpu.SemaphoreType.DMA((count,))],
            input_output_aliases={1 + count: 0} if given else {},
            compiler_params=pltpu.CompilerParams(vmem_limit_bytes=4 * MIB),
            name="assemble",
        )(targets, *(got[d] for d in which), *given)
    return jnp.transpose(owned, (0, 2, 1))


def gate_kernel(*refs):
    count = (len(refs) - GATE) // 2
    for given, out in zip(refs[:count], refs[count + GATE :]):
        out[...] = given[...]


def assemble_kernel(which, first, order_ref, *refs):
    parts, (out_ref, sems) = refs[: len(which)], refs[-2:]
    copies = []
    for i, (d, ref) in enumerate(zip(which, parts)):
        rows = pl.ds(first, ref.shape[0])
        copies.append(pltpu.make_async_copy(ref, out_ref.at[order_ref[d], rows, :], sems.at[i]))
        copies[-1].start()
    wait_all(copies)


def added(terms, first, rows):
    return sum(term[first : first + rows].astype(jnp.float32) for term in terms).astype(jnp.bfloat16)


def solution(mesh):
    return jax.shard_map(
        shards,
        mesh=mesh,
        in_specs=(P("chan", None), P(None, "chan", None), P(None, "chan", "vox"), P("vox"), P()),
        out_specs=P("vox", None, "chan"),
        check_vma=False,
    )
```
